32 devices in a mesh: batch: 4 (over y, x), centre: 8 (over z, core).
Axes of the slice: x: 2, y: 2, z: 4, core: 2. Of those that a mesh axis runs over, the one named last changes fastest.
Arguments:
- batch_pool: bfloat16 [1312, 1024], P(('batch', 'centre')), may hold values from -6 to 6
- batch_index: int32 [1024], P(('batch', 'centre')), may hold values from 0 to 1311, as said below
- centre_pool: bfloat16 [18440, 1024], P('centre'), may hold values from -6 to 6
- centre_index: int32 [16384], P('centre'), may hold values from 0 to 18439, as said below
- targets: float32 [1024, 301], P(('batch', 'centre')), may hold values from -6 to 6
- coefficients: float32 [16384, 301], P('centre'), may hold values from -1.5 to 1.5
Outputs:
- updated: float32 [16384, 301], P('centre')
- residual: float32 [1024, 301], P(('batch', 'centre'))
The draws below stay inside these ranges and needn't reach their ends.
Inputs may be any that keep to these rules, and one draw needn't show every extreme that they name: `batch_index`: the entries of each aligned block of 32 are distinct and lie in the same aligned block of 41 pool rows, block for block. `centre_index`: the entries of each aligned block of 2048 are distinct and lie in the same aligned block of 2305 pool rows, block for block.
All inputs are finite; a program needn't handle non-finite values.
Results may differ from the reference program's by a relative error of at most 0.0034.
Values may be sent and summed in bfloat16 or wider, within the bound.
No kernel may reach another device: no remote copies, remote signals or barrier semaphores. Data moves between devices by JAX's collectives and lax.ppermute only.
A program may use at most 64 MiB of HBM per device.

```python
import math
import jax
import jax.numpy as jnp
from jax import lax

D = 1024
OUT = 301
ROWS_DEV = 32
CEN_DEV = 2048
ROW_POOL = 41
CEN_POOL = 2305
BATCH = 1024
CENTRES = 16384
BATCH_POOL = 1312
CENTRE_POOL = 18440
N_BATCH = 4


def feature_rows(base_key, row_constant, numbers):
    cluster_total = min(256, CENTRE_POOL // 8)
    places = 1.0 + jnp.arange(D, dtype=jnp.float32)
    harmonic = jnp.sum(1.0 / places)
    scales = 1.0 / jnp.sqrt(places * harmonic)
    mean_key = jax.random.fold_in(base_key, 21)
    rows_key = jax.random.fold_in(base_key, row_constant)
    means = jnp.clip(jax.random.normal(mean_key, (cluster_total, D), jnp.float32), -3.5, 3.5)
    spread = jnp.ones((cluster_total,), jnp.float32)
    means = 3.4641016 * means

    def one_row(number):
        row_key = jax.random.fold_in(rows_key, number)
        cluster = jax.random.randint(jax.random.fold_in(row_key, 1), (), 0, cluster_total)
        noise_key = jax.random.fold_in(row_key, 2)
        noise = jnp.clip(jax.random.normal(noise_key, (D,), jnp.float32), -4.0, 4.0)
        values = means[cluster] + 0.70710678 * spread[cluster] * noise
        return values * scales
    rows = jax.vmap(one_row)(numbers)
    return jnp.clip(rows, -6.0, 6.0).astype(jnp.bfloat16)


def pick_indices(key, blocks, pool_size, count):

    def one_block(number):
        order = jax.random.permutation(jax.random.fold_in(key, number), pool_size)
        return order[:count].astype(jnp.int32) + number * pool_size
    return jax.vmap(one_block)(jnp.arange(blocks, dtype=jnp.int32)).reshape(-1)


def draw_batch_pool(key, part):
    numbers = jnp.arange(BATCH_POOL, dtype=jnp.int32)
    own_rows = feature_rows(key, 11, numbers)
    sources = jax.random.randint(jax.random.fold_in(key, 15), (BATCH_POOL,), 0, CENTRE_POOL)
    copied = feature_rows(key, 12, sources)
    picked = numbers % 8 == 0
    return jnp.where(picked[:, None], copied, own_rows)


def draw_centre_pool(key, part):
    return feature_rows(key, 12, jnp.arange(CENTRE_POOL, dtype=jnp.int32))


def draw_batch_index(key, part):
    return pick_indices(jax.random.fold_in(key, 13), BATCH_POOL // ROW_POOL, ROW_POOL, ROWS_DEV)


def draw_centre_index(key, part):
    return pick_indices(jax.random.fold_in(key, 14), CENTRE_POOL // CEN_POOL, CEN_POOL, CEN_DEV)


def levels(key, dims, cuts, least, high):
    loudness = 1.0
    for axis_at, shards_of in cuts:
        steps = jax.random.uniform(jax.random.fold_in(jax.random.fold_in(key, 6), axis_at), (shards_of,), jnp.float32, least / len(cuts), high / len(cuts))
        loudness = loudness * jnp.repeat(jnp.exp(steps), dims[axis_at] // shards_of).reshape((-1,) + (1,) * (len(dims) - 1 - axis_at))
    return loudness


def scatter_about(own_key, shape, scale, reach, split=(), kind=jnp.bfloat16):
    array = scale * jax.random.normal(own_key, shape, jnp.float32)
    if split:
        array = array * levels(own_key, shape, split, -0.22, 0.18)
    return jnp.clip(array, -reach, reach).astype(kind)


def setup_inputs(seed: int = 0) -> dict:
    arg_keys = jax.random.split(jax.random.key(seed), 7)
    batch_pool = draw_batch_pool(jax.random.fold_in(arg_keys[6], 71), 0)
    batch_index = draw_batch_index(jax.random.fold_in(arg_keys[6], 71), 0)
    centre_pool = draw_centre_pool(jax.random.fold_in(arg_keys[6], 71), 0)
    centre_index = draw_centre_index(jax.random.fold_in(arg_keys[6], 71), 0)
    targets = scatter_about(arg_keys[4], (BATCH, OUT), 1.0, 6.0, ((0, 32),), jnp.float32)
    coefficients = scatter_about(arg_keys[5], (CENTRES, OUT), 0.25, 1.5, ((0, 8),), jnp.float32)
    return {"batch_pool": batch_pool, "batch_index": batch_index, "centre_pool": centre_pool, "centre_index": centre_index, "targets": targets, "coefficients": coefficients}


def kernel_block(samples, centres, centre_square):
    cross = jnp.dot(samples, centres.T, preferred_element_type=jnp.float32)
    wide = samples.astype(jnp.float32)
    sample_square = lax.optimization_barrier(jnp.sum(wide * wide, axis=1))
    squared = sample_square[:, None] + centre_square[None, :] - 2.0 * cross
    return jnp.exp(-jnp.sqrt(jnp.maximum(squared, 0.0))).astype(jnp.bfloat16)

def reference(batch_pool, batch_index, centre_pool, centre_index, targets, coefficients):
    samples = batch_pool[batch_index]
    centres = centre_pool[centre_index]
    centre_wide = centres.astype(jnp.float32)
    centre_square = lax.optimization_barrier(jnp.sum(centre_wide * centre_wide, axis=1))
    coefficient_half = coefficients.astype(jnp.bfloat16)
    blocks = N_BATCH
    span = samples.shape[0] // blocks
    sample_blocks = samples.reshape(blocks, span, samples.shape[1])
    target_blocks = targets.reshape(blocks, span, targets.shape[1])

    def advance(total, pair):
        block_rows, block_targets = pair
        kernel = kernel_block(block_rows, centres, centre_square)
        prediction = jnp.dot(kernel, coefficient_half, preferred_element_type=jnp.float32)
        residual = prediction - block_targets
        total = total + jnp.dot(kernel.T, residual.astype(jnp.bfloat16), preferred_element_type=jnp.float32)
        return (total, residual)
    start_total = jnp.zeros((centres.shape[0], coefficients.shape[1]), jnp.float32)
    gradient, residual = lax.scan(advance, start_total, (sample_blocks, target_blocks))
    updated = coefficients - 8.0 / math.sqrt(BATCH) * gradient
    return (updated, residual.reshape(BATCH, coefficients.shape[1]))
```

```python
import math

import jax
import jax.numpy as jnp
from jax import lax
from jax.sharding import PartitionSpec as P


def partner_shift(axis, distance):
    count = lax.axis_size(axis)
    return [(i, (i + distance) % count) for i in range(count)]


def from_all(value, axis):
    return [value] + [
        lax.ppermute(value, axis, partner_shift(axis, k)) for k in range(1, lax.axis_size(axis))
    ]


def on_device(batch_pool, batch_index, centre_pool, centre_index, targets, coefficients):
    own_count = batch_index.shape[0]
    batch_size, centre_size = lax.axis_size("batch"), lax.axis_size("centre")
    batch_place, centre_place = lax.axis_index("batch"), lax.axis_index("centre")
    device_place = batch_place * centre_size + centre_place
    local_rows = jnp.take(
        batch_pool, batch_index - device_place * batch_pool.shape[0], axis=0, mode="clip"
    )
    pieces = from_all(local_rows, "centre")

    centres = jnp.take(
        centre_pool, centre_index - centre_place * centre_pool.shape[0], axis=0, mode="clip"
    )
    centre_square = jnp.sum(jnp.square(centres.astype(jnp.float32)), axis=1)
    coefficient_half = coefficients.astype(jnp.bfloat16)

    piece = jnp.concatenate(pieces, axis=0)
    cross = lax.dot_general(
        piece, centres, (((1,), (1,)), ((), ())), preferred_element_type=jnp.float32
    )
    piece_square = jnp.sum(jnp.square(piece.astype(jnp.float32)), axis=1)
    squared = piece_square[:, None] + centre_square[None, :] - 2.0 * cross
    kernel = jnp.exp(-jnp.sqrt(jnp.maximum(squared, 0.0))).astype(jnp.bfloat16)
    terms = jnp.dot(kernel, coefficient_half, preferred_element_type=jnp.float32)

    predicted = terms[:own_count]
    for k in range(1, centre_size):
        predicted = predicted + lax.ppermute(
            terms[k * own_count : (k + 1) * own_count],
            "centre",
            partner_shift("centre", centre_size - k),
        )
    residual = predicted - targets
    residual_all = jnp.concatenate(from_all(residual.astype(jnp.bfloat16), "centre"), axis=0)

    span = centre_index.shape[0] // batch_size

    def span_gradient(place):
        return lax.dot_general(
            residual_all,
            lax.dynamic_slice_in_dim(kernel, place * span, span, axis=1),
            (((0,), (0,)), ((), ())),
            preferred_element_type=jnp.float32,
        )

    total = span_gradient(batch_place)
    for k in range(1, batch_size):
        sent = span_gradient((batch_place + k) % batch_size).astype(jnp.bfloat16)
        total = total + lax.ppermute(sent, "batch", partner_shift("batch", k)).astype(jnp.float32)
    spans = from_all(total.astype(jnp.bfloat16), "batch")
    gradient = jnp.zeros((coefficients.shape[1], centre_index.shape[0]), jnp.bfloat16)
    for k, part in enumerate(spans):
        place = (batch_place - k) % batch_size
        gradient = lax.dynamic_update_slice_in_dim(gradient, part, place * span, axis=1)
    batch_total = own_count * batch_size * centre_size
    step_size = 8.0 / math.sqrt(batch_total)
    updated = coefficients - step_size * gradient.astype(jnp.float32).T
    return (updated, residual)


def solution(mesh):
    return jax.shard_map(
        on_device,
        mesh=mesh,
        in_specs=(
            P(("batch", "centre"), None),
            P(("batch", "centre")),
            P("centre", None),
            P("centre"),
            P(("batch", "centre"), None),
            P("centre", None),
        ),
        out_specs=(P("centre", None), P(("batch", "centre"), None)),
        check_vma=False,
    )
```

```python
import math

import jax
import jax.numpy as jnp
from jax import lax
from jax.sharding import PartitionSpec as P


def flip(value, axis, distance):
    count = lax.axis_size(axis)
    return lax.ppermute(value, axis, [(i, i ^ distance) for i in range(count)])


def gather_doubling(value, axis, dimension):
    place = lax.axis_index(axis)
    distance = 1
    while distance < lax.axis_size(axis):
        other = flip(value, axis, distance)
        upper = (place & distance) != 0
        value = jnp.concatenate(
            [jnp.where(upper, other, value), jnp.where(upper, value, other)], axis=dimension
        )
        distance *= 2
    return value


def on_device(batch_pool, batch_index, centre_pool, centre_index, targets, coefficients):
    own_count = batch_index.shape[0]
    batch_size, centre_size = lax.axis_size("batch"), lax.axis_size("centre")
    batch_place, centre_place = lax.axis_index("batch"), lax.axis_index("centre")
    device_place = batch_place * centre_size + centre_place
    local_rows = jnp.take(
        batch_pool, batch_index - device_place * batch_pool.shape[0], axis=0, mode="clip"
    )
    copies = jnp.broadcast_to(local_rows, (centre_size,) + local_rows.shape)
    piece = lax.all_to_all(copies, "centre", 0, 0).reshape(-1, local_rows.shape[1])

    centres = jnp.take(
        centre_pool, centre_index - centre_place * centre_pool.shape[0], axis=0, mode="clip"
    )
    centre_square = jnp.sum(jnp.square(centres.astype(jnp.float32)), axis=1)
    coefficient_half = coefficients.astype(jnp.bfloat16)

    cross = lax.dot_general(
        piece, centres, (((1,), (1,)), ((), ())), preferred_element_type=jnp.float32
    )
    piece_square = jnp.sum(jnp.square(piece.astype(jnp.float32)), axis=1)
    squared = piece_square[:, None] + centre_square[None, :] - 2.0 * cross
    kernel = jnp.exp(-jnp.sqrt(jnp.maximum(squared, 0.0))).astype(jnp.bfloat16)
    terms = jnp.dot(kernel, coefficient_half, preferred_element_type=jnp.float32)

    shares = lax.all_to_all(terms.reshape(centre_size, own_count, -1), "centre", 0, 0)
    residual = jnp.sum(shares, axis=0) - targets
    residual_all = gather_doubling(residual.astype(jnp.bfloat16), "centre", 0)

    span = centre_index.shape[0] // batch_size
    spans = [
        lax.dot_general(
            residual_all,
            kernel[:, place * span : (place + 1) * span],
            (((0,), (0,)), ((), ())),
            preferred_element_type=jnp.float32,
        ).astype(jnp.bfloat16)
        for place in range(batch_size)
    ]
    shares = lax.all_to_all(jnp.stack(spans), "batch", 0, 0)
    total = jnp.sum(shares.astype(jnp.float32), axis=0).astype(jnp.bfloat16)
    gradient = gather_doubling(total, "batch", 1)
    batch_total = own_count * batch_size * centre_size
    step_size = 8.0 / math.sqrt(batch_total)
    updated = coefficients - step_size * gradient.astype(jnp.float32).T
    return (updated, residual)


def solution(mesh):
    return jax.shard_map(
        on_device,
        mesh=mesh,
        in_specs=(
            P(("batch", "centre"), None),
            P(("batch", "centre")),
            P("centre", None),
            P("centre"),
            P(("batch", "centre"), None),
            P("centre", None),
        ),
        out_specs=(P("centre", None), P(("batch", "centre"), None)),
        check_vma=False,
    )
```

```python
import math

import jax
import jax.numpy as jnp
from jax import lax
from jax.sharding import PartitionSpec as P


def flip(value, axis, distance):
    count = lax.axis_size(axis)
    return lax.ppermute(value, axis, [(i, i ^ distance) for i in range(count)])


def gather_rows(value, axis, distances):
    for distance in distances:
        value = jnp.concatenate([value, flip(value, axis, distance)], axis=0)
    return value


def gather_groups(value, axis, distances):
    ways = len(distances)
    if ways == 0 or value.shape[0] % (16 * ways):
        return gather_rows(value, axis, distances)
    rows = value.shape[0] // ways
    blocks = {}
    for way in range(ways):
        turned = distances[way:] + distances[:way]
        held = gather_rows(value[way * rows : (way + 1) * rows], axis, turned)
        places = [0]
        for distance in turned:
            places = places + [place ^ distance for place in places]
        for i, place in enumerate(places):
            blocks[place, way] = held[i * rows : (i + 1) * rows]
    count = lax.axis_size(axis)
    return jnp.concatenate(
        [blocks[place, way] for place in range(count) for way in range(ways)], axis=0
    )


def contract_first(left, right):
    return lax.dot_general(
        left, right, (((0,), (0,)), ((), ())), preferred_element_type=jnp.float32
    )


def powers(first, count):
    return [1 << i for i in range(first, count.bit_length() - 1)]


def on_device(batch_pool, batch_index, centre_pool, centre_index, targets, coefficients):
    own_count = batch_index.shape[0]
    batch_size, centre_size = lax.axis_size("batch"), lax.axis_size("centre")
    batch_place, centre_place = lax.axis_index("batch"), lax.axis_index("centre")
    device_place = batch_place * centre_size + centre_place
    batch_total = own_count * batch_size * centre_size
    far = powers(1, centre_size)
    hold_all = batch_total * (centre_index.shape[0] + batch_pool.shape[1]) * 2 <= 1 << 24

    local_rows = jnp.take(
        batch_pool, batch_index - device_place * batch_pool.shape[0], axis=0, mode="clip"
    )
    side = gather_rows(local_rows, "centre", far)
    other_side = flip(side, "centre", 1)

    centres = jnp.take(
        centre_pool, centre_index - centre_place * centre_pool.shape[0], axis=0, mode="clip"
    )
    centre_square = jnp.sum(jnp.square(centres.astype(jnp.float32)), axis=1)
    coefficient_half = coefficients.astype(jnp.bfloat16)

    def kernel_of(rows):
        cross = lax.dot_general(
            rows, centres, (((1,), (1,)), ((), ())), preferred_element_type=jnp.float32
        )
        row_square = jnp.sum(jnp.square(rows.astype(jnp.float32)), axis=1)
        squared = row_square[:, None] + centre_square[None, :] - 2.0 * cross
        return jnp.exp(-jnp.sqrt(jnp.maximum(squared, 0.0))).astype(jnp.bfloat16)

    kernel = kernel_of(jnp.concatenate([side, other_side], axis=0))
    terms = jnp.dot(kernel, coefficient_half, preferred_element_type=jnp.float32)

    rows = side.shape[0]
    near = powers(0, batch_size)
    if hold_all:
        side_rows = gather_groups(side, "batch", near)[rows:]
        other_rows = flip(side_rows, "centre", 1)

    total = terms[:rows] + flip(terms[rows:], "centre", 1)
    for step, distance in enumerate(reversed(far)):
        half = total.shape[0] // 2
        total = total[:half] + flip(total[half:], "centre", distance)
        if hold_all and step == 0:
            total, kernel_side = lax.optimization_barrier((total, kernel_of(side_rows)))
    if hold_all:
        total, kernel_other = lax.optimization_barrier((total, kernel_of(other_rows)))
    residual = total - targets
    residual_side = gather_rows(residual.astype(jnp.bfloat16), "centre", far)

    step_size = 8.0 / math.sqrt(batch_total)
    if hold_all:
        residual_side = gather_groups(residual_side, "batch", near)
        residual_other = flip(residual_side, "centre", 1)
        gradient = contract_first(residual_side[:rows], kernel[:rows])
        gradient = gradient + contract_first(residual_side[rows:], kernel_side)
        gradient = gradient + contract_first(residual_other[:rows], kernel[rows:])
        gradient = gradient + contract_first(residual_other[rows:], kernel_other)
    else:
        residual_all = jnp.concatenate(
            [residual_side, flip(residual_side, "centre", 1)], axis=0
        )
        gradient = lax.psum(contract_first(residual_all, kernel), "batch")
    updated = coefficients - step_size * gradient.T
    return (updated, residual)


def solution(mesh):
    return jax.shard_map(
        on_device,
        mesh=mesh,
        in_specs=(
            P(("batch", "centre"), None),
            P(("batch", "centre")),
            P("centre", None),
            P("centre"),
            P(("batch", "centre"), None),
            P("centre", None),
        ),
        out_specs=(P("centre", None), P(("batch", "centre"), None)),
        check_vma=False,
    )
```

```python
import functools
import math

import jax
import jax.numpy as jnp
from jax import lax
from jax.experimental import pallas as pl
from jax.experimental.pallas import tpu as pltpu
from jax.sharding import PartitionSpec as P

LANES = 128


def flip(value, axis, distance):
    count = lax.axis_size(axis)
    return lax.ppermute(value, axis, [(i, i ^ distance) for i in range(count)])


def after(value, *others):
    return lax.optimization_barrier((value,) + others)[0]


def span_of(total, most):
    span = total
    while span > most and span % 2 == 0 and (span // 2) % LANES == 0:
        span //= 2
    return span


def pick_rows_kernel(whole, index_ref, pool_ref, rows_ref, square_ref):
    span = index_ref.shape[1]
    wanted = jnp.concatenate(
        [
            jnp.broadcast_to(index_ref[:, at : at + LANES], (LANES, LANES)).T
            for at in range(0, span, LANES)
        ],
        axis=0,
    )
    lane = lax.broadcasted_iota(jnp.int32, (span, LANES), 1)
    chosen = jnp.concatenate(
        [
            jnp.where(wanted == lane + at, 1.0, 0.0).astype(jnp.bfloat16)
            for at in range(0, whole, LANES)
        ],
        axis=1,
    )
    rows = jnp.dot(chosen, pool_ref[:whole, :], preferred_element_type=jnp.float32)
    for at in range(whole, pool_ref.shape[0]):
        rows = rows + jnp.where(
            wanted[:, :1] == at, pool_ref[at : at + 1, :].astype(jnp.float32), 0.0
        )
    rows_ref[...] = rows.astype(jnp.bfloat16)
    square = jnp.sum(rows * rows, axis=1, keepdims=True)
    square_ref[...] = jnp.concatenate(
        [
            jnp.broadcast_to(square[at : at + LANES], (LANES, LANES)).T[:1]
            for at in range(0, span, LANES)
        ],
        axis=1,
    )


def pick_rows(pool, index):
    count, depth = index.shape[0], pool.shape[1]
    span = span_of(count, 512)
    whole = pool.shape[0] // LANES * LANES
    return pl.pallas_call(
        functools.partial(pick_rows_kernel, whole),
        grid=(count // span,),
        in_specs=[
            pl.BlockSpec((1, span), lambda i: (0, i)),
            pl.BlockSpec(pool.shape, lambda i: (0, 0)),
        ],
        out_specs=[
            pl.BlockSpec((span, depth), lambda i: (i, 0)),
            pl.BlockSpec((1, span), lambda i: (0, i)),
        ],
        out_shape=[
            jax.ShapeDtypeStruct((count, depth), jnp.bfloat16),
            jax.ShapeDtypeStruct((1, count), jnp.float32),
        ],
        cost_estimate=pl.CostEstimate(
            flops=2 * count * whole * depth, bytes_accessed=8 * count * depth, transcendentals=0
        ),
        compiler_params=pltpu.CompilerParams(vmem_limit_bytes=48 << 20),
    )(index.reshape(1, count), pool)


def descend_kernel(step, base_ref, *refs):
    out_ref = refs[-1]
    gradient = jnp.zeros(base_ref.shape, jnp.float32)
    for residual_ref, kernel_ref in zip(refs[0:-1:2], refs[1:-1:2]):
        gradient = gradient + jnp.dot(
            residual_ref[...], kernel_ref[...], preferred_element_type=jnp.float32
        )
    out_ref[...] = base_ref[...] - step * gradient


def descend(base, pairs, step):
    outs, count = base.shape
    span = span_of(count, 512)
    specs, operands, rows = [], [], 0
    for residual, kernel, first in pairs:
        size = residual.shape[1]
        at = first // size
        specs.append(pl.BlockSpec((outs, size), lambda i: (0, 0)))
        specs.append(pl.BlockSpec((size, span), functools.partial(lambda at, i: (at, i), at)))
        operands += [residual, kernel]
        rows += size
    return pl.pallas_call(
        functools.partial(descend_kernel, step),
        grid=(count // span,),
        in_specs=[pl.BlockSpec((outs, span), lambda i: (0, i))] + specs,
        out_specs=pl.BlockSpec((outs, span), lambda i: (0, i)),
        out_shape=jax.ShapeDtypeStruct(base.shape, jnp.float32),
        cost_estimate=pl.CostEstimate(
            flops=2 * outs * count * rows, bytes_accessed=12 * outs * count, transcendentals=0
        ),
        compiler_params=pltpu.CompilerParams(vmem_limit_bytes=48 << 20),
    )(base, *operands)


def on_device(batch_pool, batch_index, centre_pool, centre_index, targets, coefficients):
    own_count = batch_index.shape[0]
    batch_size, centre_size = lax.axis_size("batch"), lax.axis_size("centre")
    batch_place, centre_place = lax.axis_index("batch"), lax.axis_index("centre")
    device_place = batch_place * centre_size + centre_place
    batch_total = own_count * batch_size * centre_size
    far_size, far_place = centre_size // 2, centre_place // 2
    rows = far_size * own_count
    hold_all = batch_total * (centre_index.shape[0] + batch_pool.shape[1]) * 2 <= 1 << 24

    chosen = (batch_index - device_place * batch_pool.shape[0])[:, None] == jnp.arange(
        batch_pool.shape[0]
    )
    local_rows = jnp.dot(
        chosen.astype(jnp.bfloat16), batch_pool, preferred_element_type=jnp.float32
    ).astype(jnp.bfloat16)
    pieces = [local_rows] + [flip(local_rows, "centre", 2 * k) for k in range(1, far_size)]

    centres, centre_square = pick_rows(
        centre_pool, centre_index - centre_place * centre_pool.shape[0]
    )
    pieces = [after(piece, centres) for piece in pieces]
    base = coefficients.T
    coefficient_half = base.astype(jnp.bfloat16)
    placed_targets = jnp.where(
        jnp.arange(rows) // own_count == far_place, jnp.tile(targets.T, (1, far_size)), 0.0
    )

    side = jnp.zeros((rows, batch_pool.shape[1]), jnp.bfloat16)
    for k, piece in enumerate(pieces):
        side = lax.dynamic_update_slice_in_dim(side, piece, (far_place ^ k) * own_count, axis=0)
    other = flip(side, "centre", 1)

    def kernel_of(samples):
        cross = lax.dot_general(
            samples, centres, (((1,), (1,)), ((), ())), preferred_element_type=jnp.float32
        )
        square = jnp.sum(jnp.square(samples.astype(jnp.float32)), axis=1)
        squared = square[:, None] + centre_square - 2.0 * cross
        return jnp.exp(-jnp.sqrt(jnp.maximum(squared, 0.0))).astype(jnp.bfloat16)

    kernel = kernel_of(jnp.concatenate([side, other], axis=0))
    terms = lax.dot_general(
        coefficient_half, kernel, (((1,), (1,)), ((), ())), preferred_element_type=jnp.float32
    )
    if hold_all:
        side_rows = jnp.concatenate(
            [flip(side, "batch", k) for k in range(1, batch_size)], axis=0
        )

    total = terms[:, :rows] - placed_targets + flip(terms[:, rows:], "centre", 1)
    distance = 2
    while distance < centre_size:
        total = total + flip(total, "centre", distance)
        if hold_all and distance == 2:
            side_rows = after(side_rows, total)
            other_rows = flip(side_rows, "centre", 1)
            kernel_side = kernel_of(side_rows)
        distance *= 2
    if hold_all:
        total, kernel_side = lax.optimization_barrier((total, kernel_side))
    residual = lax.dynamic_slice_in_dim(total, far_place * own_count, own_count, axis=1).T
    residual_side = total.astype(jnp.bfloat16)

    step = 8.0 / math.sqrt(batch_total)
    if hold_all:
        kernel_other = kernel_of(other_rows)
        parts = [residual_side] + [flip(residual_side, "batch", k) for k in range(1, batch_size)]
        kernel_other, *parts = lax.optimization_barrier((kernel_other, *parts))
        residual_side = jnp.concatenate(parts, axis=1)
        residual_other = flip(residual_side, "centre", 1)

        def pairs(of_all, place, rest):
            return [
                (of_all[:, :rows], kernel, place * rows),
                (of_all[:, rows:], rest, 0),
            ]

        updated = descend(base, pairs(residual_side, 0, kernel_side), step)
        updated = descend(updated, pairs(residual_other, 1, kernel_other), step)
    else:
        residual_other = flip(residual_side, "centre", 1)
        own = [(residual_side, kernel, 0), (residual_other, kernel, rows)]
        change = descend(jnp.zeros_like(base), own, step)
        updated = base + lax.psum(change, "batch")
    return (updated.T, residual)


def solution(mesh):
    return jax.shard_map(
        on_device,
        mesh=mesh,
        in_specs=(
            P(("batch", "centre"), None),
            P(("batch", "centre")),
            P("centre", None),
            P("centre"),
            P(("batch", "centre"), None),
            P("centre", None),
        ),
        out_specs=(P("centre", None), P(("batch", "centre"), None)),
        check_vma=False,
    )
```

```python
import functools
import math

import jax
import jax.numpy as jnp
from jax import lax
from jax.experimental import pallas as pl
from jax.experimental.pallas import tpu as pltpu
from jax.sharding import PartitionSpec as P

LANES = 128


def flip(value, axis, distance):
    count = lax.axis_size(axis)
    return lax.ppermute(value, axis, [(i, i ^ distance) for i in range(count)])


def after(value, *others):
    return lax.optimization_barrier((value,) + others)[0]


def span_of(total, most):
    span = total
    while span > most and span % 2 == 0 and (span // 2) % LANES == 0:
        span //= 2
    return span


def pick_rows_kernel(whole, index_ref, pool_ref, rows_ref, square_ref):
    span = index_ref.shape[1]
    wanted = jnp.concatenate(
        [
            jnp.broadcast_to(index_ref[:, at : at + LANES], (LANES, LANES)).T
            for at in range(0, span, LANES)
        ],
        axis=0,
    )
    lane = lax.broadcasted_iota(jnp.int32, (span, LANES), 1)
    chosen = jnp.concatenate(
        [
            jnp.where(wanted == lane + at, 1.0, 0.0).astype(jnp.bfloat16)
            for at in range(0, whole, LANES)
        ],
        axis=1,
    )
    rows = jnp.dot(chosen, pool_ref[:whole, :], preferred_element_type=jnp.float32)
    for at in range(whole, pool_ref.shape[0]):
        rows = rows + jnp.where(
            wanted[:, :1] == at, pool_ref[at : at + 1, :].astype(jnp.float32), 0.0
        )
    rows_ref[...] = rows.astype(jnp.bfloat16)
    square = jnp.sum(rows * rows, axis=1, keepdims=True)
    square_ref[...] = jnp.concatenate(
        [
            jnp.broadcast_to(square[at : at + LANES], (LANES, LANES)).T[:1]
            for at in range(0, span, LANES)
        ],
        axis=1,
    )


def pick_rows(pool, index):
    count, depth = index.shape[0], pool.shape[1]
    span = span_of(count, 512)
    whole = pool.shape[0] // LANES * LANES
    return pl.pallas_call(
        functools.partial(pick_rows_kernel, whole),
        grid=(count // span,),
        in_specs=[
            pl.BlockSpec((1, span), lambda i: (0, i)),
            pl.BlockSpec(pool.shape, lambda i: (0, 0)),
        ],
        out_specs=[
            pl.BlockSpec((span, depth), lambda i: (i, 0)),
            pl.BlockSpec((1, span), lambda i: (0, i)),
        ],
        out_shape=[
            jax.ShapeDtypeStruct((count, depth), jnp.bfloat16),
            jax.ShapeDtypeStruct((1, count), jnp.float32),
        ],
        cost_estimate=pl.CostEstimate(
            flops=2 * count * whole * depth, bytes_accessed=8 * count * depth, transcendentals=0
        ),
        compiler_params=pltpu.CompilerParams(vmem_limit_bytes=24 << 20),
    )(index.reshape(1, count), pool)


def descend_kernel(step, base_ref, *refs):
    out_ref = refs[-1]
    gradient = jnp.zeros(base_ref.shape, jnp.float32)
    for residual_ref, kernel_ref in zip(refs[0:-1:2], refs[1:-1:2]):
        gradient = gradient + jnp.dot(
            residual_ref[...], kernel_ref[...], preferred_element_type=jnp.float32
        )
    out_ref[...] = base_ref[...] - step * gradient


def descend(base, pairs, step):
    outs, count = base.shape
    span = span_of(count, 512)
    specs, operands, rows = [], [], 0
    for residual, kernel, first in pairs:
        size = residual.shape[1]
        at = first // size
        specs.append(pl.BlockSpec((outs, size), lambda i: (0, 0)))
        specs.append(pl.BlockSpec((size, span), functools.partial(lambda at, i: (at, i), at)))
        operands += [residual, kernel]
        rows += size
    return pl.pallas_call(
        functools.partial(descend_kernel, step),
        grid=(count // span,),
        in_specs=[pl.BlockSpec((outs, span), lambda i: (0, i))] + specs,
        out_specs=pl.BlockSpec((outs, span), lambda i: (0, i)),
        out_shape=jax.ShapeDtypeStruct(base.shape, jnp.float32),
        cost_estimate=pl.CostEstimate(
            flops=2 * outs * count * rows, bytes_accessed=12 * outs * count, transcendentals=0
        ),
        compiler_params=pltpu.CompilerParams(vmem_limit_bytes=20 << 20),
    )(base, *operands)


def contract_last(left, right):
    return lax.dot_general(
        left, right, (((1,), (1,)), ((), ())), preferred_element_type=jnp.float32
    )


def row_squares(samples):
    return jnp.sum(jnp.square(samples.astype(jnp.float32)), axis=1)


def kernel_block(samples, centres, centre_square):
    squared = row_squares(samples)[:, None] + centre_square - 2.0 * contract_last(samples, centres)
    return jnp.exp(-jnp.sqrt(jnp.maximum(squared, 0.0))).astype(jnp.bfloat16)


def on_device(batch_pool, batch_index, centre_pool, centre_index, targets, coefficients):
    own_count = batch_index.shape[0]
    batch_size, centre_size = lax.axis_size("batch"), lax.axis_size("centre")
    batch_place, centre_place = lax.axis_index("batch"), lax.axis_index("centre")
    device_place = batch_place * centre_size + centre_place
    batch_total = own_count * batch_size * centre_size
    far_size, far_place = centre_size // 2, centre_place // 2
    rows = far_size * own_count
    hold_all = batch_total * (centre_index.shape[0] + batch_pool.shape[1]) * 2 <= 1 << 24

    chosen = (batch_index - device_place * batch_pool.shape[0])[:, None] == jnp.arange(
        batch_pool.shape[0]
    )
    local_rows = jnp.dot(
        chosen.astype(jnp.bfloat16), batch_pool, preferred_element_type=jnp.float32
    ).astype(jnp.bfloat16)
    pieces = [local_rows] + [flip(local_rows, "centre", 2 * k) for k in range(1, far_size)]

    base = coefficients.T
    index = centre_index - centre_place * centre_pool.shape[0]
    placed = (jnp.arange(centre_pool.shape[0])[:, None] == index[None, :]).astype(jnp.bfloat16)
    pool_coefficients = contract_last(base.astype(jnp.bfloat16), placed).astype(jnp.bfloat16)
    pool_square = row_squares(centre_pool)
    pool_coefficients, pool_square, *pieces = lax.optimization_barrier(
        (pool_coefficients, pool_square, *pieces)
    )
    placed_targets = jnp.where(
        jnp.arange(rows) // own_count == far_place, jnp.tile(targets.T, (1, far_size)), 0.0
    )

    side = jnp.zeros((rows, batch_pool.shape[1]), jnp.bfloat16)
    for k, piece in enumerate(pieces):
        side = lax.dynamic_update_slice_in_dim(side, piece, (far_place ^ k) * own_count, axis=0)
    own = jnp.concatenate([side, flip(side, "centre", 1)], axis=0)
    pool_kernel = lax.optimization_barrier(kernel_block(own, centre_pool, pool_square[None, :]))
    terms = contract_last(pool_coefficients, pool_kernel)
    foreign = [flip(side, "batch", k) for k in range(1, batch_size)] if hold_all else []

    total = terms[:, :rows] - placed_targets + flip(terms[:, rows:], "centre", 1)
    count = index.shape[0]
    cuts = far_size.bit_length() - 1 if count % (LANES * far_size) == 0 else 1
    picked = []
    distance = 2
    while distance < centre_size:
        if len(picked) < cuts:
            at = len(picked) * (count // cuts)
            picked.append(pick_rows(centre_pool, after(index[at : at + count // cuts], total)))
        total = after(total + flip(total, "centre", distance), *picked[-1])
        distance *= 2
    if hold_all:
        foreign = lax.optimization_barrier((picked[-1][0], *foreign))[1:]
        side_rows = jnp.concatenate(foreign, axis=0)
        other_rows = flip(side_rows, "centre", 1)
    centres = jnp.concatenate([rows_of for rows_of, _ in picked], axis=0)
    centre_square = jnp.concatenate([square_of for _, square_of in picked], axis=1)
    kernel = kernel_block(own, centres, centre_square)
    total, kernel = lax.optimization_barrier((total, kernel))
    residual = lax.dynamic_slice_in_dim(total, far_place * own_count, own_count, axis=1).T
    residual_side = total.astype(jnp.bfloat16)

    step = 8.0 / math.sqrt(batch_total)
    if hold_all:
        kernel_side = kernel_block(after(side_rows, total), centres, centre_square)
        kernel_other = kernel_block(after(other_rows, total), centres, centre_square)
        parts = [residual_side] + [flip(residual_side, "batch", k) for k in range(1, batch_size)]
        kernel_side, kernel_other, *parts = lax.optimization_barrier(
            (kernel_side, kernel_other, *parts)
        )
        residual_side = jnp.concatenate(parts, axis=1)
        residual_other = flip(residual_side, "centre", 1)

        def pairs(of_all, place, rest):
            return [
                (of_all[:, :rows], kernel, place * rows),
                (of_all[:, rows:], rest, 0),
            ]

        updated = descend(base, pairs(residual_side, 0, kernel_side), step)
        updated = descend(updated, pairs(residual_other, 1, kernel_other), step)
    else:
        residual_other = flip(residual_side, "centre", 1)
        both = [(residual_side, kernel, 0), (residual_other, kernel, rows)]
        change = descend(jnp.zeros_like(base), both, step)
        updated = base + lax.psum(change, "batch")
    return (updated.T, residual)


def solution(mesh):
    return jax.shard_map(
        on_device,
        mesh=mesh,
        in_specs=(
            P(("batch", "centre"), None),
            P(("batch", "centre")),
            P("centre", None),
            P("centre"),
            P(("batch", "centre"), None),
            P("centre", None),
        ),
        out_specs=(P("centre", None), P(("batch", "centre"), None)),
        check_vma=False,
    )
```

```python
import functools
import math

import jax
import jax.numpy as jnp
from jax import lax
from jax.experimental import pallas as pl
from jax.experimental.pallas import tpu as pltpu
from jax.sharding import PartitionSpec as P

LANES = 128


def flip(value, axis, distance):
    count = lax.axis_size(axis)
    return lax.ppermute(value, axis, [(i, i ^ distance) for i in range(count)])


def after(value, *others):
    return lax.optimization_barrier((value,) + others)[0]


def contract_last(left, right):
    return lax.dot_general(
        left, right, (((1,), (1,)), ((), ())), preferred_element_type=jnp.float32
    )


def spans(total, most):
    return [(at, min(most, total - at)) for at in range(0, total, most)]


def call(body, operands, outputs, places=None, scratch=(), limit=16, flops=0):
    whole = pl.BlockSpec(memory_space=pltpu.VMEM)
    scalar = pl.BlockSpec(memory_space=pltpu.SMEM)
    shapes = [jax.ShapeDtypeStruct(shape, dtype) for shape, dtype in outputs]
    moved = sum(math.prod(x.shape) * x.dtype.itemsize for x in list(operands) + shapes)
    return pl.pallas_call(
        body,
        in_specs=[scalar if x.ndim == 1 else whole for x in operands],
        out_specs=places or [whole] * len(outputs),
        out_shape=shapes,
        scratch_shapes=list(scratch),
        cost_estimate=pl.CostEstimate(flops=flops, bytes_accessed=moved, transcendentals=0),
        compiler_params=pltpu.CompilerParams(vmem_limit_bytes=limit << 20),
    )(*operands)


def turned(column):
    return jnp.concatenate(
        [
            jnp.broadcast_to(column[at : at + LANES], (LANES, LANES)).T[:1]
            for at in range(0, column.shape[0], LANES)
        ],
        axis=1,
    )


def pool_rows(pool_ref, at, size):
    if at + size <= pool_ref.shape[0]:
        return pool_ref[at : at + size, :]
    place = lax.broadcasted_iota(jnp.int32, (size, pool_ref.shape[1]), 0)
    rows = jnp.zeros(place.shape, jnp.float32)
    for row in range(at, pool_ref.shape[0]):
        rows = jnp.where(place == row - at, pool_ref[row : row + 1, :].astype(jnp.float32), rows)
    return rows.astype(jnp.bfloat16)


def place_body(first_ref, index_ref, base_ref, pool_ref, placed_ref, square_ref):
    index = index_ref[...] - first_ref[0]
    half = base_ref[...].astype(jnp.bfloat16)
    for at, size in spans(placed_ref.shape[1], 2 * LANES):
        place = lax.broadcasted_iota(jnp.int32, (size, index.shape[1]), 0) + at
        chosen = jnp.where(index == place, 1.0, 0.0).astype(jnp.bfloat16)
        placed_ref[:, at : at + size] = contract_last(half, chosen).astype(jnp.bfloat16)
        rows = pool_rows(pool_ref, at, size).astype(jnp.float32)
        square_ref[:, at : at + size] = turned(jnp.sum(rows * rows, axis=1, keepdims=True))


def place_coefficients(first, index, base, pool):
    width = -(-pool.shape[0] // LANES) * LANES
    return call(
        place_body,
        [first, index, base, pool],
        [((base.shape[0], width), jnp.bfloat16), ((1, width), jnp.float32)],
        flops=2 * base.shape[0] * base.shape[1] * width,
    )


def terms_body(samples_ref, pool_ref, square_ref, placed_ref, terms_ref):
    samples = samples_ref[...]
    wide = samples.astype(jnp.float32)
    own_square = jnp.sum(wide * wide, axis=1, keepdims=True)
    for at, size in spans(placed_ref.shape[1], 2 * LANES):
        cross = contract_last(samples, pool_rows(pool_ref, at, size))
        squared = own_square + square_ref[:, at : at + size] - 2.0 * cross
        kernel = jnp.exp(-jnp.sqrt(jnp.maximum(squared, 0.0))).astype(jnp.bfloat16)
        terms = contract_last(placed_ref[:, at : at + size], kernel)
        terms_ref[...] = terms if at == 0 else terms_ref[...] + terms


def pool_terms(samples, pool, square, placed):
    return call(
        terms_body,
        [samples, pool, square, placed],
        [((placed.shape[0], samples.shape[0]), jnp.float32)],
        flops=2 * samples.shape[0] * placed.shape[1] * (placed.shape[0] + samples.shape[1]),
    )[0]


def pick_body(first_ref, index_ref, pool_ref, rows_ref, square_ref):
    whole = pool_ref.shape[0] // LANES * LANES
    for at, size in spans(rows_ref.shape[0], 4 * LANES):
        wanted = jnp.concatenate(
            [
                jnp.broadcast_to(index_ref[:, part : part + LANES], (LANES, LANES)).T
                for part in range(at, at + size, LANES)
            ],
            axis=0,
        ) - first_ref[0]
        lane = lax.broadcasted_iota(jnp.int32, (size, LANES), 1)
        chosen = jnp.concatenate(
            [
                jnp.where(wanted == lane + part, 1.0, 0.0).astype(jnp.bfloat16)
                for part in range(0, whole, LANES)
            ],
            axis=1,
        )
        rows = jnp.dot(chosen, pool_ref[:whole, :], preferred_element_type=jnp.float32)
        for row in range(whole, pool_ref.shape[0]):
            rows = rows + jnp.where(
                wanted[:, :1] == row, pool_ref[row : row + 1, :].astype(jnp.float32), 0.0
            )
        rows_ref[at : at + size, :] = rows.astype(jnp.bfloat16)
        square_ref[:, at : at + size] = turned(jnp.sum(rows * rows, axis=1, keepdims=True))


def pick_rows(first, index, pool):
    count, depth = index.shape[1], pool.shape[1]
    return call(
        pick_body,
        [first, index, pool],
        [((count, depth), jnp.bfloat16), ((1, count), jnp.float32)],
        limit=24,
        flops=2 * count * depth * pool.shape[0],
    )


def gradient_of(residuals, kernels, at, size):
    gradient = None
    for parts, (kernel_ref, first) in zip(residuals, kernels):
        left = jnp.concatenate([part[...] for part in parts], axis=1)
        right = kernel_ref[first : first + left.shape[1], at : at + size]
        term = jnp.dot(left, right, preferred_element_type=jnp.float32)
        gradient = term if gradient is None else gradient + term
    return gradient


def descend_body(step, parts, first, out_copies, base_ref, own_ref, rest_ref, *refs):
    residuals = [refs[:1], refs[1:parts]] if parts > 1 else [refs[:1]]
    kernels = [(own_ref, first), (rest_ref, 0)]
    out_ref = refs[parts]
    count = base_ref.shape[1]
    copies = []
    for turn, (at, size) in enumerate(spans(count, 4 * LANES)):
        result = base_ref[:, at : at + size] - step * gradient_of(residuals, kernels, at, size)
        if not out_copies:
            out_ref[:, at : at + size] = result
            continue
        held_ref, done_ref = refs[parts + 1 :]
        held_ref[:, at : at + size] = result
        copies.append(
            pltpu.make_async_copy(
                held_ref.at[:, pl.ds(at, size)], out_ref.at[:, pl.ds(at, size)], done_ref.at[turn]
            )
        )
        copies[-1].start()
    for copy in copies:
        copy.wait()


def descend(base, own, rest, residuals, first, step, last):
    shape = (base.shape, jnp.float32)
    scratch, places = (), None
    if last:
        turns = len(spans(base.shape[1], 4 * LANES))
        scratch = [pltpu.VMEM(*shape), pltpu.SemaphoreType.DMA((turns,))]
        places = [pl.BlockSpec(memory_space=pl.ANY)]
    rows = sum(part.shape[1] for part in residuals)
    return call(
        functools.partial(descend_body, step, len(residuals), first, last),
        [base, own, rest, *residuals],
        [shape],
        places,
        scratch,
        flops=2 * rows * math.prod(base.shape),
    )[0]


def row_squares(samples):
    return jnp.sum(jnp.square(samples.astype(jnp.float32)), axis=1)


def kernel_block(samples, centres, centre_square):
    squared = row_squares(samples)[:, None] + centre_square - 2.0 * contract_last(samples, centres)
    return jnp.exp(-jnp.sqrt(jnp.maximum(squared, 0.0))).astype(jnp.bfloat16)


def on_device(batch_pool, batch_index, centre_pool, centre_index, targets, coefficients):
    own_count = batch_index.shape[0]
    batch_size, centre_size = lax.axis_size("batch"), lax.axis_size("centre")
    batch_place, centre_place = lax.axis_index("batch"), lax.axis_index("centre")
    device_place = batch_place * centre_size + centre_place
    batch_total = own_count * batch_size * centre_size
    far_size, far_place = centre_size // 2, centre_place // 2
    rows = far_size * own_count
    hold_all = batch_total * (centre_index.shape[0] + batch_pool.shape[1]) * 2 <= 1 << 24

    chosen = jnp.arange(batch_pool.shape[0])[:, None] + device_place * batch_pool.shape[0] == (
        batch_index[None, :]
    )
    local_rows = lax.dot_general(
        chosen.astype(jnp.bfloat16),
        batch_pool,
        (((0,), (0,)), ((), ())),
        preferred_element_type=jnp.float32,
    ).astype(jnp.bfloat16)
    pieces = [local_rows] + [flip(local_rows, "centre", 2 * k) for k in range(1, far_size)]

    base = coefficients.T
    first = jnp.reshape(centre_place * centre_pool.shape[0], (1,)).astype(jnp.int32)
    index = centre_index.reshape(1, -1)
    placed, pool_square = place_coefficients(first, index, base, centre_pool)
    placed, *pieces = lax.optimization_barrier((placed, *pieces))
    placed_targets = jnp.where(
        jnp.arange(rows) // own_count == far_place, jnp.tile(targets.T, (1, far_size)), 0.0
    )

    side = jnp.zeros((rows, batch_pool.shape[1]), jnp.bfloat16)
    for k, piece in enumerate(pieces):
        side = lax.dynamic_update_slice_in_dim(side, piece, (far_place ^ k) * own_count, axis=0)
    other = flip(side, "centre", 1)
    terms = pool_terms(side, centre_pool, pool_square, placed)
    other_terms = pool_terms(other, centre_pool, pool_square, placed)
    foreign = [flip(side, "batch", k) for k in range(1, batch_size)] if hold_all else []

    total = terms - placed_targets + flip(other_terms, "centre", 1)
    count = index.shape[1]
    cuts = far_size.bit_length() - 1 if count % (LANES * far_size) == 0 else 1
    picked = []
    distance = 2
    while distance < centre_size:
        if len(picked) < cuts:
            at = len(picked) * (count // cuts)
            part = after(index[:, at : at + count // cuts], total)
            picked.append(pick_rows(first, part, centre_pool))
        total = after(total + flip(total, "centre", distance), *picked[-1])
        distance *= 2
    if hold_all:
        foreign = lax.optimization_barrier((picked[-1][0], *foreign))[1:]
        side_rows = jnp.concatenate(foreign, axis=0)
        other_rows = flip(side_rows, "centre", 1)
    centres = jnp.concatenate([rows_of for rows_of, _ in picked], axis=0)
    centre_square = jnp.concatenate([square_of for _, square_of in picked], axis=1)
    kernel = kernel_block(jnp.concatenate([side, other], axis=0), centres, centre_square)
    total, kernel = lax.optimization_barrier((total, kernel))
    residual = lax.dynamic_slice_in_dim(total, far_place * own_count, own_count, axis=1).T
    residual_side = total.astype(jnp.bfloat16)

    step = 8.0 / math.sqrt(batch_total)
    if hold_all:
        kernel_side = kernel_block(after(side_rows, total), centres, centre_square)
        kernel_other = kernel_block(after(other_rows, total), centres, centre_square)
        parts = [residual_side] + [flip(residual_side, "batch", k) for k in range(1, batch_size)]
        kernel_side, kernel_other, *parts = lax.optimization_barrier(
            (kernel_side, kernel_other, *parts)
        )
        others = [flip(part, "centre", 1) for part in parts]
        updated = descend(base, kernel, kernel_side, parts, 0, step, False)
        updated = descend(updated, kernel, kernel_other, others, rows, step, True)
    else:
        other_part = flip(residual_side, "centre", 1)
        change = descend(jnp.zeros_like(base), kernel, kernel, [residual_side], 0, step, False)
        change = descend(change, kernel, kernel, [other_part], rows, step, False)
        updated = base + lax.psum(change, "batch")
    return (updated.T, residual)


def solution(mesh):
    return jax.shard_map(
        on_device,
        mesh=mesh,
        in_specs=(
            P(("batch", "centre"), None),
            P(("batch", "centre")),
            P("centre", None),
            P("centre"),
            P(("batch", "centre"), None),
            P("centre", None),
        ),
        out_specs=(P("centre", None), P(("batch", "centre"), None)),
        check_vma=False,
    )
```

```python
import functools
import math

import jax
import jax.numpy as jnp
from jax import lax
from jax.experimental import pallas as pl
from jax.experimental.pallas import tpu as pltpu
from jax.sharding import PartitionSpec as P

LANES = 128


def flip(value, axis, distance):
    count = lax.axis_size(axis)
    return lax.ppermute(value, axis, [(i, i ^ distance) for i in range(count)])


def after(value, *others):
    return lax.optimization_barrier((value,) + others)[0]


def contract_last(left, right):
    return lax.dot_general(
        left, right, (((1,), (1,)), ((), ())), preferred_element_type=jnp.float32
    )


def spans(total, most):
    return [(at, min(most, total - at)) for at in range(0, total, most)]


WHOLE = pl.BlockSpec(memory_space=pltpu.VMEM)
SCALARS = pl.BlockSpec(memory_space=pltpu.SMEM)
FAR = pl.BlockSpec(memory_space=pltpu.HBM)


def call(body, operands, outputs, scratch=(), flops=0):
    fetching = any(place is FAR for _, place in operands)
    arrays = [array for array, _ in operands]
    shapes = [jax.ShapeDtypeStruct(shape, dtype) for shape, dtype, _ in outputs]
    moved = sum(math.prod(x.shape) * x.dtype.itemsize for x in arrays + shapes)
    return pl.pallas_call(
        body,
        in_specs=[place for _, place in operands],
        out_specs=[place for _, _, place in outputs],
        out_shape=shapes,
        scratch_shapes=list(scratch),
        cost_estimate=pl.CostEstimate(flops=flops, bytes_accessed=moved, transcendentals=0),
        compiler_params=pltpu.CompilerParams(vmem_limit_bytes=(55 if fetching else 24) << 20),
    )(*arrays)


def turned(column):
    return jnp.concatenate(
        [
            jnp.broadcast_to(column[at : at + LANES], (LANES, LANES)).T[:1]
            for at in range(0, column.shape[0], LANES)
        ],
        axis=1,
    )


def pool_rows(pool_ref, at, size):
    if at + size <= pool_ref.shape[0]:
        return pool_ref[at : at + size, :]
    place = lax.broadcasted_iota(jnp.int32, (size, pool_ref.shape[1]), 0)
    rows = jnp.zeros(place.shape, jnp.float32)
    for row in range(at, pool_ref.shape[0]):
        rows = jnp.where(place == row - at, pool_ref[row : row + 1, :].astype(jnp.float32), rows)
    return rows.astype(jnp.bfloat16)


def place_body(first_ref, index_far, base_far, pool_far, *refs):
    placed_ref, square_ref, index_ref, pool_ref, base_ref, done_ref = refs
    fetches = [
        pltpu.make_async_copy(far, near, done_ref.at[turn])
        for turn, (far, near) in enumerate(
            [(index_far, index_ref), (base_far, base_ref), (pool_far, pool_ref)]
        )
    ]
    for fetch in fetches:
        fetch.start()
    fetches[0].wait()
    index = index_ref[...] - first_ref[0]
    index_ref[...] = index
    fetches[1].wait()
    half = base_ref[...].astype(jnp.bfloat16)
    for at, size in spans(placed_ref.shape[1], 2 * LANES):
        place = lax.broadcasted_iota(jnp.int32, (size, index.shape[1]), 0) + at
        chosen = jnp.where(index == place, 1.0, 0.0).astype(jnp.bfloat16)
        placed_ref[:, at : at + size] = contract_last(half, chosen).astype(jnp.bfloat16)
        if at == 0:
            fetches[2].wait()
        rows = pool_rows(pool_ref, at, size).astype(jnp.float32)
        square_ref[at : at + size, :] = jnp.sum(rows * rows, axis=1, keepdims=True)


def place_coefficients(first, index, base, pool):
    width = -(-pool.shape[0] // LANES) * LANES
    return call(
        place_body,
        [(first, SCALARS), (index, FAR), (base, FAR), (pool, FAR)],
        [
            ((base.shape[0], width), jnp.bfloat16, WHOLE),
            ((width, 1), jnp.float32, WHOLE),
            (index.shape, jnp.int32, WHOLE),
            (pool.shape, jnp.bfloat16, WHOLE),
        ],
        [pltpu.VMEM(base.shape, jnp.float32), pltpu.SemaphoreType.DMA((3,))],
        flops=2 * base.shape[0] * base.shape[1] * width,
    )


def kernel_of(squared):
    return jnp.exp(-jnp.sqrt(jnp.maximum(squared, 0.0))).astype(jnp.bfloat16)


def terms_body(samples_ref, pool_ref, square_ref, placed_ref, terms_ref):
    samples = samples_ref[...]
    wide = samples.astype(jnp.float32)
    own_square = turned(jnp.sum(wide * wide, axis=1, keepdims=True))
    for at, size in spans(placed_ref.shape[1], 2 * LANES):
        cross = contract_last(pool_rows(pool_ref, at, size), samples)
        kernel = kernel_of(square_ref[at : at + size, :] + own_square - 2.0 * cross)
        terms = jnp.dot(
            placed_ref[:, at : at + size], kernel, preferred_element_type=jnp.float32
        )
        terms_ref[...] = terms if at == 0 else terms_ref[...] + terms


def pool_terms(samples, pool, square, placed):
    return call(
        terms_body,
        [(samples, WHOLE), (pool, WHOLE), (square, WHOLE), (placed, WHOLE)],
        [((placed.shape[0], samples.shape[0]), jnp.float32, WHOLE)],
        flops=2 * samples.shape[0] * placed.shape[1] * (placed.shape[0] + samples.shape[1]),
    )[0]


def pick_body(first, index_ref, pool_ref, rows_ref, square_ref):
    whole = pool_ref.shape[0] // LANES * LANES
    for at, size in spans(rows_ref.shape[0], 4 * LANES):
        wanted = jnp.concatenate(
            [
                jnp.broadcast_to(index_ref[:, part : part + LANES], (LANES, LANES)).T
                for part in range(first + at, first + at + size, LANES)
            ],
            axis=0,
        )
        lane = lax.broadcasted_iota(jnp.int32, (size, LANES), 1)
        chosen = jnp.concatenate(
            [
                jnp.where(wanted == lane + part, 1.0, 0.0).astype(jnp.bfloat16)
                for part in range(0, whole, LANES)
            ],
            axis=1,
        )
        rows = jnp.dot(chosen, pool_ref[:whole, :], preferred_element_type=jnp.float32)
        for row in range(whole, pool_ref.shape[0]):
            rows = rows + jnp.where(
                wanted[:, :1] == row, pool_ref[row : row + 1, :].astype(jnp.float32), 0.0
            )
        rows_ref[at : at + size, :] = rows.astype(jnp.bfloat16)
        square_ref[:, at : at + size] = turned(jnp.sum(rows * rows, axis=1, keepdims=True))


def pick_rows(index, pool, first, count):
    return call(
        functools.partial(pick_body, first),
        [(index, WHOLE), (pool, WHOLE)],
        [((count, pool.shape[1]), jnp.bfloat16, WHOLE), ((1, count), jnp.float32, WHOLE)],
        flops=2 * count * pool.shape[0] * pool.shape[1],
    )


def block_body(parts, *refs):
    samples = jnp.concatenate([ref[...] for ref in refs[:parts]], axis=0)
    kernel_ref = refs[-1]
    wide = samples.astype(jnp.float32)
    own_square = jnp.sum(wide * wide, axis=1, keepdims=True)
    start = 0
    for rows_ref, square_ref in zip(refs[parts:-1:2], refs[parts + 1 : -1 : 2]):
        for at, size in spans(rows_ref.shape[0], 2 * LANES):
            cross = contract_last(samples, rows_ref[at : at + size, :])
            kernel = kernel_of(own_square + square_ref[:, at : at + size] - 2.0 * cross)
            kernel_ref[:, start + at : start + at + size] = kernel
        start += rows_ref.shape[0]


def kernel_block(samples, picked):
    rows = sum(part.shape[0] for part in samples)
    count = sum(square.shape[1] for _, square in picked)
    return call(
        functools.partial(block_body, len(samples)),
        [(part, WHOLE) for part in samples]
        + [(array, WHOLE) for pair in picked for array in pair],
        [((rows, count), jnp.bfloat16, WHOLE)],
        flops=2 * rows * count * samples[0].shape[1],
    )[0]


def gradient_of(residuals, kernels, at, size):
    gradient = None
    for parts, (kernel_ref, first) in zip(residuals, kernels):
        left = jnp.concatenate([part[...] for part in parts], axis=1)
        right = kernel_ref[first : first + left.shape[1], at : at + size]
        term = jnp.dot(left, right, preferred_element_type=jnp.float32)
        gradient = term if gradient is None else gradient + term
    return gradient


def descend_body(step, parts, first, fetch, store, base_ref, own_ref, rest_ref, *refs):
    residuals = [refs[:1], refs[1:parts]] if parts > 1 else [refs[:1]]
    kernels = [(own_ref, first), (rest_ref, 0)]
    out_ref, scratch = refs[parts], refs[parts + 1 :]
    cuts = spans(base_ref.shape[1], 4 * LANES)

    def copies(source, target, done_ref):
        return [
            pltpu.make_async_copy(
                source.at[:, pl.ds(at, size)], target.at[:, pl.ds(at, size)], done_ref.at[turn]
            )
            for turn, (at, size) in enumerate(cuts)
        ]

    near_ref, held_ref, fetches, stores = base_ref, out_ref, [], []
    if fetch:
        near_ref = scratch[0]
        fetches = copies(base_ref, near_ref, scratch[1])
    if store:
        held_ref = scratch[0]
        stores = copies(held_ref, out_ref, scratch[1])
    for copy in fetches:
        copy.start()
    for turn, (at, size) in enumerate(cuts):
        gradient = gradient_of(residuals, kernels, at, size)
        if fetch:
            fetches[turn].wait()
        held_ref[:, at : at + size] = near_ref[:, at : at + size] - step * gradient
        if store:
            stores[turn].start()
    for copy in stores:
        copy.wait()


def descend(base, own, rest, residuals, first, step, fetch=False, store=False):
    scratch = []
    if fetch or store:
        turns = len(spans(base.shape[1], 4 * LANES))
        scratch = [pltpu.VMEM(base.shape, jnp.float32), pltpu.SemaphoreType.DMA((turns,))]
    rows = sum(part.shape[1] for part in residuals)
    return call(
        functools.partial(descend_body, step, len(residuals), first, fetch, store),
        [(base, FAR if fetch else WHOLE), (own, WHOLE), (rest, WHOLE)]
        + [(part, WHOLE) for part in residuals],
        [(base.shape, jnp.float32, FAR if store else WHOLE)],
        scratch,
        flops=2 * rows * math.prod(base.shape),
    )[0]


def on_device(batch_pool, batch_index, centre_pool, centre_index, targets, coefficients):
    own_count = batch_index.shape[0]
    batch_size, centre_size = lax.axis_size("batch"), lax.axis_size("centre")
    batch_place, centre_place = lax.axis_index("batch"), lax.axis_index("centre")
    device_place = batch_place * centre_size + centre_place
    batch_total = own_count * batch_size * centre_size
    far_size, far_place = centre_size // 2, centre_place // 2
    rows = far_size * own_count
    hold_all = batch_total * (centre_index.shape[0] + batch_pool.shape[1]) * 2 <= 1 << 24

    chosen = jnp.arange(batch_pool.shape[0])[:, None] + device_place * batch_pool.shape[0] == (
        batch_index[None, :]
    )
    local_rows = lax.dot_general(
        chosen.astype(jnp.bfloat16),
        batch_pool,
        (((0,), (0,)), ((), ())),
        preferred_element_type=jnp.float32,
    ).astype(jnp.bfloat16)
    pieces = [local_rows] + [flip(local_rows, "centre", 2 * k) for k in range(1, far_size)]

    base = coefficients.T
    first = jnp.reshape(centre_place * centre_pool.shape[0], (1,)).astype(jnp.int32)
    index = centre_index.reshape(1, -1)
    placed, pool_square, index, pool = place_coefficients(first, index, base, centre_pool)
    placed, *pieces = lax.optimization_barrier((placed, *pieces))
    placed_targets = jnp.where(
        jnp.arange(rows) // own_count == far_place, jnp.tile(targets.T, (1, far_size)), 0.0
    )

    side = jnp.zeros((rows, batch_pool.shape[1]), jnp.bfloat16)
    for k, piece in enumerate(pieces):
        side = lax.dynamic_update_slice_in_dim(side, piece, (far_place ^ k) * own_count, axis=0)
    other = flip(side, "centre", 1)
    terms = pool_terms(side, pool, pool_square, placed)
    other_terms = pool_terms(after(other, terms), pool, pool_square, placed)
    foreign = [flip(side, "batch", k) for k in range(1, batch_size)] if hold_all else []

    total = terms - placed_targets + flip(other_terms, "centre", 1)
    count = index.shape[1]
    cuts = far_size.bit_length() - 1 if count % (LANES * far_size) == 0 else 1
    picked = []
    distance = 2
    while distance < centre_size:
        if len(picked) < cuts:
            at, size = len(picked) * (count // cuts), count // cuts
            picked.append(pick_rows(after(index, total), pool, at, size))
        total = after(total + flip(total, "centre", distance), *picked[-1])
        distance *= 2
    if hold_all:
        foreign = lax.optimization_barrier((picked[-1][0], *foreign))[1:]
        side_rows = jnp.concatenate(foreign, axis=0)
        other_rows = flip(side_rows, "centre", 1)
    kernel = kernel_block([side, other], picked)
    total, kernel = lax.optimization_barrier((total, kernel))
    residual = lax.dynamic_slice_in_dim(total, far_place * own_count, own_count, axis=1).T
    residual_side = total.astype(jnp.bfloat16)

    step = 8.0 / math.sqrt(batch_total)
    if hold_all:
        kernel_side = kernel_block([after(side_rows, total)], picked)
        kernel_other = kernel_block([after(other_rows, total)], picked)
        parts = [residual_side] + [flip(residual_side, "batch", k) for k in range(1, batch_size)]
        kernel_side, kernel_other, *parts = lax.optimization_barrier(
            (kernel_side, kernel_other, *parts)
        )
        others = [flip(part, "centre", 1) for part in parts]
        updated = descend(base, kernel, kernel_side, parts, 0, step, fetch=True)
        updated = descend(updated, kernel, kernel_other, others, rows, step, store=True)
    else:
        other_part = flip(residual_side, "centre", 1)
        change = descend(jnp.zeros_like(base), kernel, kernel, [residual_side], 0, step)
        change = descend(change, kernel, kernel, [other_part], rows, step)
        updated = base + lax.psum(change, "batch")
    return (updated.T, residual)


def solution(mesh):
    return jax.shard_map(
        on_device,
        mesh=mesh,
        in_specs=(
            P(("batch", "centre"), None),
            P(("batch", "centre")),
            P("centre", None),
            P("centre"),
            P(("batch", "centre"), None),
            P("centre", None),
        ),
        out_specs=(P("centre", None), P(("batch", "centre"), None)),
        check_vma=False,
    )
```

```python
import functools
import math

import jax
import jax.numpy as jnp
from jax import lax
from jax.experimental import pallas as pl
from jax.experimental.pallas import tpu as pltpu
from jax.sharding import PartitionSpec as P

LANES = 128


def flip(value, axis, distance):
    count = lax.axis_size(axis)
    return lax.ppermute(value, axis, [(i, i ^ distance) for i in range(count)])


def after(value, *others):
    return lax.optimization_barrier((value,) + others)[0]


def contract_last(left, right):
    return lax.dot_general(
        left, right, (((1,), (1,)), ((), ())), preferred_element_type=jnp.float32
    )


def spans(total, most):
    return [(at, min(most, total - at)) for at in range(0, total, most)]


WHOLE = pl.BlockSpec(memory_space=pltpu.VMEM)
SCALARS = pl.BlockSpec(memory_space=pltpu.SMEM)
FAR = pl.BlockSpec(memory_space=pltpu.HBM)


def call(body, operands, outputs, scratch=(), limit=28):
    arrays = [array for array, _ in operands]
    shapes = [jax.ShapeDtypeStruct(shape, dtype) for shape, dtype, _ in outputs]
    return pl.pallas_call(
        body,
        in_specs=[place for _, place in operands],
        out_specs=[place for _, _, place in outputs],
        out_shape=shapes,
        scratch_shapes=list(scratch),
        cost_estimate=pl.CostEstimate(flops=1024, bytes_accessed=1024, transcendentals=0),
        compiler_params=pltpu.CompilerParams(vmem_limit_bytes=limit << 20),
    )(*arrays)


def turned(column):
    return jnp.concatenate(
        [
            jnp.broadcast_to(column[at : at + LANES], (LANES, LANES)).T[:1]
            for at in range(0, column.shape[0], LANES)
        ],
        axis=1,
    )


def pool_rows(pool_ref, at, size):
    if at + size <= pool_ref.shape[0]:
        return pool_ref[at : at + size, :]
    place = lax.broadcasted_iota(jnp.int32, (size, pool_ref.shape[1]), 0)
    rows = jnp.zeros(place.shape, jnp.float32)
    for row in range(at, pool_ref.shape[0]):
        rows = jnp.where(place == row - at, pool_ref[row : row + 1, :].astype(jnp.float32), rows)
    return rows.astype(jnp.bfloat16)


def place_body(first_ref, index_far, base_far, pool_far, *refs):
    placed_ref, square_ref, index_ref, pool_ref, base_ref, done_ref = refs
    fetches = [
        pltpu.make_async_copy(far, near, done_ref.at[turn])
        for turn, (far, near) in enumerate(
            [(index_far, index_ref), (base_far, base_ref), (pool_far, pool_ref)]
        )
    ]
    for fetch in fetches:
        fetch.start()
    fetches[0].wait()
    index = index_ref[...] - first_ref[0]
    index_ref[...] = index
    fetches[1].wait()
    half = base_ref[...].astype(jnp.bfloat16)
    for at, size in spans(placed_ref.shape[1], 2 * LANES):
        place = lax.broadcasted_iota(jnp.int32, (size, index.shape[1]), 0) + at
        chosen = jnp.where(index == place, 1.0, 0.0).astype(jnp.bfloat16)
        placed_ref[:, at : at + size] = contract_last(half, chosen).astype(jnp.bfloat16)
        if at == 0:
            fetches[2].wait()
        rows = pool_rows(pool_ref, at, size).astype(jnp.float32)
        square_ref[:, at : at + size] = turned(jnp.sum(rows * rows, axis=1, keepdims=True))


def place_coefficients(first, index, base, pool):
    width = -(-pool.shape[0] // LANES) * LANES
    return call(
        place_body,
        [(first, SCALARS), (index, FAR), (base, FAR), (pool, FAR)],
        [
            ((base.shape[0], width), jnp.bfloat16, WHOLE),
            ((1, width), jnp.float32, WHOLE),
            (index.shape, jnp.int32, WHOLE),
            (pool.shape, jnp.bfloat16, WHOLE),
        ],
        [pltpu.VMEM(base.shape, jnp.float32), pltpu.SemaphoreType.DMA((3,))],
        limit=44,
    )


def kernel_of(squared):
    return jnp.exp(-jnp.sqrt(jnp.maximum(squared, 0.0))).astype(jnp.bfloat16)


def column_of(row):
    return jnp.concatenate(
        [
            jnp.broadcast_to(row[:, at : at + LANES], (LANES, LANES)).T
            for at in range(0, row.shape[1], LANES)
        ],
        axis=0,
    )


def terms_body(samples_ref, pool_ref, square_ref, placed_ref, terms_ref, kernel_ref):
    samples = samples_ref[...]
    wide = samples.astype(jnp.float32)
    own_square = turned(jnp.sum(wide * wide, axis=1, keepdims=True))
    for at, size in spans(placed_ref.shape[1], 4 * LANES):
        cross = contract_last(pool_rows(pool_ref, at, size), samples)
        pool_square = column_of(square_ref[:, at : at + size])[:, :1]
        kernel_ref[at : at + size, :] = kernel_of(pool_square + own_square - 2.0 * cross)
    terms_ref[...] = jnp.dot(
        placed_ref[...], kernel_ref[...], preferred_element_type=jnp.float32
    )


def pool_terms(samples, pool, square, placed):
    return call(
        terms_body,
        [(samples, WHOLE), (pool, WHOLE), (square, WHOLE), (placed, WHOLE)],
        [((placed.shape[0], samples.shape[0]), jnp.float32, WHOLE)],
        [pltpu.VMEM((placed.shape[1], samples.shape[0]), jnp.bfloat16)],
    )[0]


def pick_body(first, index_ref, pool_ref, side_ref, other_ref, rows_ref, square_ref, kernel_ref):
    whole = pool_ref.shape[0] // LANES * LANES
    samples = jnp.concatenate([side_ref[...], other_ref[...]], axis=0)
    wide = samples.astype(jnp.float32)
    own_square = jnp.sum(wide * wide, axis=1, keepdims=True)
    for at, size in spans(rows_ref.shape[0], 4 * LANES):
        wanted = column_of(index_ref[:, first + at : first + at + size])
        lane = lax.broadcasted_iota(jnp.int32, (size, LANES), 1)
        chosen = jnp.concatenate(
            [
                jnp.where(wanted == lane + part, 1.0, 0.0).astype(jnp.bfloat16)
                for part in range(0, whole, LANES)
            ],
            axis=1,
        )
        rows = jnp.dot(chosen, pool_ref[:whole, :], preferred_element_type=jnp.float32)
        for row in range(whole, pool_ref.shape[0]):
            rows = rows + jnp.where(
                wanted[:, :1] == row, pool_ref[row : row + 1, :].astype(jnp.float32), 0.0
            )
        half = rows.astype(jnp.bfloat16)
        square = turned(jnp.sum(rows * rows, axis=1, keepdims=True))
        rows_ref[at : at + size, :] = half
        square_ref[:, at : at + size] = square
        kernel_ref[:, at : at + size] = kernel_of(
            own_square + square - 2.0 * contract_last(samples, half)
        )


def pick_rows(index, pool, side, other, first, count):
    rows = side.shape[0] + other.shape[0]
    return call(
        functools.partial(pick_body, first),
        [(index, WHOLE), (pool, WHOLE), (side, WHOLE), (other, WHOLE)],
        [
            ((count, pool.shape[1]), jnp.bfloat16, WHOLE),
            ((1, count), jnp.float32, WHOLE),
            ((rows, count), jnp.bfloat16, WHOLE),
        ],
    )


def block_body(parts, *refs):
    samples = jnp.concatenate([ref[...] for ref in refs[:parts]], axis=0)
    kernel_ref = refs[-1]
    wide = samples.astype(jnp.float32)
    own_square = jnp.sum(wide * wide, axis=1, keepdims=True)
    start = 0
    for rows_ref, square_ref in zip(refs[parts:-1:2], refs[parts + 1 : -1 : 2]):
        for at, size in spans(rows_ref.shape[0], 2 * LANES):
            cross = contract_last(samples, rows_ref[at : at + size, :])
            kernel = kernel_of(own_square + square_ref[:, at : at + size] - 2.0 * cross)
            kernel_ref[:, start + at : start + at + size] = kernel
        start += rows_ref.shape[0]


def kernel_block(samples, picked):
    rows = sum(part.shape[0] for part in samples)
    count = sum(square.shape[1] for _, square, _ in picked)
    return call(
        functools.partial(block_body, len(samples)),
        [(part, WHOLE) for part in samples]
        + [(array, WHOLE) for each in picked for array in each[:2]],
        [((rows, count), jnp.bfloat16, WHOLE)],
    )[0]


def descend_body(step, owns, parts, first, fetch, store, base_ref, rest_ref, *refs):
    own_refs, refs = refs[:owns], refs[owns:]
    out_ref, scratch = refs[parts], refs[parts + 1 :]
    cuts = spans(base_ref.shape[1], 4 * LANES)

    def copies(source, target, done_ref):
        return [
            pltpu.make_async_copy(
                source.at[:, pl.ds(at, size)], target.at[:, pl.ds(at, size)], done_ref.at[turn]
            )
            for turn, (at, size) in enumerate(cuts)
        ]

    near_ref, held_ref, fetches, stores = base_ref, out_ref, [], []
    if fetch:
        near_ref = scratch[0]
        fetches = copies(base_ref, near_ref, scratch[1])
    if store:
        held_ref = scratch[0]
        stores = copies(held_ref, out_ref, scratch[1])
    for copy in fetches:
        copy.start()
    own_part = refs[0][...]
    if parts > 1:
        rest_parts = jnp.concatenate([ref[...] for ref in refs[1:parts]], axis=1)
    own_count = own_refs[0].shape[1]
    for turn, (at, size) in enumerate(cuts):
        own_ref, own_at = own_refs[at // own_count], at % own_count
        own = own_ref[first : first + own_part.shape[1], own_at : own_at + size]
        gradient = jnp.dot(own_part, own, preferred_element_type=jnp.float32)
        if parts > 1:
            gradient = gradient + jnp.dot(
                rest_parts, rest_ref[:, at : at + size], preferred_element_type=jnp.float32
            )
        if fetch:
            fetches[turn].wait()
        held_ref[:, at : at + size] = near_ref[:, at : at + size] - step * gradient
        if store:
            stores[turn].start()
    for copy in stores:
        copy.wait()


def descend(base, owns, rest, residuals, first, step, fetch=False, store=False):
    scratch = []
    if fetch or store:
        turns = len(spans(base.shape[1], 4 * LANES))
        scratch = [pltpu.VMEM(base.shape, jnp.float32), pltpu.SemaphoreType.DMA((turns,))]
    body = functools.partial(descend_body, step, len(owns), len(residuals), first, fetch, store)
    return call(
        body,
        [(base, FAR if fetch else WHOLE), (rest, WHOLE)]
        + [(array, WHOLE) for array in [*owns, *residuals]],
        [(base.shape, jnp.float32, FAR if store else WHOLE)],
        scratch,
        limit=48 if fetch else 28,
    )[0]


def on_device(batch_pool, batch_index, centre_pool, centre_index, targets, coefficients):
    own_count = batch_index.shape[0]
    batch_size, centre_size = lax.axis_size("batch"), lax.axis_size("centre")
    batch_place, centre_place = lax.axis_index("batch"), lax.axis_index("centre")
    device_place = batch_place * centre_size + centre_place
    batch_total = own_count * batch_size * centre_size
    far_size, far_place = centre_size // 2, centre_place // 2
    rows = far_size * own_count
    hold_all = batch_total * (centre_index.shape[0] + batch_pool.shape[1]) * 2 <= 1 << 24

    chosen = (batch_index - device_place * batch_pool.shape[0])[:, None] == jnp.arange(
        batch_pool.shape[0]
    )
    local_rows = jnp.dot(
        chosen.astype(jnp.bfloat16), batch_pool, preferred_element_type=jnp.float32
    ).astype(jnp.bfloat16)
    pieces = [local_rows] + [flip(local_rows, "centre", 2 * k) for k in range(1, far_size)]

    base = coefficients.T
    first = jnp.reshape(centre_place * centre_pool.shape[0], (1,)).astype(jnp.int32)
    index = centre_index.reshape(1, -1)
    placed, pool_square, index, pool = place_coefficients(first, index, base, centre_pool)
    placed, *pieces = lax.optimization_barrier((placed, *pieces))
    placed_targets = jnp.where(
        jnp.arange(rows) // own_count == far_place, jnp.tile(targets.T, (1, far_size)), 0.0
    )

    side = jnp.zeros((rows, batch_pool.shape[1]), jnp.bfloat16)
    for k, piece in enumerate(pieces):
        side = lax.dynamic_update_slice_in_dim(side, piece, (far_place ^ k) * own_count, axis=0)
    other = flip(side, "centre", 1)
    terms = pool_terms(side, pool, pool_square, placed)
    other_terms = pool_terms(after(other, terms), pool, pool_square, placed)
    foreign = [flip(side, "batch", k) for k in range(1, batch_size)] if hold_all else []

    total = terms - placed_targets + flip(other_terms, "centre", 1)
    count = index.shape[1]
    cuts = far_size.bit_length() - 1 if count % (LANES * far_size) == 0 else 1
    picked = []
    distance = 2
    while distance < centre_size:
        if len(picked) < cuts:
            at, size = len(picked) * (count // cuts), count // cuts
            picked.append(pick_rows(after(index, total), pool, side, other, at, size))
        total = after(total + flip(total, "centre", distance), *picked[-1])
        distance *= 2
    if hold_all:
        foreign = lax.optimization_barrier((total, *foreign))[1:]
        side_rows = jnp.concatenate(foreign, axis=0)
        other_rows = flip(side_rows, "centre", 1)
    kernels = [kernel for _, _, kernel in picked]
    residual = lax.dynamic_slice_in_dim(total, far_place * own_count, own_count, axis=1).T
    residual_side = total.astype(jnp.bfloat16)

    step = 8.0 / math.sqrt(batch_total)
    if hold_all:
        kernel_side = kernel_block([side_rows], picked)
        kernel_other = kernel_block([other_rows], picked)
        parts = [residual_side] + [flip(residual_side, "batch", k) for k in range(1, batch_size)]
        kernel_side, kernel_other, *parts = lax.optimization_barrier(
            (kernel_side, kernel_other, *parts)
        )
        others = [flip(part, "centre", 1) for part in parts]
        updated = descend(base, kernels, kernel_side, parts, 0, step, fetch=True)
        updated = descend(updated, kernels, kernel_other, others, rows, step, store=True)
    else:
        other_part = flip(residual_side, "centre", 1)
        change = descend(jnp.zeros_like(base), kernels, kernels[0], [residual_side], 0, step)
        change = descend(change, kernels, kernels[0], [other_part], rows, step)
        updated = base + lax.psum(change, "batch")
    return (updated.T, residual)


def solution(mesh):
    return jax.shard_map(
        on_device,
        mesh=mesh,
        in_specs=(
            P(("batch", "centre"), None),
            P(("batch", "centre")),
            P("centre", None),
            P("centre"),
            P(("batch", "centre"), None),
            P("centre", None),
        ),
        out_specs=(P("centre", None), P(("batch", "centre"), None)),
        check_vma=False,
    )
```

```python
import functools
import math

import jax
import jax.numpy as jnp
from jax import lax
from jax.experimental import pallas as pl
from jax.experimental.pallas import tpu as pltpu
from jax.sharding import PartitionSpec as P

LANES = 128


def flip(value, axis, distance):
    count = lax.axis_size(axis)
    return lax.ppermute(value, axis, [(i, i ^ distance) for i in range(count)])


def after(value, *others):
    return lax.optimization_barrier((value,) + others)[0]


def contract_last(left, right):
    return lax.dot_general(
        left, right, (((1,), (1,)), ((), ())), preferred_element_type=jnp.float32
    )


def spans(total, most):
    return [(at, min(most, total - at)) for at in range(0, total, most)]


def tiles(count):
    return -(-count // LANES) * LANES


WHOLE = pl.BlockSpec(memory_space=pltpu.VMEM)
SCALARS = pl.BlockSpec(memory_space=pltpu.SMEM)
FAR = pl.BlockSpec(memory_space=pltpu.HBM)


def call(body, operands, outputs, scratch=(), limit=28):
    arrays = [array for array, _ in operands]
    shapes = [jax.ShapeDtypeStruct(shape, dtype) for shape, dtype, _ in outputs]
    return pl.pallas_call(
        body,
        in_specs=[place for _, place in operands],
        out_specs=[place for _, _, place in outputs],
        out_shape=shapes,
        scratch_shapes=list(scratch),
        cost_estimate=pl.CostEstimate(flops=1024, bytes_accessed=1024, transcendentals=0),
        compiler_params=pltpu.CompilerParams(vmem_limit_bytes=limit << 20),
    )(*arrays)


def turned(column):
    return jnp.concatenate(
        [
            jnp.broadcast_to(column[at : at + LANES], (LANES, LANES)).T[:1]
            for at in range(0, column.shape[0], LANES)
        ],
        axis=1,
    )


def pool_rows(pool_ref, at, size):
    if at + size <= pool_ref.shape[0]:
        return pool_ref[at : at + size, :]
    place = lax.broadcasted_iota(jnp.int32, (size, pool_ref.shape[1]), 0)
    rows = jnp.zeros(place.shape, jnp.float32)
    for row in range(at, pool_ref.shape[0]):
        rows = jnp.where(place == row - at, pool_ref[row : row + 1, :].astype(jnp.float32), rows)
    return rows.astype(jnp.bfloat16)


def place_body(first_ref, index_in, base_ref, pool_far, *refs):
    placed_ref, square_ref, index_ref, pool_ref, done_ref = refs
    fetch = pltpu.make_async_copy(pool_far, pool_ref, done_ref)
    fetch.start()
    index = index_in[...] - first_ref[0]
    index_ref[...] = index
    half = base_ref[...].astype(jnp.bfloat16)
    cuts = spans(placed_ref.shape[1], 2 * LANES)
    left, arrival = list(cuts), min(3, len(cuts) - 1)
    for turn, (at, size) in enumerate(cuts):
        place = lax.broadcasted_iota(jnp.int32, (size, index.shape[1]), 0) + at
        chosen = jnp.where(index == place, 1.0, 0.0).astype(jnp.bfloat16)
        placed_ref[:, at : at + size] = contract_last(half, chosen).astype(jnp.bfloat16)
        if turn == arrival:
            fetch.wait()
        share = -(-len(left) // (len(cuts) - turn)) if turn >= arrival else 0
        for from_row, count in left[:share]:
            rows = pool_rows(pool_ref, from_row, count).astype(jnp.float32)
            square_ref[:, from_row : from_row + count] = turned(
                jnp.sum(rows * rows, axis=1, keepdims=True)
            )
        left = left[share:]


def place_coefficients(first, index, base, pool):
    width = tiles(pool.shape[0])
    return call(
        place_body,
        [(first, SCALARS), (index, WHOLE), (base, WHOLE), (pool, FAR)],
        [
            ((base.shape[0], width), jnp.bfloat16, WHOLE),
            ((1, width), jnp.float32, WHOLE),
            (index.shape, jnp.int32, WHOLE),
            (pool.shape, jnp.bfloat16, WHOLE),
        ],
        [pltpu.SemaphoreType.DMA(())],
        limit=44,
    )


def turn_over(source_ref, target_ref):
    for row in range(0, source_ref.shape[0], LANES):
        for column in range(0, source_ref.shape[1], LANES):
            target_ref[column : column + LANES, row : row + LANES] = source_ref[
                row : row + LANES, column : column + LANES
            ].T


def arrange_body(place_ref, targets_ref, *refs):
    pieces, (side_ref, placed_ref, wide_ref, tall_ref) = refs[:-4], refs[-4:]
    count = targets_ref.shape[0]
    for k, piece_ref in enumerate(pieces):
        at = pl.multiple_of((place_ref[0] ^ k) * count, count)
        side_ref[pl.ds(at, count), :] = piece_ref[...]
    wide_ref[...] = jnp.zeros_like(wide_ref)
    at = pl.multiple_of(place_ref[0] * count, count)
    wide_ref[pl.ds(at, count), : targets_ref.shape[1]] = targets_ref[...]
    turn_over(wide_ref, tall_ref)
    placed_ref[...] = tall_ref[: placed_ref.shape[0], : placed_ref.shape[1]]


def arrange(place, targets, pieces):
    count, outs = targets.shape
    rows = count * len(pieces)
    high, wide = tiles(rows), tiles(outs)
    return call(
        arrange_body,
        [(place, SCALARS), (targets, WHOLE)] + [(piece, WHOLE) for piece in pieces],
        [
            ((rows, pieces[0].shape[1]), jnp.bfloat16, WHOLE),
            ((outs, rows), jnp.float32, WHOLE),
        ],
        [pltpu.VMEM((high, wide), jnp.float32), pltpu.VMEM((wide, high), jnp.float32)],
    )


def own_body(place_ref, total_ref, own_ref, tall_ref, wide_ref):
    outs, rows = total_ref.shape
    count = own_ref.shape[0]
    tall_ref[...] = jnp.zeros_like(tall_ref)
    tall_ref[:outs, :rows] = total_ref[...]
    turn_over(tall_ref, wide_ref)
    at = pl.multiple_of(place_ref[0] * count, count)
    own_ref[...] = wide_ref[pl.ds(at, count), :outs]


def own_rows(place, total, count):
    outs, rows = total.shape
    high, wide = tiles(rows), tiles(outs)
    return call(
        own_body,
        [(place, SCALARS), (total, WHOLE)],
        [((count, outs), jnp.float32, WHOLE)],
        [pltpu.VMEM((wide, high), jnp.float32), pltpu.VMEM((high, wide), jnp.float32)],
    )[0]


def kernel_of(squared):
    return jnp.exp(-jnp.sqrt(jnp.maximum(squared, 0.0))).astype(jnp.bfloat16)


def column_of(row):
    return jnp.concatenate(
        [
            jnp.broadcast_to(row[:, at : at + LANES], (LANES, LANES)).T
            for at in range(0, row.shape[1], LANES)
        ],
        axis=0,
    )


def terms_body(samples_ref, pool_ref, square_ref, placed_ref, terms_ref, kernel_ref):
    samples = samples_ref[...]
    wide = samples.astype(jnp.float32)
    own_square = turned(jnp.sum(wide * wide, axis=1, keepdims=True))
    for at, size in spans(placed_ref.shape[1], 4 * LANES):
        cross = contract_last(pool_rows(pool_ref, at, size), samples)
        pool_square = column_of(square_ref[:, at : at + size])[:, :1]
        kernel_ref[at : at + size, :] = kernel_of(pool_square + own_square - 2.0 * cross)
    terms_ref[...] = jnp.dot(
        placed_ref[...], kernel_ref[...], preferred_element_type=jnp.float32
    )


def pool_terms(samples, pool, square, placed):
    return call(
        terms_body,
        [(samples, WHOLE), (pool, WHOLE), (square, WHOLE), (placed, WHOLE)],
        [((placed.shape[0], samples.shape[0]), jnp.float32, WHOLE)],
        [pltpu.VMEM((placed.shape[1], samples.shape[0]), jnp.bfloat16)],
    )[0]


def pick_body(first, index_ref, pool_ref, side_ref, other_ref, rows_ref, square_ref, kernel_ref):
    whole = pool_ref.shape[0] // LANES * LANES
    samples = jnp.concatenate([side_ref[...], other_ref[...]], axis=0)
    wide = samples.astype(jnp.float32)
    own_square = jnp.sum(wide * wide, axis=1, keepdims=True)
    for at, size in spans(rows_ref.shape[0], 4 * LANES):
        wanted = column_of(index_ref[:, first + at : first + at + size])
        lane = lax.broadcasted_iota(jnp.int32, (size, LANES), 1)
        chosen = jnp.concatenate(
            [
                jnp.where(wanted == lane + part, 1.0, 0.0).astype(jnp.bfloat16)
                for part in range(0, whole, LANES)
            ],
            axis=1,
        )
        rows = jnp.dot(chosen, pool_ref[:whole, :], preferred_element_type=jnp.float32)
        for row in range(whole, pool_ref.shape[0]):
            rows = rows + jnp.where(
                wanted[:, :1] == row, pool_ref[row : row + 1, :].astype(jnp.float32), 0.0
            )
        half = rows.astype(jnp.bfloat16)
        square = turned(jnp.sum(rows * rows, axis=1, keepdims=True))
        rows_ref[at : at + size, :] = half
        square_ref[:, at : at + size] = square
        kernel_ref[:, at : at + size] = kernel_of(
            own_square + square - 2.0 * contract_last(samples, half)
        )


def pick_rows(index, pool, side, other, first, count):
    rows = side.shape[0] + other.shape[0]
    return call(
        functools.partial(pick_body, first),
        [(index, WHOLE), (pool, WHOLE), (side, WHOLE), (other, WHOLE)],
        [
            ((count, pool.shape[1]), jnp.bfloat16, WHOLE),
            ((1, count), jnp.float32, WHOLE),
            ((rows, count), jnp.bfloat16, WHOLE),
        ],
    )


def block_body(parts, *refs):
    samples = jnp.concatenate([ref[...] for ref in refs[:parts]], axis=0)
    kernel_ref = refs[-1]
    wide = samples.astype(jnp.float32)
    own_square = jnp.sum(wide * wide, axis=1, keepdims=True)
    start = 0
    for rows_ref, square_ref in zip(refs[parts:-1:2], refs[parts + 1 : -1 : 2]):
        for at, size in spans(rows_ref.shape[0], 2 * LANES):
            cross = contract_last(samples, rows_ref[at : at + size, :])
            kernel = kernel_of(own_square + square_ref[:, at : at + size] - 2.0 * cross)
            kernel_ref[:, start + at : start + at + size] = kernel
        start += rows_ref.shape[0]


def kernel_block(samples, picked):
    rows = sum(part.shape[0] for part in samples)
    count = sum(square.shape[1] for _, square, _ in picked)
    return call(
        functools.partial(block_body, len(samples)),
        [(part, WHOLE) for part in samples]
        + [(array, WHOLE) for each in picked for array in each[:2]],
        [((rows, count), jnp.bfloat16, WHOLE)],
    )[0]


def descend_body(step, owns, parts, first, fetch, store, base_ref, rest_ref, *refs):
    own_refs, refs = refs[:owns], refs[owns:]
    out_ref, scratch = refs[parts], refs[parts + 1 :]
    cuts = spans(base_ref.shape[1], 4 * LANES)

    def copies(source, target, done_ref):
        return [
            pltpu.make_async_copy(
                source.at[:, pl.ds(at, size)], target.at[:, pl.ds(at, size)], done_ref.at[turn]
            )
            for turn, (at, size) in enumerate(cuts)
        ]

    near_ref, held_ref, fetches, stores = base_ref, out_ref, [], []
    if fetch:
        near_ref = scratch[0]
        fetches = copies(base_ref, near_ref, scratch[1])
    if store:
        held_ref = scratch[0]
        stores = copies(held_ref, out_ref, scratch[1])
    for copy in fetches:
        copy.start()
    own_part = refs[0][...]
    if parts > 1:
        rest_parts = jnp.concatenate([ref[...] for ref in refs[1:parts]], axis=1)
    own_count = own_refs[0].shape[1]
    for turn, (at, size) in enumerate(cuts):
        own_ref, own_at = own_refs[at // own_count], at % own_count
        own = own_ref[first : first + own_part.shape[1], own_at : own_at + size]
        gradient = jnp.dot(own_part, own, preferred_element_type=jnp.float32)
        if parts > 1:
            gradient = gradient + jnp.dot(
                rest_parts, rest_ref[:, at : at + size], preferred_element_type=jnp.float32
            )
        if fetch:
            fetches[turn].wait()
        held_ref[:, at : at + size] = near_ref[:, at : at + size] - step * gradient
        if store:
            stores[turn].start()
    for copy in stores:
        copy.wait()


def descend(base, owns, rest, residuals, first, step, fetch=False, store=False):
    scratch = []
    if fetch or store:
        turns = len(spans(base.shape[1], 4 * LANES))
        scratch = [pltpu.VMEM(base.shape, jnp.float32), pltpu.SemaphoreType.DMA((turns,))]
    body = functools.partial(descend_body, step, len(owns), len(residuals), first, fetch, store)
    return call(
        body,
        [(base, FAR if fetch else WHOLE), (rest, WHOLE)]
        + [(array, WHOLE) for array in [*owns, *residuals]],
        [(base.shape, jnp.float32, FAR if store else WHOLE)],
        scratch,
        limit=48 if fetch else 28,
    )[0]


def on_device(batch_pool, batch_index, centre_pool, centre_index, targets, coefficients):
    own_count = batch_index.shape[0]
    batch_size, centre_size = lax.axis_size("batch"), lax.axis_size("centre")
    batch_place, centre_place = lax.axis_index("batch"), lax.axis_index("centre")
    device_place = batch_place * centre_size + centre_place
    batch_total = own_count * batch_size * centre_size
    far_size, far_place = centre_size // 2, lax.shift_right_logical(centre_place, 1)
    rows = far_size * own_count
    hold_all = batch_total * (centre_index.shape[0] + batch_pool.shape[1]) * 2 <= 1 << 24

    chosen = (batch_index - device_place * batch_pool.shape[0])[:, None] == jnp.arange(
        batch_pool.shape[0]
    )
    local_rows = jnp.dot(
        chosen.astype(jnp.bfloat16), batch_pool, preferred_element_type=jnp.float32
    ).astype(jnp.bfloat16)
    pieces = [local_rows] + [flip(local_rows, "centre", 2 * k) for k in range(1, far_size)]

    base = coefficients.T
    first = jnp.reshape(centre_place * centre_pool.shape[0], (1,)).astype(jnp.int32)
    place = jnp.reshape(far_place, (1,)).astype(jnp.int32)
    first, place = lax.optimization_barrier((first, place))
    index = centre_index.reshape(1, -1)
    placed, pool_square, index, pool = place_coefficients(first, index, base, centre_pool)
    placed, *pieces = lax.optimization_barrier((placed, *pieces))
    side, placed_targets = arrange(place, targets, pieces)
    other = flip(side, "centre", 1)
    terms = pool_terms(side, pool, pool_square, placed)
    other_terms = pool_terms(after(other, terms), pool, pool_square, placed)
    foreign = [flip(side, "batch", k) for k in range(1, batch_size)] if hold_all else []

    total = terms - placed_targets + flip(other_terms, "centre", 1)
    count = index.shape[1]
    cuts = far_size.bit_length() - 1 if count % (LANES * far_size) == 0 else 1
    picked = []
    distance = 2
    while distance < centre_size:
        if len(picked) < cuts:
            at, size = len(picked) * (count // cuts), count // cuts
            picked.append(pick_rows(after(index, total), pool, side, other, at, size))
        total = after(total + flip(total, "centre", distance), *picked[-1])
        distance *= 2
    if hold_all:
        foreign = lax.optimization_barrier((total, *foreign))[1:]
        side_rows = jnp.concatenate(foreign, axis=0)
        other_rows = flip(side_rows, "centre", 1)
    kernels = [kernel for _, _, kernel in picked]
    residual = own_rows(place, total, own_count)
    residual_side = total.astype(jnp.bfloat16)

    step = 8.0 / math.sqrt(batch_total)
    if hold_all:
        kernel_side = kernel_block([side_rows], picked)
        kernel_other = kernel_block([other_rows], picked)
        parts = [residual_side] + [flip(residual_side, "batch", k) for k in range(1, batch_size)]
        kernel_side, kernel_other, *parts = lax.optimization_barrier(
            (kernel_side, kernel_other, *parts)
        )
        others = [flip(part, "centre", 1) for part in parts]
        updated = descend(base, kernels, kernel_side, parts, 0, step, fetch=True)
        updated = descend(updated, kernels, kernel_other, others, rows, step, store=True)
    else:
        other_part = flip(residual_side, "centre", 1)
        change = descend(jnp.zeros_like(base), kernels, kernels[0], [residual_side], 0, step)
        change = descend(change, kernels, kernels[0], [other_part], rows, step)
        updated = base + lax.psum(change, "batch")
    return (updated.T, residual)


def solution(mesh):
    return jax.shard_map(
        on_device,
        mesh=mesh,
        in_specs=(
            P(("batch", "centre"), None),
            P(("batch", "centre")),
            P("centre", None),
            P("centre"),
            P(("batch", "centre"), None),
            P("centre", None),
        ),
        out_specs=(P("centre", None), P(("batch", "centre"), None)),
        check_vma=False,
    )
```

```python
import functools
import math

import jax
import jax.numpy as jnp
from jax import lax
from jax.experimental import pallas as pl
from jax.experimental.pallas import tpu as pltpu
from jax.sharding import PartitionSpec as P

LANES = 128


def flip(value, axis, distance):
    count = lax.axis_size(axis)
    return lax.ppermute(value, axis, [(i, i ^ distance) for i in range(count)])


def after(value, *others):
    return lax.optimization_barrier((value,) + others)[0]


def contract_last(left, right):
    return lax.dot_general(
        left, right, (((1,), (1,)), ((), ())), preferred_element_type=jnp.float32
    )


def spans(total, most):
    return [(at, min(most, total - at)) for at in range(0, total, most)]


def tiles(count):
    return -(-count // LANES) * LANES


WHOLE = pl.BlockSpec(memory_space=pltpu.VMEM)
SCALARS = pl.BlockSpec(memory_space=pltpu.SMEM)
FAR = pl.BlockSpec(memory_space=pltpu.HBM)


def call(body, operands, outputs, scratch=(), limit=28):
    arrays = [array for array, _ in operands]
    shapes = [jax.ShapeDtypeStruct(shape, dtype) for shape, dtype, _ in outputs]
    return pl.pallas_call(
        body,
        in_specs=[place for _, place in operands],
        out_specs=[place for _, _, place in outputs],
        out_shape=shapes,
        scratch_shapes=list(scratch),
        cost_estimate=pl.CostEstimate(flops=1024, bytes_accessed=1024, transcendentals=0),
        compiler_params=pltpu.CompilerParams(vmem_limit_bytes=limit << 20),
    )(*arrays)


def turned(column):
    return jnp.concatenate(
        [
            jnp.broadcast_to(column[at : at + LANES], (LANES, LANES)).T[:1]
            for at in range(0, column.shape[0], LANES)
        ],
        axis=1,
    )


def pool_rows(pool_ref, at, size):
    if at + size <= pool_ref.shape[0]:
        return pool_ref[at : at + size, :]
    place = lax.broadcasted_iota(jnp.int32, (size, pool_ref.shape[1]), 0)
    rows = jnp.zeros(place.shape, jnp.float32)
    for row in range(at, pool_ref.shape[0]):
        rows = jnp.where(place == row - at, pool_ref[row : row + 1, :].astype(jnp.float32), rows)
    return rows.astype(jnp.bfloat16)


def place_body(index_ref, base_ref, pool_far, placed_ref, square_ref, kept_ref, pool_ref, done_ref):
    fetch = pltpu.make_async_copy(pool_far, pool_ref, done_ref)
    fetch.start()
    index = index_ref[...]
    base = base_ref[...]
    kept_ref[...] = base
    half = base.astype(jnp.bfloat16)
    cuts = spans(placed_ref.shape[1], 2 * LANES)
    left, arrival = list(cuts), min(3, len(cuts) - 1)
    for turn, (at, size) in enumerate(cuts):
        place = lax.broadcasted_iota(jnp.int32, (size, index.shape[1]), 0) + at
        chosen = jnp.where(index == place, 1.0, 0.0).astype(jnp.bfloat16)
        placed_ref[:, at : at + size] = contract_last(half, chosen).astype(jnp.bfloat16)
        if turn == arrival:
            fetch.wait()
        share = -(-len(left) // (len(cuts) - turn)) if turn >= arrival else 0
        for from_row, count in left[:share]:
            rows = pool_rows(pool_ref, from_row, count).astype(jnp.float32)
            square_ref[:, from_row : from_row + count] = turned(
                jnp.sum(rows * rows, axis=1, keepdims=True)
            )
        left = left[share:]


def place_coefficients(index, base, pool):
    width = tiles(pool.shape[0])
    return call(
        place_body,
        [(index, WHOLE), (base, WHOLE), (pool, FAR)],
        [
            ((base.shape[0], width), jnp.bfloat16, WHOLE),
            ((1, width), jnp.float32, WHOLE),
            (base.shape, jnp.float32, WHOLE),
            (pool.shape, jnp.bfloat16, WHOLE),
        ],
        [pltpu.SemaphoreType.DMA(())],
        limit=41,
    )


def turn_over(source_ref, target_ref):
    for row in range(0, source_ref.shape[0], LANES):
        for column in range(0, source_ref.shape[1], LANES):
            target_ref[column : column + LANES, row : row + LANES] = source_ref[
                row : row + LANES, column : column + LANES
            ].T


def arrange_body(place_ref, targets_ref, *refs):
    pieces, (side_ref, placed_ref, wide_ref, tall_ref) = refs[:-4], refs[-4:]
    count = targets_ref.shape[0]
    for k, piece_ref in enumerate(pieces):
        at = pl.multiple_of((place_ref[0] ^ k) * count, count)
        side_ref[pl.ds(at, count), :] = piece_ref[...]
    wide_ref[...] = jnp.zeros_like(wide_ref)
    at = pl.multiple_of(place_ref[0] * count, count)
    wide_ref[pl.ds(at, count), : targets_ref.shape[1]] = targets_ref[...]
    turn_over(wide_ref, tall_ref)
    placed_ref[...] = tall_ref[: placed_ref.shape[0], : placed_ref.shape[1]]


def arrange(place, targets, pieces):
    count, outs = targets.shape
    rows = count * len(pieces)
    high, wide = tiles(rows), tiles(outs)
    return call(
        arrange_body,
        [(place, SCALARS), (targets, WHOLE)] + [(piece, WHOLE) for piece in pieces],
        [
            ((rows, pieces[0].shape[1]), jnp.bfloat16, WHOLE),
            ((outs, rows), jnp.float32, WHOLE),
        ],
        [pltpu.VMEM((high, wide), jnp.float32), pltpu.VMEM((wide, high), jnp.float32)],
    )


def kernel_of(squared):
    least = jnp.maximum(squared, 1e-30)
    return jnp.exp2(least * -math.log2(math.e) * lax.rsqrt(least)).astype(jnp.bfloat16)


def halves_and_squares(samples):
    wide = samples.astype(jnp.float32)
    return (wide * -2.0).astype(jnp.bfloat16), jnp.sum(wide * wide, axis=1, keepdims=True)


def column_of(row):
    return jnp.concatenate(
        [
            jnp.broadcast_to(row[:, at : at + LANES], (LANES, LANES)).T
            for at in range(0, row.shape[1], LANES)
        ],
        axis=0,
    )


def terms_body(side_ref, other_ref, pool_ref, square_ref, placed_ref, *refs):
    terms_ref, other_terms_ref, kernel_ref = refs
    samples = jnp.concatenate([side_ref[...], other_ref[...]], axis=0)
    samples, own_square = halves_and_squares(samples)
    own_square = turned(own_square)
    for at, size in spans(placed_ref.shape[1], 4 * LANES):
        cross = contract_last(pool_rows(pool_ref, at, size), samples)
        pool_square = column_of(square_ref[:, at : at + size])[:, :1]
        kernel_ref[at : at + size, :] = kernel_of(pool_square + own_square + cross)
    terms = jnp.dot(placed_ref[...], kernel_ref[...], preferred_element_type=jnp.float32)
    rows = side_ref.shape[0]
    terms_ref[...] = terms[:, :rows]
    other_terms_ref[...] = terms[:, rows:]


def pool_terms(side, other, pool, square, placed):
    outs, rows = placed.shape[0], side.shape[0]
    return call(
        terms_body,
        [(array, WHOLE) for array in (side, other, pool, square, placed)],
        [((outs, rows), jnp.float32, WHOLE)] * 2,
        [pltpu.VMEM((placed.shape[1], 2 * rows), jnp.bfloat16)],
    )


def pick_body(first, index_ref, pool_ref, side_ref, other_ref, rows_ref, square_ref, kernel_ref):
    whole = pool_ref.shape[0] // LANES * LANES
    samples = jnp.concatenate([side_ref[...], other_ref[...]], axis=0)
    samples, own_square = halves_and_squares(samples)
    for at, size in spans(rows_ref.shape[0], 8 * LANES):
        wanted = column_of(index_ref[:, first + at : first + at + size])
        lane = lax.broadcasted_iota(jnp.int32, (size, LANES), 1)
        chosen = jnp.concatenate(
            [
                jnp.where(wanted == lane + part, 1.0, 0.0).astype(jnp.bfloat16)
                for part in range(0, whole, LANES)
            ],
            axis=1,
        )
        rows = jnp.dot(chosen, pool_ref[:whole, :], preferred_element_type=jnp.float32)
        for row in range(whole, pool_ref.shape[0]):
            rows = rows + jnp.where(
                wanted[:, :1] == row, pool_ref[row : row + 1, :].astype(jnp.float32), 0.0
            )
        half = rows.astype(jnp.bfloat16)
        square = turned(jnp.sum(rows * rows, axis=1, keepdims=True))
        rows_ref[at : at + size, :] = half
        square_ref[:, at : at + size] = square
        kernel_ref[:, at : at + size] = kernel_of(
            own_square + square + contract_last(samples, half)
        )


def pick_rows(index, pool, side, other, first, count):
    rows = side.shape[0] + other.shape[0]
    return call(
        functools.partial(pick_body, first),
        [(index, WHOLE), (pool, WHOLE), (side, WHOLE), (other, WHOLE)],
        [
            ((count, pool.shape[1]), jnp.bfloat16, WHOLE),
            ((1, count), jnp.float32, WHOLE),
            ((rows, count), jnp.bfloat16, WHOLE),
        ],
    )


def block_body(parts, *refs):
    samples = jnp.concatenate([ref[...] for ref in refs[:parts]], axis=0)
    kernel_ref = refs[-1]
    samples, own_square = halves_and_squares(samples)
    start = 0
    for rows_ref, square_ref in zip(refs[parts:-1:2], refs[parts + 1 : -1 : 2]):
        for at, size in spans(rows_ref.shape[0], 2 * LANES):
            cross = contract_last(samples, rows_ref[at : at + size, :])
            kernel = kernel_of(own_square + square_ref[:, at : at + size] + cross)
            kernel_ref[:, start + at : start + at + size] = kernel
        start += rows_ref.shape[0]


def kernel_block(samples, picked):
    rows = sum(part.shape[0] for part in samples)
    count = sum(square.shape[1] for _, square, _ in picked)
    return call(
        functools.partial(block_body, len(samples)),
        [(part, WHOLE) for part in samples]
        + [(array, WHOLE) for each in picked for array in each[:2]],
        [((rows, count), jnp.bfloat16, WHOLE)],
    )[0]


def gradient_span(residual_ref, kernel_refs, owns, first, at, size):
    own_refs, rest_refs = kernel_refs[:owns], kernel_refs[owns:]
    span = own_refs[0].shape[1]
    own_ref, own_at = own_refs[at // span], at % span
    rows = residual_ref.shape[1] - sum(rest_ref.shape[0] for rest_ref in rest_refs)
    gradient = jnp.dot(
        residual_ref[:, :rows],
        own_ref[first : first + rows, own_at : own_at + size],
        preferred_element_type=jnp.float32,
    )
    for rest_ref in rest_refs:
        gradient = gradient + jnp.dot(
            residual_ref[:, rows:], rest_ref[:, at : at + size], preferred_element_type=jnp.float32
        )
    return gradient


def descend_body(step, owns, kernels, place_ref, total_ref, residual_ref, base_ref, *refs):
    kernel_refs, refs = refs[:kernels], refs[kernels:]
    out_ref, own_far, tall_ref, wide_ref, own_ref, done_ref = refs
    outs, rows = total_ref.shape
    count = own_ref.shape[0]
    tall_ref[...] = jnp.zeros_like(tall_ref)
    tall_ref[:outs, :rows] = total_ref[...]
    turn_over(tall_ref, wide_ref)
    at = pl.multiple_of(place_ref[0] * count, count)
    own_ref[...] = wide_ref[pl.ds(at, count), :outs]
    store = pltpu.make_async_copy(own_ref, own_far, done_ref)
    store.start()
    for at, size in spans(base_ref.shape[1], 4 * LANES):
        gradient = gradient_span(residual_ref, kernel_refs, owns, 0, at, size)
        out_ref[:, at : at + size] = base_ref[:, at : at + size] - step * gradient
    store.wait()


def descend(place, total, count, residual, base, owns, rests, step):
    outs, rows = total.shape
    high, wide = tiles(rows), tiles(outs)
    kernels = [*owns, *rests]
    return call(
        functools.partial(descend_body, step, len(owns), len(kernels)),
        [(place, SCALARS)] + [(array, WHOLE) for array in (total, residual, base, *kernels)],
        [(base.shape, jnp.float32, WHOLE), ((count, outs), jnp.float32, FAR)],
        [
            pltpu.VMEM((wide, high), jnp.float32),
            pltpu.VMEM((high, wide), jnp.float32),
            pltpu.VMEM((count, outs), jnp.float32),
            pltpu.SemaphoreType.DMA(()),
        ],
    )


def finish_body(step, owns, kernels, first, residual_ref, base_ref, *refs):
    kernel_refs, (out_far, held_ref, done_ref) = refs[:kernels], refs[kernels:]
    stores = []
    for turn, (at, size) in enumerate(spans(base_ref.shape[1], 4 * LANES)):
        gradient = gradient_span(residual_ref, kernel_refs, owns, first, at, size)
        held_ref[:, at : at + size] = base_ref[:, at : at + size] - step * gradient
        span = pl.ds(at, size)
        stores.append(
            pltpu.make_async_copy(held_ref.at[:, span], out_far.at[:, span], done_ref.at[turn])
        )
        stores[-1].start()
    for store in stores:
        store.wait()


def finish(residual, base, owns, rests, first, step):
    turns = len(spans(base.shape[1], 4 * LANES))
    kernels = [*owns, *rests]
    return call(
        functools.partial(finish_body, step, len(owns), len(kernels), first),
        [(array, WHOLE) for array in (residual, base, *kernels)],
        [(base.shape, jnp.float32, FAR)],
        [pltpu.VMEM(base.shape, jnp.float32), pltpu.SemaphoreType.DMA((turns,))],
    )[0]


def on_device(batch_pool, batch_index, centre_pool, centre_index, targets, coefficients):
    own_count = batch_index.shape[0]
    batch_size, centre_size = lax.axis_size("batch"), lax.axis_size("centre")
    batch_place, centre_place = lax.axis_index("batch"), lax.axis_index("centre")
    device_place = batch_place * centre_size + centre_place
    batch_total = own_count * batch_size * centre_size
    far_size, far_place = centre_size // 2, lax.shift_right_logical(centre_place, 1)
    rows = far_size * own_count
    hold_all = batch_total * (centre_index.shape[0] + batch_pool.shape[1]) * 2 <= 1 << 24

    count = centre_index.shape[0]
    indices = lax.optimization_barrier(
        jnp.concatenate(
            [
                centre_index - centre_place * centre_pool.shape[0],
                batch_index - device_place * batch_pool.shape[0],
            ]
        )
    )
    chosen = indices[count:, None] == jnp.arange(batch_pool.shape[0])
    local_rows = jnp.dot(
        chosen.astype(jnp.bfloat16), batch_pool, preferred_element_type=jnp.float32
    ).astype(jnp.bfloat16)
    pieces = [local_rows] + [flip(local_rows, "centre", 2 * k) for k in range(1, far_size)]

    place = jnp.reshape(far_place, (1,)).astype(jnp.int32)
    index, place = lax.optimization_barrier((indices[:count].reshape(1, -1), place))
    placed, pool_square, base, pool = place_coefficients(index, coefficients.T, centre_pool)
    placed, *pieces = lax.optimization_barrier((placed, *pieces))
    side, placed_targets = arrange(place, targets, pieces)
    other = flip(side, "centre", 1)
    terms, other_terms = pool_terms(side, other, pool, pool_square, placed)
    foreign = [flip(side, "batch", k) for k in range(1, batch_size)] if hold_all else []

    total = terms - placed_targets + flip(other_terms, "centre", 1)
    cuts = far_size.bit_length() - 1 if count % (LANES * far_size) == 0 else 1
    picked = []
    distance = 2
    while distance < centre_size:
        if len(picked) < cuts:
            at, size = len(picked) * (count // cuts), count // cuts
            picked.append(pick_rows(after(index, total), pool, side, other, at, size))
        total = after(total + flip(total, "centre", distance), *picked[-1])
        distance *= 2
    if hold_all:
        foreign = lax.optimization_barrier((total, *foreign))[1:]
        side_rows = jnp.concatenate(foreign, axis=0)
        other_rows = flip(side_rows, "centre", 1)
    kernels = [kernel for _, _, kernel in picked]
    residual_side = total.astype(jnp.bfloat16)
    rests, other_rests = [], []
    if hold_all:
        rests, other_rests = [kernel_block([side_rows], picked)], [kernel_block([other_rows], picked)]
        parts = [residual_side] + [flip(residual_side, "batch", k) for k in range(1, batch_size)]
        rests, other_rests, parts = lax.optimization_barrier((rests, other_rests, parts))
        residual_side = jnp.concatenate(parts, axis=1)
    residual_other = flip(residual_side, "centre", 1)

    step = 8.0 / math.sqrt(batch_total)
    start = base if hold_all else jnp.zeros_like(base)
    updated, residual = descend(
        place, total, own_count, residual_side, start, kernels, rests, step
    )
    updated = finish(residual_other, updated, kernels, other_rests, rows, step)
    if not hold_all:
        updated = base + lax.psum(updated, "batch")
    return (updated.T, residual)


def solution(mesh):
    return jax.shard_map(
        on_device,
        mesh=mesh,
        in_specs=(
            P(("batch", "centre"), None),
            P(("batch", "centre")),
            P("centre", None),
            P("centre"),
            P(("batch", "centre"), None),
            P("centre", None),
        ),
        out_specs=(P("centre", None), P(("batch", "centre"), None)),
        check_vma=False,
    )
```

```python
import functools
import math

import jax
import jax.numpy as jnp
from jax import lax
from jax.experimental import pallas as pl
from jax.experimental.pallas import tpu as pltpu
from jax.sharding import PartitionSpec as P

LANES = 128


def flip(value, axis, distance):
    count = lax.axis_size(axis)
    return lax.ppermute(value, axis, [(i, i ^ distance) for i in range(count)])


def after(value, *others):
    return lax.optimization_barrier((value,) + others)[0]


def contract_last(left, right):
    return lax.dot_general(
        left, right, (((1,), (1,)), ((), ())), preferred_element_type=jnp.float32
    )


def spans(total, most):
    return [(at, min(most, total - at)) for at in range(0, total, most)]


def tiles(count):
    return -(-count // LANES) * LANES


WHOLE = pl.BlockSpec(memory_space=pltpu.VMEM)
SCALARS = pl.BlockSpec(memory_space=pltpu.SMEM)
FAR = pl.BlockSpec(memory_space=pltpu.HBM)


def call(body, operands, outputs, scratch=(), limit=28):
    arrays = [array for array, _ in operands]
    shapes = [jax.ShapeDtypeStruct(shape, dtype) for shape, dtype, _ in outputs]
    return pl.pallas_call(
        body,
        in_specs=[place for _, place in operands],
        out_specs=[place for _, _, place in outputs],
        out_shape=shapes,
        scratch_shapes=list(scratch),
        cost_estimate=pl.CostEstimate(flops=1024, bytes_accessed=1024, transcendentals=0),
        compiler_params=pltpu.CompilerParams(vmem_limit_bytes=limit << 20),
    )(*arrays)


def turned(column):
    return jnp.concatenate(
        [
            jnp.broadcast_to(column[at : at + LANES], (LANES, LANES)).T[:1]
            for at in range(0, column.shape[0], LANES)
        ],
        axis=1,
    )


def pool_rows(pool_ref, at, size):
    if at + size <= pool_ref.shape[0]:
        return pool_ref[at : at + size, :]
    place = lax.broadcasted_iota(jnp.int32, (size, pool_ref.shape[1]), 0)
    rows = jnp.zeros(place.shape, jnp.float32)
    for row in range(at, pool_ref.shape[0]):
        rows = jnp.where(place == row - at, pool_ref[row : row + 1, :].astype(jnp.float32), rows)
    return rows.astype(jnp.bfloat16)


def place_body(index_ref, base_ref, pool_far, placed_ref, square_ref, kept_ref, pool_ref, done_ref):
    fetch = pltpu.make_async_copy(pool_far, pool_ref, done_ref)
    fetch.start()
    index = index_ref[...]
    base = base_ref[...]
    kept_ref[...] = base
    half = base.astype(jnp.bfloat16)
    cuts = spans(placed_ref.shape[1], 2 * LANES)
    left, arrival = list(cuts), min(3, len(cuts) - 1)
    for turn, (at, size) in enumerate(cuts):
        place = lax.broadcasted_iota(jnp.int32, (size, index.shape[1]), 0) + at
        chosen = jnp.where(index == place, 1.0, 0.0).astype(jnp.bfloat16)
        placed_ref[:, at : at + size] = contract_last(half, chosen).astype(jnp.bfloat16)
        if turn == arrival:
            fetch.wait()
        share = -(-len(left) // (len(cuts) - turn)) if turn >= arrival else 0
        for from_row, count in left[:share]:
            rows = pool_rows(pool_ref, from_row, count).astype(jnp.float32)
            square_ref[:, from_row : from_row + count] = turned(
                jnp.sum(rows * rows, axis=1, keepdims=True)
            )
        left = left[share:]


def place_coefficients(index, base, pool):
    width = tiles(pool.shape[0])
    return call(
        place_body,
        [(index, WHOLE), (base, WHOLE), (pool, FAR)],
        [
            ((base.shape[0], width), jnp.bfloat16, WHOLE),
            ((1, width), jnp.float32, WHOLE),
            (base.shape, jnp.float32, WHOLE),
            (pool.shape, jnp.bfloat16, WHOLE),
        ],
        [pltpu.SemaphoreType.DMA(())],
        limit=41,
    )


def turn_over(source_ref, target_ref):
    for row in range(0, source_ref.shape[0], LANES):
        for column in range(0, source_ref.shape[1], LANES):
            target_ref[column : column + LANES, row : row + LANES] = source_ref[
                row : row + LANES, column : column + LANES
            ].T


def arrange_body(place_ref, targets_ref, *refs):
    pieces, (side_ref, placed_ref, wide_ref, tall_ref) = refs[:-4], refs[-4:]
    count = targets_ref.shape[0]
    for k, piece_ref in enumerate(pieces):
        at = pl.multiple_of((place_ref[0] ^ k) * count, count)
        side_ref[pl.ds(at, count), :] = piece_ref[...]
    wide_ref[...] = jnp.zeros_like(wide_ref)
    at = pl.multiple_of(place_ref[0] * count, count)
    wide_ref[pl.ds(at, count), : targets_ref.shape[1]] = targets_ref[...]
    turn_over(wide_ref, tall_ref)
    placed_ref[...] = tall_ref[: placed_ref.shape[0], : placed_ref.shape[1]]


def arrange(place, targets, pieces):
    count, outs = targets.shape
    rows = count * len(pieces)
    high, wide = tiles(rows), tiles(outs)
    return call(
        arrange_body,
        [(place, SCALARS), (targets, WHOLE)] + [(piece, WHOLE) for piece in pieces],
        [
            ((rows, pieces[0].shape[1]), jnp.bfloat16, WHOLE),
            ((outs, rows), jnp.float32, WHOLE),
        ],
        [pltpu.VMEM((high, wide), jnp.float32), pltpu.VMEM((wide, high), jnp.float32)],
    )


def kernel_of(squared):
    least = jnp.maximum(squared, 1e-30)
    return jnp.exp2(least * -math.log2(math.e) * lax.rsqrt(least)).astype(jnp.bfloat16)


def halves_and_squares(samples):
    wide = samples.astype(jnp.float32)
    return (wide * -2.0).astype(jnp.bfloat16), jnp.sum(wide * wide, axis=1, keepdims=True)


def column_of(row):
    return jnp.concatenate(
        [
            jnp.broadcast_to(row[:, at : at + LANES], (LANES, LANES)).T
            for at in range(0, row.shape[1], LANES)
        ],
        axis=0,
    )


def terms_body(side_ref, other_ref, pool_ref, square_ref, placed_ref, *refs):
    terms_ref, other_terms_ref, kernel_ref = refs
    samples = jnp.concatenate([side_ref[...], other_ref[...]], axis=0)
    samples, own_square = halves_and_squares(samples)
    own_square = turned(own_square)
    for at, size in spans(placed_ref.shape[1], 4 * LANES):
        cross = contract_last(pool_rows(pool_ref, at, size), samples)
        pool_square = column_of(square_ref[:, at : at + size])[:, :1]
        kernel_ref[at : at + size, :] = kernel_of(pool_square + own_square + cross)
    terms = jnp.dot(placed_ref[...], kernel_ref[...], preferred_element_type=jnp.float32)
    rows = side_ref.shape[0]
    terms_ref[...] = terms[:, :rows]
    other_terms_ref[...] = terms[:, rows:]


def pool_terms(side, other, pool, square, placed):
    outs, rows = placed.shape[0], side.shape[0]
    return call(
        terms_body,
        [(array, WHOLE) for array in (side, other, pool, square, placed)],
        [((outs, rows), jnp.float32, WHOLE)] * 2,
        [pltpu.VMEM((placed.shape[1], 2 * rows), jnp.bfloat16)],
    )


def pick_span(index_ref, pool_ref, rows_ref, square_ref, first, at, size):
    whole = pool_ref.shape[0] // LANES * LANES
    wanted = column_of(index_ref[:, first + at : first + at + size])
    lane = lax.broadcasted_iota(jnp.int32, (size, LANES), 1)
    chosen = jnp.concatenate(
        [
            jnp.where(wanted == lane + part, 1.0, 0.0).astype(jnp.bfloat16)
            for part in range(0, whole, LANES)
        ],
        axis=1,
    )
    rows = jnp.dot(chosen, pool_ref[:whole, :], preferred_element_type=jnp.float32)
    for row in range(whole, pool_ref.shape[0]):
        rows = rows + jnp.where(
            wanted[:, :1] == row, pool_ref[row : row + 1, :].astype(jnp.float32), 0.0
        )
    rows_ref[at : at + size, :] = rows.astype(jnp.bfloat16)
    square_ref[:, at : at + size] = turned(jnp.sum(rows * rows, axis=1, keepdims=True))


def pick_body(first, index_ref, pool_ref, rows_ref, square_ref):
    for at, size in spans(rows_ref.shape[0], 8 * LANES):
        pick_span(index_ref, pool_ref, rows_ref, square_ref, first, at, size)


def pick_rows(index, pool, first, count):
    return call(
        functools.partial(pick_body, first),
        [(index, WHOLE), (pool, WHOLE)],
        [((count, pool.shape[1]), jnp.bfloat16, WHOLE), ((1, count), jnp.float32, WHOLE)],
    )


def pick_own_body(first, index_ref, pool_ref, side_ref, other_ref, *refs):
    *before, rows_ref, square_ref, kernel_ref = refs
    samples = jnp.concatenate([side_ref[...], other_ref[...]], axis=0)
    samples, own_square = halves_and_squares(samples)
    start = 0
    for early_ref, early_square_ref in zip(before[::2], before[1::2]):
        span = early_ref.shape[0]
        kernel_ref[:, start : start + span] = kernel_of(
            own_square + early_square_ref[...] + contract_last(samples, early_ref[...])
        )
        start += span
    for at, size in spans(rows_ref.shape[0], 8 * LANES):
        pick_span(index_ref, pool_ref, rows_ref, square_ref, first, at, size)
        kernel_ref[:, start + at : start + at + size] = kernel_of(
            own_square
            + square_ref[:, at : at + size]
            + contract_last(samples, rows_ref[at : at + size, :])
        )


def pick_rows_and_own(index, pool, side, other, before, first, count):
    rows = side.shape[0] + other.shape[0]
    early = sum(square.shape[1] for _, square in before)
    return call(
        functools.partial(pick_own_body, first),
        [(array, WHOLE) for array in (index, pool, side, other)]
        + [(array, WHOLE) for pair in before for array in pair],
        [
            ((count, pool.shape[1]), jnp.bfloat16, WHOLE),
            ((1, count), jnp.float32, WHOLE),
            ((rows, early + count), jnp.bfloat16, WHOLE),
        ],
    )


def block_body(parts, *refs):
    samples = jnp.concatenate([ref[...] for ref in refs[:parts]], axis=0)
    kernel_ref = refs[-1]
    samples, own_square = halves_and_squares(samples)
    start = 0
    for rows_ref, square_ref in zip(refs[parts:-1:2], refs[parts + 1 : -1 : 2]):
        for at, size in spans(rows_ref.shape[0], 2 * LANES):
            cross = contract_last(samples, rows_ref[at : at + size, :])
            kernel = kernel_of(own_square + square_ref[:, at : at + size] + cross)
            kernel_ref[:, start + at : start + at + size] = kernel
        start += rows_ref.shape[0]


def kernel_block(samples, picked):
    rows = sum(part.shape[0] for part in samples)
    count = sum(square.shape[1] for _, square in picked)
    return call(
        functools.partial(block_body, len(samples)),
        [(part, WHOLE) for part in samples]
        + [(array, WHOLE) for pair in picked for array in pair],
        [((rows, count), jnp.bfloat16, WHOLE)],
    )[0]


def gradient_span(residual_ref, kernel_refs, owns, first, at, size):
    own_refs, rest_refs = kernel_refs[:owns], kernel_refs[owns:]
    span = own_refs[0].shape[1]
    own_ref, own_at = own_refs[at // span], at % span
    rows = residual_ref.shape[1] - sum(rest_ref.shape[0] for rest_ref in rest_refs)
    gradient = jnp.dot(
        residual_ref[:, :rows],
        own_ref[first : first + rows, own_at : own_at + size],
        preferred_element_type=jnp.float32,
    )
    for rest_ref in rest_refs:
        gradient = gradient + jnp.dot(
            residual_ref[:, rows:], rest_ref[:, at : at + size], preferred_element_type=jnp.float32
        )
    return gradient


def descend_body(step, owns, kernels, place_ref, total_ref, residual_ref, base_ref, *refs):
    kernel_refs, refs = refs[:kernels], refs[kernels:]
    out_ref, own_far, tall_ref, wide_ref, own_ref, done_ref = refs
    outs, rows = total_ref.shape
    count = own_ref.shape[0]
    tall_ref[...] = jnp.zeros_like(tall_ref)
    tall_ref[:outs, :rows] = total_ref[...]
    turn_over(tall_ref, wide_ref)
    at = pl.multiple_of(place_ref[0] * count, count)
    own_ref[...] = wide_ref[pl.ds(at, count), :outs]
    store = pltpu.make_async_copy(own_ref, own_far, done_ref)
    store.start()
    for at, size in spans(base_ref.shape[1], 4 * LANES):
        gradient = gradient_span(residual_ref, kernel_refs, owns, 0, at, size)
        out_ref[:, at : at + size] = base_ref[:, at : at + size] - step * gradient
    store.wait()


def descend(place, total, count, residual, base, owns, rests, step):
    outs, rows = total.shape
    high, wide = tiles(rows), tiles(outs)
    kernels = [*owns, *rests]
    return call(
        functools.partial(descend_body, step, len(owns), len(kernels)),
        [(place, SCALARS)] + [(array, WHOLE) for array in (total, residual, base, *kernels)],
        [(base.shape, jnp.float32, WHOLE), ((count, outs), jnp.float32, FAR)],
        [
            pltpu.VMEM((wide, high), jnp.float32),
            pltpu.VMEM((high, wide), jnp.float32),
            pltpu.VMEM((count, outs), jnp.float32),
            pltpu.SemaphoreType.DMA(()),
        ],
    )


def finish_body(step, owns, kernels, first, residual_ref, base_ref, *refs):
    kernel_refs, (out_far, held_ref, done_ref) = refs[:kernels], refs[kernels:]
    stores = []
    for turn, (at, size) in enumerate(spans(base_ref.shape[1], 4 * LANES)):
        gradient = gradient_span(residual_ref, kernel_refs, owns, first, at, size)
        held_ref[:, at : at + size] = base_ref[:, at : at + size] - step * gradient
        span = pl.ds(at, size)
        stores.append(
            pltpu.make_async_copy(held_ref.at[:, span], out_far.at[:, span], done_ref.at[turn])
        )
        stores[-1].start()
    for store in stores:
        store.wait()


def finish(residual, base, owns, rests, first, step):
    turns = len(spans(base.shape[1], 4 * LANES))
    kernels = [*owns, *rests]
    return call(
        functools.partial(finish_body, step, len(owns), len(kernels), first),
        [(array, WHOLE) for array in (residual, base, *kernels)],
        [(base.shape, jnp.float32, FAR)],
        [pltpu.VMEM(base.shape, jnp.float32), pltpu.SemaphoreType.DMA((turns,))],
    )[0]


def on_device(batch_pool, batch_index, centre_pool, centre_index, targets, coefficients):
    own_count = batch_index.shape[0]
    batch_size, centre_size = lax.axis_size("batch"), lax.axis_size("centre")
    batch_place, centre_place = lax.axis_index("batch"), lax.axis_index("centre")
    device_place = batch_place * centre_size + centre_place
    batch_total = own_count * batch_size * centre_size
    far_size, far_place = centre_size // 2, lax.shift_right_logical(centre_place, 1)
    rows = far_size * own_count
    hold_all = batch_total * (centre_index.shape[0] + batch_pool.shape[1]) * 2 <= 1 << 24

    count = centre_index.shape[0]
    indices = lax.optimization_barrier(
        jnp.concatenate(
            [
                centre_index - centre_place * centre_pool.shape[0],
                batch_index - device_place * batch_pool.shape[0],
            ]
        )
    )
    chosen = indices[count:, None] == jnp.arange(batch_pool.shape[0])
    local_rows = jnp.dot(
        chosen.astype(jnp.bfloat16), batch_pool, preferred_element_type=jnp.float32
    ).astype(jnp.bfloat16)
    pieces = [local_rows] + [flip(local_rows, "centre", 2 * k) for k in range(1, far_size)]

    place = jnp.reshape(far_place, (1,)).astype(jnp.int32)
    index, place = lax.optimization_barrier((indices[:count].reshape(1, -1), place))
    placed, pool_square, base, pool = place_coefficients(index, coefficients.T, centre_pool)
    placed, *pieces = lax.optimization_barrier((placed, *pieces))
    side, placed_targets = arrange(place, targets, pieces)
    other = flip(side, "centre", 1)
    steps = far_size.bit_length() - 1
    span = count // (2 * steps) if steps and count % (2 * steps * LANES) == 0 else count
    early = span // 2 if span < count and span % (2 * LANES) == 0 else 0
    picked = []
    if early:
        picked.append(pick_rows(after(index, side), pool, 0, early))
        other = after(other, *picked[-1])
    terms, other_terms = pool_terms(side, other, pool, pool_square, placed)
    foreign = [flip(side, "batch", k) for k in range(1, batch_size)] if hold_all else []

    flipped = flip(other_terms, "centre", 1)
    if early:
        picked.append(pick_rows(after(index, other_terms), pool, early, early))
        flipped = after(flipped, *picked[-1])
    total = terms - placed_targets + flipped
    kernels, at = [], 2 * early
    distance = 2
    while distance < centre_size:
        if at < count:
            size = span if not kernels else 2 * span
            size = min(size, count - at)
            before = [] if kernels else picked
            *pair, kernel = pick_rows_and_own(
                after(index, total), pool, side, other, before, at, size
            )
            picked, kernels, at = [*picked, pair], [*kernels, kernel], at + size
        total = after(total + flip(total, "centre", distance), *picked[-1])
        distance *= 2
    if hold_all:
        foreign = lax.optimization_barrier((total, *foreign))[1:]
        side_rows = jnp.concatenate(foreign, axis=0)
        other_rows = flip(side_rows, "centre", 1)
    residual_side = total.astype(jnp.bfloat16)
    rests, other_rests = [], []
    if hold_all:
        rests, other_rests = [kernel_block([side_rows], picked)], [kernel_block([other_rows], picked)]
        parts = [residual_side] + [flip(residual_side, "batch", k) for k in range(1, batch_size)]
        rests, other_rests, parts = lax.optimization_barrier((rests, other_rests, parts))
        residual_side = jnp.concatenate(parts, axis=1)
    residual_other = flip(residual_side, "centre", 1)

    step = 8.0 / math.sqrt(batch_total)
    start = base if hold_all else jnp.zeros_like(base)
    updated, residual = descend(
        place, total, own_count, residual_side, start, kernels, rests, step
    )
    updated = finish(residual_other, updated, kernels, other_rests, rows, step)
    if not hold_all:
        updated = base + lax.psum(updated, "batch")
    return (updated.T, residual)


def solution(mesh):
    return jax.shard_map(
        on_device,
        mesh=mesh,
        in_specs=(
            P(("batch", "centre"), None),
            P(("batch", "centre")),
            P("centre", None),
            P("centre"),
            P(("batch", "centre"), None),
            P("centre", None),
        ),
        out_specs=(P("centre", None), P(("batch", "centre"), None)),
        check_vma=False,
    )
```

```python
import functools
import math

import jax
import jax.numpy as jnp
from jax import lax
from jax.experimental import pallas as pl
from jax.experimental.pallas import tpu as pltpu
from jax.sharding import PartitionSpec as P

LANES = 128


def flip(value, axis, distance):
    count = lax.axis_size(axis)
    return lax.ppermute(value, axis, [(i, i ^ distance) for i in range(count)])


def after(value, *others):
    return lax.optimization_barrier((value,) + others)[0]


def contract_last(left, right):
    return lax.dot_general(
        left, right, (((1,), (1,)), ((), ())), preferred_element_type=jnp.float32
    )


def spans(total, most):
    return [(at, min(most, total - at)) for at in range(0, total, most)]


def tiles(count):
    return -(-count // LANES) * LANES


WHOLE = pl.BlockSpec(memory_space=pltpu.VMEM)
SCALARS = pl.BlockSpec(memory_space=pltpu.SMEM)
FAR = pl.BlockSpec(memory_space=pltpu.HBM)


def call(body, operands, outputs, scratch=(), limit=28):
    arrays = [array for array, _ in operands]
    shapes = [jax.ShapeDtypeStruct(shape, dtype) for shape, dtype, _ in outputs]
    return pl.pallas_call(
        body,
        in_specs=[place for _, place in operands],
        out_specs=[place for _, _, place in outputs],
        out_shape=shapes,
        scratch_shapes=list(scratch),
        cost_estimate=pl.CostEstimate(flops=1024, bytes_accessed=1024, transcendentals=0),
        compiler_params=pltpu.CompilerParams(vmem_limit_bytes=limit << 20),
    )(*arrays)


def narrow(index, pool_ref):
    return index.astype(jnp.int16 if pool_ref.shape[0] < 1 << 15 else jnp.int32)


def one_hot(hit):
    return jnp.where(hit, jnp.bfloat16(1.0), jnp.bfloat16(0.0))


def turned(column):
    return jnp.concatenate(
        [
            jnp.broadcast_to(column[at : at + LANES], (LANES, 8)).T[:1]
            for at in range(0, column.shape[0], LANES)
        ],
        axis=1,
    )


def pool_rows(pool_ref, at, size):
    if at + size <= pool_ref.shape[0]:
        return pool_ref[at : at + size, :]
    place = lax.broadcasted_iota(jnp.int32, (size, pool_ref.shape[1]), 0)
    rows = jnp.zeros(place.shape, jnp.float32)
    for row in range(at, pool_ref.shape[0]):
        rows = jnp.where(place == row - at, pool_ref[row : row + 1, :].astype(jnp.float32), rows)
    return rows.astype(jnp.bfloat16)


def place_body(index_ref, base_ref, pool_far, placed_ref, square_ref, kept_ref, pool_ref, done_ref):
    fetch = pltpu.make_async_copy(pool_far, pool_ref, done_ref)
    fetch.start()
    index = narrow(index_ref[...], pool_ref)
    base = base_ref[...]
    kept_ref[...] = base
    half = base.astype(jnp.bfloat16)
    cuts = spans(placed_ref.shape[1], 2 * LANES)
    left, arrival = list(cuts), min(3, len(cuts) - 1)
    for turn, (at, size) in enumerate(cuts):
        place = lax.broadcasted_iota(index.dtype, (size, index.shape[1]), 0)
        chosen = one_hot(index - jnp.asarray(at, index.dtype) == place)
        placed_ref[:, at : at + size] = contract_last(half, chosen).astype(jnp.bfloat16)
        if turn == arrival:
            fetch.wait()
        share = -(-len(left) // (len(cuts) - turn)) if turn >= arrival else 0
        for from_row, count in left[:share]:
            rows = pool_rows(pool_ref, from_row, count).astype(jnp.float32)
            square_ref[from_row : from_row + count, :] = jnp.broadcast_to(
                jnp.sum(rows * rows, axis=1, keepdims=True), (count, LANES)
            )
        left = left[share:]


def place_coefficients(index, base, pool):
    width = tiles(pool.shape[0])
    return call(
        place_body,
        [(index, WHOLE), (base, WHOLE), (pool, FAR)],
        [
            ((base.shape[0], width), jnp.bfloat16, WHOLE),
            ((width, LANES), jnp.float32, WHOLE),
            (base.shape, jnp.float32, WHOLE),
            (pool.shape, jnp.bfloat16, WHOLE),
        ],
        [pltpu.SemaphoreType.DMA(())],
        limit=40,
    )


def turn_over(source_ref, target_ref):
    for row in range(0, source_ref.shape[0], LANES):
        for column in range(0, source_ref.shape[1], LANES):
            target_ref[column : column + LANES, row : row + LANES] = source_ref[
                row : row + LANES, column : column + LANES
            ].T


def arrange_body(place_ref, targets_ref, *refs):
    pieces, (side_ref, placed_ref, wide_ref, tall_ref) = refs[:-4], refs[-4:]
    count = targets_ref.shape[0]
    for k, piece_ref in enumerate(pieces):
        at = pl.multiple_of((place_ref[0] ^ k) * count, count)
        side_ref[pl.ds(at, count), :] = piece_ref[...]
    wide_ref[...] = jnp.zeros_like(wide_ref)
    at = pl.multiple_of(place_ref[0] * count, count)
    wide_ref[pl.ds(at, count), : targets_ref.shape[1]] = targets_ref[...]
    turn_over(wide_ref, tall_ref)
    placed_ref[...] = tall_ref[: placed_ref.shape[0], : placed_ref.shape[1]]


def arrange(place, targets, pieces):
    count, outs = targets.shape
    rows = count * len(pieces)
    high, wide = tiles(rows), tiles(outs)
    return call(
        arrange_body,
        [(place, SCALARS), (targets, WHOLE)] + [(piece, WHOLE) for piece in pieces],
        [
            ((rows, pieces[0].shape[1]), jnp.bfloat16, WHOLE),
            ((outs, rows), jnp.float32, WHOLE),
        ],
        [pltpu.VMEM((high, wide), jnp.float32), pltpu.VMEM((wide, high), jnp.float32)],
    )


def kernel_of(squared):
    least = jnp.maximum(squared, 1e-30)
    return jnp.exp2(least * -math.log2(math.e) * lax.rsqrt(least)).astype(jnp.bfloat16)


def halves_and_squares(samples):
    wide = samples.astype(jnp.float32)
    return (wide * -2.0).astype(jnp.bfloat16), jnp.sum(wide * wide, axis=1, keepdims=True)


def column_of(row):
    return jnp.concatenate(
        [
            jnp.broadcast_to(row[:, at : at + LANES], (LANES, LANES)).T
            for at in range(0, row.shape[1], LANES)
        ],
        axis=0,
    )


def terms_body(side_ref, other_ref, pool_ref, square_ref, placed_ref, *refs):
    terms_ref, other_terms_ref, kernel_ref = refs
    samples = jnp.concatenate([side_ref[...], other_ref[...]], axis=0)
    samples, own_square = halves_and_squares(samples)
    own_square = turned(own_square)
    for at, size in spans(placed_ref.shape[1], 4 * LANES):
        cross = contract_last(pool_rows(pool_ref, at, size), samples)
        for lane in range(0, samples.shape[0], LANES):
            lanes = slice(lane, lane + LANES)
            squared = square_ref[at : at + size, :] + own_square[:, lanes] + cross[:, lanes]
            kernel_ref[at : at + size, lanes] = kernel_of(squared)
    terms = jnp.dot(placed_ref[...], kernel_ref[...], preferred_element_type=jnp.float32)
    rows = side_ref.shape[0]
    terms_ref[...] = terms[:, :rows]
    other_terms_ref[...] = terms[:, rows:]


def pool_terms(side, other, pool, square, placed):
    outs, rows = placed.shape[0], side.shape[0]
    return call(
        terms_body,
        [(array, WHOLE) for array in (side, other, pool, square, placed)],
        [((outs, rows), jnp.float32, WHOLE)] * 2,
        [pltpu.VMEM((placed.shape[1], 2 * rows), jnp.bfloat16)],
    )


def pick_span(index_ref, pool_ref, rows_ref, square_ref, first, at, size):
    whole = pool_ref.shape[0] // LANES * LANES
    wanted = column_of(index_ref[:, first + at : first + at + size])
    place = narrow(wanted, pool_ref)
    lane = lax.broadcasted_iota(place.dtype, (size, LANES), 1)
    chosen = jnp.concatenate(
        [
            one_hot(place - jnp.asarray(part, place.dtype) == lane)
            for part in range(0, whole, LANES)
        ],
        axis=1,
    )
    rows = jnp.dot(chosen, pool_ref[:whole, :], preferred_element_type=jnp.float32)
    for row in range(whole, pool_ref.shape[0]):
        rows = rows + jnp.where(
            wanted[:, :1] == row, pool_ref[row : row + 1, :].astype(jnp.float32), 0.0
        )
    rows_ref[at : at + size, :] = rows.astype(jnp.bfloat16)
    square_ref[:, at : at + size] = turned(jnp.sum(rows * rows, axis=1, keepdims=True))


def pick_body(first, index_ref, pool_ref, rows_ref, square_ref):
    for at, size in spans(rows_ref.shape[0], 8 * LANES):
        pick_span(index_ref, pool_ref, rows_ref, square_ref, first, at, size)


def pick_rows(index, pool, first, count):
    return call(
        functools.partial(pick_body, first),
        [(index, WHOLE), (pool, WHOLE)],
        [((count, pool.shape[1]), jnp.bfloat16, WHOLE), ((1, count), jnp.float32, WHOLE)],
    )


def pick_own_body(first, index_ref, pool_ref, side_ref, other_ref, *refs):
    *before, rows_ref, square_ref, kernel_ref = refs
    samples = jnp.concatenate([side_ref[...], other_ref[...]], axis=0)
    samples, own_square = halves_and_squares(samples)
    start = 0
    for early_ref, early_square_ref in zip(before[::2], before[1::2]):
        span = early_ref.shape[0]
        kernel_ref[:, start : start + span] = kernel_of(
            own_square + early_square_ref[...] + contract_last(samples, early_ref[...])
        )
        start += span
    for at, size in spans(rows_ref.shape[0], 8 * LANES):
        pick_span(index_ref, pool_ref, rows_ref, square_ref, first, at, size)
        kernel_ref[:, start + at : start + at + size] = kernel_of(
            own_square
            + square_ref[:, at : at + size]
            + contract_last(samples, rows_ref[at : at + size, :])
        )


def pick_rows_and_own(index, pool, side, other, before, first, count):
    rows = side.shape[0] + other.shape[0]
    early = sum(square.shape[1] for _, square in before)
    return call(
        functools.partial(pick_own_body, first),
        [(array, WHOLE) for array in (index, pool, side, other)]
        + [(array, WHOLE) for pair in before for array in pair],
        [
            ((count, pool.shape[1]), jnp.bfloat16, WHOLE),
            ((1, count), jnp.float32, WHOLE),
            ((rows, early + count), jnp.bfloat16, WHOLE),
        ],
    )


def block_body(parts, *refs):
    samples = jnp.concatenate([ref[...] for ref in refs[:parts]], axis=0)
    kernel_ref = refs[-1]
    samples, own_square = halves_and_squares(samples)
    start = 0
    for rows_ref, square_ref in zip(refs[parts:-1:2], refs[parts + 1 : -1 : 2]):
        for at, size in spans(rows_ref.shape[0], 2 * LANES):
            cross = contract_last(samples, rows_ref[at : at + size, :])
            kernel = kernel_of(own_square + square_ref[:, at : at + size] + cross)
            kernel_ref[:, start + at : start + at + size] = kernel
        start += rows_ref.shape[0]


def kernel_block(samples, picked):
    rows = sum(part.shape[0] for part in samples)
    count = sum(square.shape[1] for _, square in picked)
    return call(
        functools.partial(block_body, len(samples)),
        [(part, WHOLE) for part in samples]
        + [(array, WHOLE) for pair in picked for array in pair],
        [((rows, count), jnp.bfloat16, WHOLE)],
    )[0]


def gradient_span(residual_ref, kernel_refs, owns, first, at, size):
    own_refs, rest_refs = kernel_refs[:owns], kernel_refs[owns:]
    span = own_refs[0].shape[1]
    own_ref, own_at = own_refs[at // span], at % span
    rows = residual_ref.shape[1] - sum(rest_ref.shape[0] for rest_ref in rest_refs)
    gradient = jnp.dot(
        residual_ref[:, :rows],
        own_ref[first : first + rows, own_at : own_at + size],
        preferred_element_type=jnp.float32,
    )
    for rest_ref in rest_refs:
        gradient = gradient + jnp.dot(
            residual_ref[:, rows:], rest_ref[:, at : at + size], preferred_element_type=jnp.float32
        )
    return gradient


def descend_body(step, owns, kernels, place_ref, total_ref, residual_ref, base_ref, *refs):
    kernel_refs, refs = refs[:kernels], refs[kernels:]
    out_ref, own_far, tall_ref, wide_ref, own_ref, done_ref = refs
    outs, rows = total_ref.shape
    count = own_ref.shape[0]
    tall_ref[...] = jnp.zeros_like(tall_ref)
    tall_ref[:outs, :rows] = total_ref[...]
    turn_over(tall_ref, wide_ref)
    at = pl.multiple_of(place_ref[0] * count, count)
    own_ref[...] = wide_ref[pl.ds(at, count), :outs]
    store = pltpu.make_async_copy(own_ref, own_far, done_ref)
    store.start()
    for at, size in spans(base_ref.shape[1], 4 * LANES):
        gradient = gradient_span(residual_ref, kernel_refs, owns, 0, at, size)
        out_ref[:, at : at + size] = base_ref[:, at : at + size] - step * gradient
    store.wait()


def descend(place, total, count, residual, base, owns, rests, step):
    outs, rows = total.shape
    high, wide = tiles(rows), tiles(outs)
    kernels = [*owns, *rests]
    return call(
        functools.partial(descend_body, step, len(owns), len(kernels)),
        [(place, SCALARS)] + [(array, WHOLE) for array in (total, residual, base, *kernels)],
        [(base.shape, jnp.float32, WHOLE), ((count, outs), jnp.float32, FAR)],
        [
            pltpu.VMEM((wide, high), jnp.float32),
            pltpu.VMEM((high, wide), jnp.float32),
            pltpu.VMEM((count, outs), jnp.float32),
            pltpu.SemaphoreType.DMA(()),
        ],
    )


def finish_body(step, owns, kernels, first, residual_ref, base_ref, *refs):
    kernel_refs, (out_far, held_ref, done_ref) = refs[:kernels], refs[kernels:]
    stores = []
    for turn, (at, size) in enumerate(spans(base_ref.shape[1], 4 * LANES)):
        gradient = gradient_span(residual_ref, kernel_refs, owns, first, at, size)
        held_ref[:, at : at + size] = base_ref[:, at : at + size] - step * gradient
        span = pl.ds(at, size)
        stores.append(
            pltpu.make_async_copy(held_ref.at[:, span], out_far.at[:, span], done_ref.at[turn])
        )
        stores[-1].start()
    for store in stores:
        store.wait()


def finish(residual, base, owns, rests, first, step):
    turns = len(spans(base.shape[1], 4 * LANES))
    kernels = [*owns, *rests]
    return call(
        functools.partial(finish_body, step, len(owns), len(kernels), first),
        [(array, WHOLE) for array in (residual, base, *kernels)],
        [(base.shape, jnp.float32, FAR)],
        [pltpu.VMEM(base.shape, jnp.float32), pltpu.SemaphoreType.DMA((turns,))],
    )[0]


def on_device(batch_pool, batch_index, centre_pool, centre_index, targets, coefficients):
    own_count = batch_index.shape[0]
    batch_size, centre_size = lax.axis_size("batch"), lax.axis_size("centre")
    batch_place, centre_place = lax.axis_index("batch"), lax.axis_index("centre")
    device_place = batch_place * centre_size + centre_place
    batch_total = own_count * batch_size * centre_size
    far_size, far_place = centre_size // 2, lax.shift_right_logical(centre_place, 1)
    rows = far_size * own_count
    hold_all = batch_total * (centre_index.shape[0] + batch_pool.shape[1]) * 2 <= 1 << 24

    count = centre_index.shape[0]
    indices = lax.optimization_barrier(
        jnp.concatenate(
            [
                centre_index - centre_place * centre_pool.shape[0],
                batch_index - device_place * batch_pool.shape[0],
            ]
        )
    )
    chosen = indices[count:, None] == jnp.arange(batch_pool.shape[0])
    local_rows = jnp.dot(
        chosen.astype(jnp.bfloat16), batch_pool, preferred_element_type=jnp.float32
    ).astype(jnp.bfloat16)
    pieces = [local_rows] + [flip(local_rows, "centre", 2 * k) for k in range(1, far_size)]

    place = jnp.reshape(far_place, (1,)).astype(jnp.int32)
    index, place = lax.optimization_barrier((indices[:count].reshape(1, -1), place))
    placed, pool_square, base, pool = place_coefficients(index, coefficients.T, centre_pool)
    placed, *pieces = lax.optimization_barrier((placed, *pieces))
    side, placed_targets = arrange(place, targets, pieces)
    other = flip(side, "centre", 1)
    steps = far_size.bit_length() - 1
    span = count // (2 * steps) if steps and count % (2 * steps * LANES) == 0 else count
    early = span // 2 if span < count and span % (2 * LANES) == 0 else 0
    picked = []
    if early:
        picked.append(pick_rows(after(index, side), pool, 0, early))
        other = after(other, *picked[-1])
    terms, other_terms = pool_terms(side, other, pool, pool_square, placed)
    foreign = [flip(side, "batch", k) for k in range(1, batch_size)] if hold_all else []

    flipped = flip(other_terms, "centre", 1)
    if early:
        picked.append(pick_rows(after(index, other_terms), pool, early, early))
        flipped = after(flipped, *picked[-1])
    total = terms - placed_targets + flipped
    kernels, at = [], 2 * early
    distance = 2
    while distance < centre_size:
        if at < count:
            size = span if not kernels else 2 * span
            size = min(size, count - at)
            before = [] if kernels else picked
            *pair, kernel = pick_rows_and_own(
                after(index, total), pool, side, other, before, at, size
            )
            picked, kernels, at = [*picked, pair], [*kernels, kernel], at + size
        total = after(total + flip(total, "centre", distance), *picked[-1])
        distance *= 2
    if hold_all:
        foreign = lax.optimization_barrier((total, *foreign))[1:]
        side_rows = jnp.concatenate(foreign, axis=0)
        other_rows = flip(side_rows, "centre", 1)
    residual_side = total.astype(jnp.bfloat16)
    rests, other_rests = [], []
    if hold_all:
        rests, other_rests = [kernel_block([side_rows], picked)], [kernel_block([other_rows], picked)]
        parts = [residual_side] + [flip(residual_side, "batch", k) for k in range(1, batch_size)]
        rests, other_rests, parts = lax.optimization_barrier((rests, other_rests, parts))
        residual_side = jnp.concatenate(parts, axis=1)
    residual_other = flip(residual_side, "centre", 1)

    step = 8.0 / math.sqrt(batch_total)
    start = base if hold_all else jnp.zeros_like(base)
    updated, residual = descend(
        place, total, own_count, residual_side, start, kernels, rests, step
    )
    updated = finish(residual_other, updated, kernels, other_rests, rows, step)
    if not hold_all:
        updated = base + lax.psum(updated, "batch")
    return (updated.T, residual)


def solution(mesh):
    return jax.shard_map(
        on_device,
        mesh=mesh,
        in_specs=(
            P(("batch", "centre"), None),
            P(("batch", "centre")),
            P("centre", None),
            P("centre"),
            P(("batch", "centre"), None),
            P("centre", None),
        ),
        out_specs=(P("centre", None), P(("batch", "centre"), None)),
        check_vma=False,
    )
```

```python
import functools
import math

import jax
import jax.numpy as jnp
from jax import lax
from jax.experimental import pallas as pl
from jax.experimental.pallas import tpu as pltpu
from jax.sharding import PartitionSpec as P

LANES = 128


def flip(value, axis, distance):
    count = lax.axis_size(axis)
    return lax.ppermute(value, axis, [(i, i ^ distance) for i in range(count)])


def after(value, *others):
    return lax.optimization_barrier((value,) + others)[0]


def contract_last(left, right):
    return lax.dot_general(
        left, right, (((1,), (1,)), ((), ())), preferred_element_type=jnp.float32
    )


def spans(total, most):
    return [(at, min(most, total - at)) for at in range(0, total, most)]


def tiles(count):
    return -(-count // LANES) * LANES


WHOLE = pl.BlockSpec(memory_space=pltpu.VMEM)
SCALARS = pl.BlockSpec(memory_space=pltpu.SMEM)
FAR = pl.BlockSpec(memory_space=pltpu.HBM)


def call(body, operands, outputs, scratch=(), limit=28):
    arrays = [array for array, _ in operands]
    shapes = [jax.ShapeDtypeStruct(shape, dtype) for shape, dtype, _ in outputs]
    return pl.pallas_call(
        body,
        in_specs=[place for _, place in operands],
        out_specs=[place for _, _, place in outputs],
        out_shape=shapes,
        scratch_shapes=list(scratch),
        cost_estimate=pl.CostEstimate(flops=1024, bytes_accessed=1024, transcendentals=0),
        compiler_params=pltpu.CompilerParams(vmem_limit_bytes=limit << 20),
    )(*arrays)


def narrow(index, pool_ref):
    return index.astype(jnp.int16 if pool_ref.shape[0] < 1 << 15 else jnp.int32)


def one_hot(hit):
    return jnp.where(hit, jnp.bfloat16(1.0), jnp.bfloat16(0.0))


def turned(column):
    return jnp.concatenate(
        [
            jnp.broadcast_to(column[at : at + LANES], (LANES, 8)).T[:1]
            for at in range(0, column.shape[0], LANES)
        ],
        axis=1,
    )


def pool_rows(pool_ref, at, size):
    if at + size <= pool_ref.shape[0]:
        return pool_ref[at : at + size, :]
    whole = (pool_ref.shape[0] - at) // LANES * LANES
    place = lax.broadcasted_iota(jnp.int32, (size - whole, pool_ref.shape[1]), 0)
    rows = jnp.zeros(place.shape, jnp.float32)
    for row in range(at + whole, pool_ref.shape[0]):
        wide = pool_ref[row : row + 1, :].astype(jnp.float32)
        rows = jnp.where(place == row - at - whole, wide, rows)
    rows = rows.astype(jnp.bfloat16)
    if whole == 0:
        return rows
    return jnp.concatenate([pool_ref[at : at + whole, :], rows], axis=0)


def place_body(index_ref, base_ref, pool_far, placed_ref, square_ref, kept_ref, pool_ref, done_ref):
    fetch = pltpu.make_async_copy(pool_far, pool_ref, done_ref)
    fetch.start()
    index = narrow(index_ref[...], pool_ref)
    base = base_ref[...]
    kept_ref[...] = base
    half = base.astype(jnp.bfloat16)
    cuts = spans(placed_ref.shape[1], 2 * LANES)
    left, arrival = list(cuts), min(3, len(cuts) - 1)
    for turn, (at, size) in enumerate(cuts):
        place = lax.broadcasted_iota(index.dtype, (size, index.shape[1]), 0)
        chosen = one_hot(index - jnp.asarray(at, index.dtype) == place)
        placed_ref[:, at : at + size] = contract_last(half, chosen).astype(jnp.bfloat16)
        if turn == arrival:
            fetch.wait()
        share = -(-len(left) // (len(cuts) - turn)) if turn >= arrival else 0
        for from_row, count in left[:share]:
            rows = pool_rows(pool_ref, from_row, count).astype(jnp.float32)
            square_ref[from_row : from_row + count, :] = jnp.broadcast_to(
                jnp.sum(rows * rows, axis=1, keepdims=True), (count, LANES)
            )
        left = left[share:]


def place_coefficients(index, base, pool):
    width = tiles(pool.shape[0])
    return call(
        place_body,
        [(index, WHOLE), (base, WHOLE), (pool, FAR)],
        [
            ((base.shape[0], width), jnp.bfloat16, WHOLE),
            ((width, LANES), jnp.float32, WHOLE),
            (base.shape, jnp.float32, WHOLE),
            (pool.shape, jnp.bfloat16, WHOLE),
        ],
        [pltpu.SemaphoreType.DMA(())],
        limit=40,
    )


def turn_over(source_ref, target_ref):
    for row in range(0, source_ref.shape[0], LANES):
        for column in range(0, source_ref.shape[1], LANES):
            target_ref[column : column + LANES, row : row + LANES] = source_ref[
                row : row + LANES, column : column + LANES
            ].T


def arrange_body(place_ref, targets_ref, *refs):
    pieces, (side_ref, placed_ref, wide_ref, tall_ref) = refs[:-4], refs[-4:]
    count = targets_ref.shape[0]
    for k, piece_ref in enumerate(pieces):
        at = pl.multiple_of((place_ref[0] ^ k) * count, count)
        side_ref[pl.ds(at, count), :] = piece_ref[...]
    wide_ref[...] = jnp.zeros_like(wide_ref)
    at = pl.multiple_of(place_ref[0] * count, count)
    wide_ref[pl.ds(at, count), : targets_ref.shape[1]] = targets_ref[...]
    turn_over(wide_ref, tall_ref)
    placed_ref[...] = tall_ref[: placed_ref.shape[0], : placed_ref.shape[1]]


def arrange(place, targets, pieces):
    count, outs = targets.shape
    rows = count * len(pieces)
    high, wide = tiles(rows), tiles(outs)
    return call(
        arrange_body,
        [(place, SCALARS), (targets, WHOLE)] + [(piece, WHOLE) for piece in pieces],
        [
            ((rows, pieces[0].shape[1]), jnp.bfloat16, WHOLE),
            ((outs, rows), jnp.float32, WHOLE),
        ],
        [pltpu.VMEM((high, wide), jnp.float32), pltpu.VMEM((wide, high), jnp.float32)],
    )


def kernel_of(squared):
    least = jnp.maximum(squared, 1e-30)
    return jnp.exp2(least * -math.log2(math.e) * lax.rsqrt(least)).astype(jnp.bfloat16)


def halves_and_squares(samples):
    wide = samples.astype(jnp.float32)
    return (wide * -2.0).astype(jnp.bfloat16), jnp.sum(wide * wide, axis=1, keepdims=True)


def column_of(row):
    return jnp.concatenate(
        [
            jnp.broadcast_to(row[:, at : at + LANES], (LANES, LANES)).T
            for at in range(0, row.shape[1], LANES)
        ],
        axis=0,
    )


def terms_body(side_ref, other_ref, pool_ref, square_ref, placed_ref, *refs):
    terms_ref, other_terms_ref, kernel_ref = refs
    samples = jnp.concatenate([side_ref[...], other_ref[...]], axis=0)
    samples, own_square = halves_and_squares(samples)
    own_square = turned(own_square)
    for at, size in spans(placed_ref.shape[1], 8 * LANES):
        cross = contract_last(pool_rows(pool_ref, at, size), samples)
        for lane in range(0, samples.shape[0], LANES):
            lanes = slice(lane, lane + LANES)
            squared = square_ref[at : at + size, :] + own_square[:, lanes] + cross[:, lanes]
            kernel_ref[at : at + size, lanes] = kernel_of(squared)
    terms = jnp.dot(placed_ref[...], kernel_ref[...], preferred_element_type=jnp.float32)
    rows = side_ref.shape[0]
    terms_ref[...] = terms[:, :rows]
    other_terms_ref[...] = terms[:, rows:]


def pool_terms(side, other, pool, square, placed):
    outs, rows = placed.shape[0], side.shape[0]
    return call(
        terms_body,
        [(array, WHOLE) for array in (side, other, pool, square, placed)],
        [((outs, rows), jnp.float32, WHOLE)] * 2,
        [pltpu.VMEM((placed.shape[1], 2 * rows), jnp.bfloat16)],
    )


def pick_span(index_ref, pool_ref, rows_ref, square_ref, first, at, size):
    whole = pool_ref.shape[0] // LANES * LANES
    wanted = column_of(index_ref[:, first + at : first + at + size])
    place = narrow(wanted, pool_ref)
    lane = lax.broadcasted_iota(place.dtype, (size, LANES), 1)
    chosen = jnp.concatenate(
        [
            one_hot(place - jnp.asarray(part, place.dtype) == lane)
            for part in range(0, whole, LANES)
        ],
        axis=1,
    )
    rows = jnp.dot(chosen, pool_ref[:whole, :], preferred_element_type=jnp.float32)
    for row in range(whole, pool_ref.shape[0]):
        rows = rows + jnp.where(
            wanted[:, :1] == row, pool_ref[row : row + 1, :].astype(jnp.float32), 0.0
        )
    rows_ref[at : at + size, :] = rows.astype(jnp.bfloat16)
    square_ref[:, at : at + size] = turned(jnp.sum(rows * rows, axis=1, keepdims=True))


def pick_body(first, index_ref, pool_ref, rows_ref, square_ref):
    for at, size in spans(rows_ref.shape[0], 8 * LANES):
        pick_span(index_ref, pool_ref, rows_ref, square_ref, first, at, size)


def pick_rows(index, pool, first, count):
    return call(
        functools.partial(pick_body, first),
        [(index, WHOLE), (pool, WHOLE)],
        [((count, pool.shape[1]), jnp.bfloat16, WHOLE), ((1, count), jnp.float32, WHOLE)],
    )


def pick_own_body(first, index_ref, pool_ref, side_ref, other_ref, *refs):
    *before, rows_ref, square_ref, kernel_ref = refs
    samples = jnp.concatenate([side_ref[...], other_ref[...]], axis=0)
    samples, own_square = halves_and_squares(samples)
    start = 0
    for early_ref, early_square_ref in zip(before[::2], before[1::2]):
        span = early_ref.shape[0]
        kernel_ref[:, start : start + span] = kernel_of(
            own_square + early_square_ref[...] + contract_last(samples, early_ref[...])
        )
        start += span
    for at, size in spans(rows_ref.shape[0], 8 * LANES):
        pick_span(index_ref, pool_ref, rows_ref, square_ref, first, at, size)
        kernel_ref[:, start + at : start + at + size] = kernel_of(
            own_square
            + square_ref[:, at : at + size]
            + contract_last(samples, rows_ref[at : at + size, :])
        )


def pick_rows_and_own(index, pool, side, other, before, first, count):
    rows = side.shape[0] + other.shape[0]
    early = sum(square.shape[1] for _, square in before)
    return call(
        functools.partial(pick_own_body, first),
        [(array, WHOLE) for array in (index, pool, side, other)]
        + [(array, WHOLE) for pair in before for array in pair],
        [
            ((count, pool.shape[1]), jnp.bfloat16, WHOLE),
            ((1, count), jnp.float32, WHOLE),
            ((rows, early + count), jnp.bfloat16, WHOLE),
        ],
    )


def block_body(parts, *refs):
    samples = jnp.concatenate([ref[...] for ref in refs[:parts]], axis=0)
    kernel_ref = refs[-1]
    samples, own_square = halves_and_squares(samples)
    start = 0
    for rows_ref, square_ref in zip(refs[parts:-1:2], refs[parts + 1 : -1 : 2]):
        for at, size in spans(rows_ref.shape[0], 2 * LANES):
            cross = contract_last(samples, rows_ref[at : at + size, :])
            kernel = kernel_of(own_square + square_ref[:, at : at + size] + cross)
            kernel_ref[:, start + at : start + at + size] = kernel
        start += rows_ref.shape[0]


def kernel_block(samples, picked):
    rows = sum(part.shape[0] for part in samples)
    count = sum(square.shape[1] for _, square in picked)
    return call(
        functools.partial(block_body, len(samples)),
        [(part, WHOLE) for part in samples]
        + [(array, WHOLE) for pair in picked for array in pair],
        [((rows, count), jnp.bfloat16, WHOLE)],
    )[0]


def gradient_span(residual_ref, kernel_refs, owns, first, at, size):
    own_refs, rest_refs = kernel_refs[:owns], kernel_refs[owns:]
    span = own_refs[0].shape[1]
    own_ref, own_at = own_refs[at // span], at % span
    rows = residual_ref.shape[1] - sum(rest_ref.shape[0] for rest_ref in rest_refs)
    gradient = jnp.dot(
        residual_ref[:, :rows],
        own_ref[first : first + rows, own_at : own_at + size],
        preferred_element_type=jnp.float32,
    )
    for rest_ref in rest_refs:
        gradient = gradient + jnp.dot(
            residual_ref[:, rows:], rest_ref[:, at : at + size], preferred_element_type=jnp.float32
        )
    return gradient


def descend_body(step, owns, kernels, place_ref, total_ref, residual_ref, base_ref, *refs):
    kernel_refs, refs = refs[:kernels], refs[kernels:]
    out_ref, own_far, tall_ref, wide_ref, own_ref, done_ref = refs
    outs, rows = total_ref.shape
    count = own_ref.shape[0]
    tall_ref[...] = jnp.zeros_like(tall_ref)
    tall_ref[:outs, :rows] = total_ref[...]
    turn_over(tall_ref, wide_ref)
    at = pl.multiple_of(place_ref[0] * count, count)
    own_ref[...] = wide_ref[pl.ds(at, count), :outs]
    store = pltpu.make_async_copy(own_ref, own_far, done_ref)
    store.start()
    for at, size in spans(base_ref.shape[1], 4 * LANES):
        gradient = gradient_span(residual_ref, kernel_refs, owns, 0, at, size)
        out_ref[:, at : at + size] = base_ref[:, at : at + size] - step * gradient
    store.wait()


def descend(place, total, count, residual, base, owns, rests, step):
    outs, rows = total.shape
    high, wide = tiles(rows), tiles(outs)
    kernels = [*owns, *rests]
    return call(
        functools.partial(descend_body, step, len(owns), len(kernels)),
        [(place, SCALARS)] + [(array, WHOLE) for array in (total, residual, base, *kernels)],
        [(base.shape, jnp.float32, WHOLE), ((count, outs), jnp.float32, FAR)],
        [
            pltpu.VMEM((wide, high), jnp.float32),
            pltpu.VMEM((high, wide), jnp.float32),
            pltpu.VMEM((count, outs), jnp.float32),
            pltpu.SemaphoreType.DMA(()),
        ],
    )


def finish_body(step, owns, kernels, first, residual_ref, base_ref, *refs):
    kernel_refs, (out_far, held_ref, done_ref) = refs[:kernels], refs[kernels:]
    stores = []
    for turn, (at, size) in enumerate(spans(base_ref.shape[1], 4 * LANES)):
        gradient = gradient_span(residual_ref, kernel_refs, owns, first, at, size)
        held_ref[:, at : at + size] = base_ref[:, at : at + size] - step * gradient
        span = pl.ds(at, size)
        stores.append(
            pltpu.make_async_copy(held_ref.at[:, span], out_far.at[:, span], done_ref.at[turn])
        )
        stores[-1].start()
    for store in stores:
        store.wait()


def finish(residual, base, owns, rests, first, step):
    turns = len(spans(base.shape[1], 4 * LANES))
    kernels = [*owns, *rests]
    return call(
        functools.partial(finish_body, step, len(owns), len(kernels), first),
        [(array, WHOLE) for array in (residual, base, *kernels)],
        [(base.shape, jnp.float32, FAR)],
        [pltpu.VMEM(base.shape, jnp.float32), pltpu.SemaphoreType.DMA((turns,))],
    )[0]


def on_device(batch_pool, batch_index, centre_pool, centre_index, targets, coefficients):
    own_count = batch_index.shape[0]
    batch_size, centre_size = lax.axis_size("batch"), lax.axis_size("centre")
    batch_place, centre_place = lax.axis_index("batch"), lax.axis_index("centre")
    device_place = batch_place * centre_size + centre_place
    batch_total = own_count * batch_size * centre_size
    far_size, far_place = centre_size // 2, lax.shift_right_logical(centre_place, 1)
    rows = far_size * own_count
    hold_all = batch_total * (centre_index.shape[0] + batch_pool.shape[1]) * 2 <= 1 << 24

    count = centre_index.shape[0]
    indices = lax.optimization_barrier(
        jnp.concatenate(
            [
                centre_index - centre_place * centre_pool.shape[0],
                batch_index - device_place * batch_pool.shape[0],
            ]
        )
    )
    chosen = indices[count:, None] == jnp.arange(batch_pool.shape[0])
    local_rows = jnp.dot(
        chosen.astype(jnp.bfloat16), batch_pool, preferred_element_type=jnp.float32
    ).astype(jnp.bfloat16)
    pieces = [local_rows] + [flip(local_rows, "centre", 2 * k) for k in range(1, far_size)]

    place = jnp.reshape(far_place, (1,)).astype(jnp.int32)
    index, place = lax.optimization_barrier((indices[:count].reshape(1, -1), place))
    placed, pool_square, base, pool = place_coefficients(index, coefficients.T, centre_pool)
    placed, *pieces = lax.optimization_barrier((placed, *pieces))
    side, placed_targets = arrange(place, targets, pieces)
    other = flip(side, "centre", 1)
    steps = far_size.bit_length() - 1
    span = count // (2 * steps) if steps and count % (2 * steps * LANES) == 0 else count
    early = span // 2 if span < count and span % (2 * LANES) == 0 else 0
    picked = []
    if early:
        picked.append(pick_rows(after(index, side), pool, 0, early))
        other = after(other, *picked[-1])
    terms, other_terms = pool_terms(side, other, pool, pool_square, placed)
    foreign = [flip(side, "batch", k) for k in range(1, batch_size)] if hold_all else []

    flipped = flip(other_terms, "centre", 1)
    if early:
        picked.append(pick_rows(after(index, other_terms), pool, early, early))
        flipped = after(flipped, *picked[-1])
    total = terms - placed_targets + flipped
    kernels, at = [], 2 * early
    distance = 2
    while distance < centre_size:
        if at < count:
            size = span if not kernels else 2 * span
            size = min(size, count - at)
            before = [] if kernels else picked
            *pair, kernel = pick_rows_and_own(
                after(index, total), pool, side, other, before, at, size
            )
            picked, kernels, at = [*picked, pair], [*kernels, kernel], at + size
        total = after(total + flip(total, "centre", distance), *picked[-1])
        distance *= 2
    if hold_all:
        foreign = lax.optimization_barrier((total, *foreign))[1:]
        side_rows = jnp.concatenate(foreign, axis=0)
        other_rows = flip(side_rows, "centre", 1)
    residual_side = total.astype(jnp.bfloat16)
    rests, other_rests = [], []
    if hold_all:
        rests, other_rests = [kernel_block([side_rows], picked)], [kernel_block([other_rows], picked)]
        parts = [residual_side] + [flip(residual_side, "batch", k) for k in range(1, batch_size)]
        rests, other_rests, parts = lax.optimization_barrier((rests, other_rests, parts))
        residual_side = jnp.concatenate(parts, axis=1)
    residual_other = flip(residual_side, "centre", 1)

    step = 8.0 / math.sqrt(batch_total)
    start = base if hold_all else jnp.zeros_like(base)
    updated, residual = descend(
        place, total, own_count, residual_side, start, kernels, rests, step
    )
    updated = finish(residual_other, updated, kernels, other_rests, rows, step)
    if not hold_all:
        updated = base + lax.psum(updated, "batch")
    return (updated.T, residual)


def solution(mesh):
    return jax.shard_map(
        on_device,
        mesh=mesh,
        in_specs=(
            P(("batch", "centre"), None),
            P(("batch", "centre")),
            P("centre", None),
            P("centre"),
            P(("batch", "centre"), None),
            P("centre", None),
        ),
        out_specs=(P("centre", None), P(("batch", "centre"), None)),
        check_vma=False,
    )
```

```python
import functools
import math

import jax
import jax.numpy as jnp
from jax import lax
from jax.experimental import pallas as pl
from jax.experimental.pallas import tpu as pltpu
from jax.sharding import PartitionSpec as P

LANES = 128


def flip(value, axis, distance):
    count = lax.axis_size(axis)
    return lax.ppermute(value, axis, [(i, i ^ distance) for i in range(count)])


def after(value, *others):
    return lax.optimization_barrier((value,) + others)[0]


def contract_last(left, right):
    return lax.dot_general(
        left, right, (((1,), (1,)), ((), ())), preferred_element_type=jnp.float32
    )


def spans(total, most):
    return [(at, min(most, total - at)) for at in range(0, total, most)]


def tiles(count):
    return -(-count // LANES) * LANES


WHOLE = pl.BlockSpec(memory_space=pltpu.VMEM)
SCALARS = pl.BlockSpec(memory_space=pltpu.SMEM)
FAR = pl.BlockSpec(memory_space=pltpu.HBM)


def call(body, operands, outputs, scratch=(), limit=28):
    arrays = [array for array, _ in operands]
    shapes = [jax.ShapeDtypeStruct(shape, dtype) for shape, dtype, _ in outputs]
    return pl.pallas_call(
        body,
        in_specs=[place for _, place in operands],
        out_specs=[place for _, _, place in outputs],
        out_shape=shapes,
        scratch_shapes=list(scratch),
        cost_estimate=pl.CostEstimate(flops=1024, bytes_accessed=1024, transcendentals=0),
        compiler_params=pltpu.CompilerParams(vmem_limit_bytes=limit << 20),
    )(*arrays)


def staggered(steps):
    held = None
    for first, then in steps:
        result = first()
        if held is not None:
            held()
        held = functools.partial(then, result)
    held()


def narrow(index, pool_ref):
    return index.astype(jnp.int16 if pool_ref.shape[0] < 1 << 15 else jnp.int32)


def one_hot(hit):
    return jnp.where(hit, jnp.bfloat16(1.0), jnp.bfloat16(0.0))


def turned(column):
    return jnp.concatenate(
        [
            jnp.broadcast_to(column[at : at + LANES], (LANES, 8)).T[:1]
            for at in range(0, column.shape[0], LANES)
        ],
        axis=1,
    )


def pool_rows(pool_ref, at, size):
    if at + size <= pool_ref.shape[0]:
        return pool_ref[at : at + size, :]
    whole = (pool_ref.shape[0] - at) // LANES * LANES
    place = lax.broadcasted_iota(jnp.int32, (size - whole, pool_ref.shape[1]), 0)
    rows = jnp.zeros(place.shape, jnp.float32)
    for row in range(at + whole, pool_ref.shape[0]):
        wide = pool_ref[row : row + 1, :].astype(jnp.float32)
        rows = jnp.where(place == row - at - whole, wide, rows)
    rows = rows.astype(jnp.bfloat16)
    if whole == 0:
        return rows
    return jnp.concatenate([pool_ref[at : at + whole, :], rows], axis=0)


def place_body(index_ref, base_ref, pool_far, placed_ref, square_ref, kept_ref, pool_ref, done_ref):
    fetch = pltpu.make_async_copy(pool_far, pool_ref, done_ref)
    fetch.start()
    index = narrow(index_ref[...], pool_ref)
    base = base_ref[...]
    kept_ref[...] = base
    half = base.astype(jnp.bfloat16)
    cuts = spans(placed_ref.shape[1], 2 * LANES)
    left, arrival = list(cuts), min(3, len(cuts) - 1)
    for turn, (at, size) in enumerate(cuts):
        place = lax.broadcasted_iota(index.dtype, (size, index.shape[1]), 0)
        chosen = one_hot(index - jnp.asarray(at, index.dtype) == place)
        placed_ref[:, at : at + size] = contract_last(half, chosen).astype(jnp.bfloat16)
        if turn == arrival:
            fetch.wait()
        share = -(-len(left) // (len(cuts) - turn)) if turn >= arrival else 0
        for from_row, count in left[:share]:
            rows = pool_rows(pool_ref, from_row, count).astype(jnp.float32)
            square_ref[from_row : from_row + count, :] = jnp.broadcast_to(
                jnp.sum(rows * rows, axis=1, keepdims=True), (count, LANES)
            )
        left = left[share:]


def place_coefficients(index, base, pool):
    width = tiles(pool.shape[0])
    return call(
        place_body,
        [(index, WHOLE), (base, WHOLE), (pool, FAR)],
        [
            ((base.shape[0], width), jnp.bfloat16, WHOLE),
            ((width, LANES), jnp.float32, WHOLE),
            (base.shape, jnp.float32, WHOLE),
            (pool.shape, jnp.bfloat16, WHOLE),
        ],
        [pltpu.SemaphoreType.DMA(())],
        limit=40,
    )


def turn_over(source_ref, target_ref):
    for row in range(0, source_ref.shape[0], LANES):
        for column in range(0, source_ref.shape[1], LANES):
            target_ref[column : column + LANES, row : row + LANES] = source_ref[
                row : row + LANES, column : column + LANES
            ].T


def arrange_body(place_ref, targets_ref, *refs):
    pieces, (side_ref, placed_ref, wide_ref, tall_ref) = refs[:-4], refs[-4:]
    count = targets_ref.shape[0]
    for k, piece_ref in enumerate(pieces):
        at = pl.multiple_of((place_ref[0] ^ k) * count, count)
        side_ref[pl.ds(at, count), :] = piece_ref[...]
    wide_ref[...] = jnp.zeros_like(wide_ref)
    at = pl.multiple_of(place_ref[0] * count, count)
    wide_ref[pl.ds(at, count), : targets_ref.shape[1]] = targets_ref[...]
    turn_over(wide_ref, tall_ref)
    placed_ref[...] = tall_ref[: placed_ref.shape[0], : placed_ref.shape[1]]


def arrange(place, targets, pieces):
    count, outs = targets.shape
    rows = count * len(pieces)
    high, wide = tiles(rows), tiles(outs)
    return call(
        arrange_body,
        [(place, SCALARS), (targets, WHOLE)] + [(piece, WHOLE) for piece in pieces],
        [
            ((rows, pieces[0].shape[1]), jnp.bfloat16, WHOLE),
            ((outs, rows), jnp.float32, WHOLE),
        ],
        [pltpu.VMEM((high, wide), jnp.float32), pltpu.VMEM((wide, high), jnp.float32)],
    )


def kernel_of(squared):
    least = jnp.maximum(squared, 1e-30)
    return jnp.exp2(least * -math.log2(math.e) * lax.rsqrt(least)).astype(jnp.bfloat16)


def halves_and_squares(samples):
    wide = samples.astype(jnp.float32)
    return (wide * -2.0).astype(jnp.bfloat16), jnp.sum(wide * wide, axis=1, keepdims=True)


def column_of(row):
    return jnp.concatenate(
        [
            jnp.broadcast_to(row[:, at : at + LANES], (LANES, LANES)).T
            for at in range(0, row.shape[1], LANES)
        ],
        axis=0,
    )


def terms_body(side_ref, other_ref, pool_ref, square_ref, placed_ref, *refs):
    terms_ref, other_terms_ref, kernel_ref = refs
    samples = jnp.concatenate([side_ref[...], other_ref[...]], axis=0)
    samples, own_square = halves_and_squares(samples)
    own_square = turned(own_square)

    def product(at, size):
        return contract_last(pool_rows(pool_ref, at, size), samples)

    def values(at, size, cross):
        for lane in range(0, samples.shape[0], LANES):
            lanes = slice(lane, lane + LANES)
            squared = square_ref[at : at + size, :] + own_square[:, lanes] + cross[:, lanes]
            kernel_ref[at : at + size, lanes] = kernel_of(squared)

    staggered(
        (functools.partial(product, at, size), functools.partial(values, at, size))
        for at, size in spans(placed_ref.shape[1], 4 * LANES)
    )
    terms = jnp.dot(placed_ref[...], kernel_ref[...], preferred_element_type=jnp.float32)
    rows = side_ref.shape[0]
    terms_ref[...] = terms[:, :rows]
    other_terms_ref[...] = terms[:, rows:]


def pool_terms(side, other, pool, square, placed):
    outs, rows = placed.shape[0], side.shape[0]
    return call(
        terms_body,
        [(array, WHOLE) for array in (side, other, pool, square, placed)],
        [((outs, rows), jnp.float32, WHOLE)] * 2,
        [pltpu.VMEM((placed.shape[1], 2 * rows), jnp.bfloat16)],
    )


def pick_steps(index_ref, pool_ref, rows_ref, square_ref, first, then=None):
    whole = pool_ref.shape[0] // LANES * LANES

    def product(at, size):
        wanted = column_of(index_ref[:, first + at : first + at + size])
        place = narrow(wanted, pool_ref)
        lane = lax.broadcasted_iota(place.dtype, (size, LANES), 1)
        chosen = jnp.concatenate(
            [
                one_hot(place - jnp.asarray(part, place.dtype) == lane)
                for part in range(0, whole, LANES)
            ],
            axis=1,
        )
        rows = jnp.dot(chosen, pool_ref[:whole, :], preferred_element_type=jnp.float32)
        return wanted, rows

    def values(at, size, result):
        wanted, rows = result
        for row in range(whole, pool_ref.shape[0]):
            rows = rows + jnp.where(
                wanted[:, :1] == row, pool_ref[row : row + 1, :].astype(jnp.float32), 0.0
            )
        rows_ref[at : at + size, :] = rows.astype(jnp.bfloat16)
        square_ref[:, at : at + size] = turned(jnp.sum(rows * rows, axis=1, keepdims=True))
        if then is not None:
            then(at, size)

    return [
        (functools.partial(product, at, size), functools.partial(values, at, size))
        for at, size in spans(rows_ref.shape[0], 4 * LANES)
    ]


def pick_body(first, index_ref, pool_ref, rows_ref, square_ref):
    staggered(pick_steps(index_ref, pool_ref, rows_ref, square_ref, first))


def pick_rows(index, pool, first, count):
    return call(
        functools.partial(pick_body, first),
        [(index, WHOLE), (pool, WHOLE)],
        [((count, pool.shape[1]), jnp.bfloat16, WHOLE), ((1, count), jnp.float32, WHOLE)],
    )


def pick_own_body(first, index_ref, pool_ref, side_ref, other_ref, *refs):
    *before, rows_ref, square_ref, kernel_ref = refs
    samples = jnp.concatenate([side_ref[...], other_ref[...]], axis=0)
    samples, own_square = halves_and_squares(samples)

    def early_product(early_ref, early_square_ref, start):
        return contract_last(samples, early_ref[...])

    def early_values(early_ref, early_square_ref, start, cross):
        kernel = kernel_of(own_square + early_square_ref[...] + cross)
        kernel_ref[:, start : start + early_ref.shape[0]] = kernel

    def own_values(at, size):
        cross = contract_last(samples, rows_ref[at : at + size, :])
        kernel = kernel_of(own_square + square_ref[:, at : at + size] + cross)
        kernel_ref[:, start + at : start + at + size] = kernel

    steps, start = [], 0
    for early_ref, early_square_ref in zip(before[::2], before[1::2]):
        place = (early_ref, early_square_ref, start)
        steps.append(
            (functools.partial(early_product, *place), functools.partial(early_values, *place))
        )
        start += early_ref.shape[0]
    staggered(steps + pick_steps(index_ref, pool_ref, rows_ref, square_ref, first, own_values))


def pick_rows_and_own(index, pool, side, other, before, first, count):
    rows = side.shape[0] + other.shape[0]
    early = sum(square.shape[1] for _, square in before)
    return call(
        functools.partial(pick_own_body, first),
        [(array, WHOLE) for array in (index, pool, side, other)]
        + [(array, WHOLE) for pair in before for array in pair],
        [
            ((count, pool.shape[1]), jnp.bfloat16, WHOLE),
            ((1, count), jnp.float32, WHOLE),
            ((rows, early + count), jnp.bfloat16, WHOLE),
        ],
    )


def block_body(parts, *refs):
    samples = jnp.concatenate([ref[...] for ref in refs[:parts]], axis=0)
    kernel_ref = refs[-1]
    samples, own_square = halves_and_squares(samples)

    def product(rows_ref, square_ref, start, at, size):
        return contract_last(samples, rows_ref[at : at + size, :])

    def values(rows_ref, square_ref, start, at, size, cross):
        kernel = kernel_of(own_square + square_ref[:, at : at + size] + cross)
        kernel_ref[:, start + at : start + at + size] = kernel

    steps, start = [], 0
    for rows_ref, square_ref in zip(refs[parts:-1:2], refs[parts + 1 : -1 : 2]):
        for at, size in spans(rows_ref.shape[0], 2 * LANES):
            place = (rows_ref, square_ref, start, at, size)
            steps.append((functools.partial(product, *place), functools.partial(values, *place)))
        start += rows_ref.shape[0]
    staggered(steps)


def kernel_block(samples, picked):
    rows = sum(part.shape[0] for part in samples)
    count = sum(square.shape[1] for _, square in picked)
    return call(
        functools.partial(block_body, len(samples)),
        [(part, WHOLE) for part in samples]
        + [(array, WHOLE) for pair in picked for array in pair],
        [((rows, count), jnp.bfloat16, WHOLE)],
    )[0]


def gradient_span(residual_ref, kernel_refs, owns, first, at, size):
    own_refs, rest_refs = kernel_refs[:owns], kernel_refs[owns:]
    span = own_refs[0].shape[1]
    own_ref, own_at = own_refs[at // span], at % span
    rows = residual_ref.shape[1] - sum(rest_ref.shape[0] for rest_ref in rest_refs)
    gradient = jnp.dot(
        residual_ref[:, :rows],
        own_ref[first : first + rows, own_at : own_at + size],
        preferred_element_type=jnp.float32,
    )
    for rest_ref in rest_refs:
        gradient = gradient + jnp.dot(
            residual_ref[:, rows:], rest_ref[:, at : at + size], preferred_element_type=jnp.float32
        )
    return gradient


def descend_body(step, owns, kernels, place_ref, total_ref, residual_ref, base_ref, *refs):
    kernel_refs, refs = refs[:kernels], refs[kernels:]
    out_ref, own_far, tall_ref, wide_ref, own_ref, done_ref = refs
    outs, rows = total_ref.shape
    count = own_ref.shape[0]
    tall_ref[...] = jnp.zeros_like(tall_ref)
    tall_ref[:outs, :rows] = total_ref[...]
    turn_over(tall_ref, wide_ref)
    at = pl.multiple_of(place_ref[0] * count, count)
    own_ref[...] = wide_ref[pl.ds(at, count), :outs]
    store = pltpu.make_async_copy(own_ref, own_far, done_ref)
    store.start()
    for at, size in spans(base_ref.shape[1], 4 * LANES):
        gradient = gradient_span(residual_ref, kernel_refs, owns, 0, at, size)
        out_ref[:, at : at + size] = base_ref[:, at : at + size] - step * gradient
    store.wait()


def descend(place, total, count, residual, base, owns, rests, step):
    outs, rows = total.shape
    high, wide = tiles(rows), tiles(outs)
    kernels = [*owns, *rests]
    return call(
        functools.partial(descend_body, step, len(owns), len(kernels)),
        [(place, SCALARS)] + [(array, WHOLE) for array in (total, residual, base, *kernels)],
        [(base.shape, jnp.float32, WHOLE), ((count, outs), jnp.float32, FAR)],
        [
            pltpu.VMEM((wide, high), jnp.float32),
            pltpu.VMEM((high, wide), jnp.float32),
            pltpu.VMEM((count, outs), jnp.float32),
            pltpu.SemaphoreType.DMA(()),
        ],
    )


def finish_body(step, owns, kernels, first, residual_ref, base_ref, *refs):
    kernel_refs, (out_far, held_ref, done_ref) = refs[:kernels], refs[kernels:]
    stores = []
    for turn, (at, size) in enumerate(spans(base_ref.shape[1], 2 * LANES)):
        gradient = gradient_span(residual_ref, kernel_refs, owns, first, at, size)
        held_ref[:, at : at + size] = base_ref[:, at : at + size] - step * gradient
        span = pl.ds(at, size)
        stores.append(
            pltpu.make_async_copy(held_ref.at[:, span], out_far.at[:, span], done_ref.at[turn])
        )
        stores[-1].start()
    for store in stores:
        store.wait()


def finish(residual, base, owns, rests, first, step):
    turns = len(spans(base.shape[1], 2 * LANES))
    kernels = [*owns, *rests]
    return call(
        functools.partial(finish_body, step, len(owns), len(kernels), first),
        [(array, WHOLE) for array in (residual, base, *kernels)],
        [(base.shape, jnp.float32, FAR)],
        [pltpu.VMEM(base.shape, jnp.float32), pltpu.SemaphoreType.DMA((turns,))],
    )[0]


def on_device(batch_pool, batch_index, centre_pool, centre_index, targets, coefficients):
    own_count = batch_index.shape[0]
    batch_size, centre_size = lax.axis_size("batch"), lax.axis_size("centre")
    batch_place, centre_place = lax.axis_index("batch"), lax.axis_index("centre")
    device_place = batch_place * centre_size + centre_place
    batch_total = own_count * batch_size * centre_size
    far_size, far_place = centre_size // 2, lax.shift_right_logical(centre_place, 1)
    rows = far_size * own_count
    hold_all = batch_total * (centre_index.shape[0] + batch_pool.shape[1]) * 2 <= 1 << 24

    count = centre_index.shape[0]
    indices = lax.optimization_barrier(
        jnp.concatenate(
            [
                centre_index - centre_place * centre_pool.shape[0],
                batch_index - device_place * batch_pool.shape[0],
            ]
        )
    )
    chosen = indices[count:, None] == jnp.arange(batch_pool.shape[0])
    local_rows = jnp.dot(
        chosen.astype(jnp.bfloat16), batch_pool, preferred_element_type=jnp.float32
    ).astype(jnp.bfloat16)
    pieces = [local_rows] + [flip(local_rows, "centre", 2 * k) for k in range(1, far_size)]

    place = jnp.reshape(far_place, (1,)).astype(jnp.int32)
    index, place = lax.optimization_barrier((indices[:count].reshape(1, -1), place))
    placed, pool_square, base, pool = place_coefficients(index, coefficients.T, centre_pool)
    placed, *pieces = lax.optimization_barrier((placed, *pieces))
    side, placed_targets = arrange(place, targets, pieces)
    other = flip(side, "centre", 1)
    steps = far_size.bit_length() - 1
    span = count // (2 * steps) if steps and count % (2 * steps * LANES) == 0 else count
    early = span // 2 if span < count and span % (2 * LANES) == 0 else 0
    picked = []
    if early:
        picked.append(pick_rows(after(index, side), pool, 0, early))
        other = after(other, *picked[-1])
    terms, other_terms = pool_terms(side, other, pool, pool_square, placed)
    foreign = [flip(side, "batch", k) for k in range(1, batch_size)] if hold_all else []

    flipped = flip(other_terms, "centre", 1)
    if early:
        picked.append(pick_rows(after(index, other_terms), pool, early, early))
        flipped = after(flipped, *picked[-1])
    total = terms - placed_targets + flipped
    kernels, at = [], 2 * early
    distance = 2
    while distance < centre_size:
        if at < count:
            size = span if not kernels else 2 * span
            size = min(size, count - at)
            before = [] if kernels else picked
            *pair, kernel = pick_rows_and_own(
                after(index, total), pool, side, other, before, at, size
            )
            picked, kernels, at = [*picked, pair], [*kernels, kernel], at + size
        total = after(total + flip(total, "centre", distance), *picked[-1])
        distance *= 2
    if hold_all:
        foreign = lax.optimization_barrier((total, *foreign))[1:]
        side_rows = jnp.concatenate(foreign, axis=0)
        other_rows = flip(side_rows, "centre", 1)
    residual_side = total.astype(jnp.bfloat16)
    rests, other_rests = [], []
    if hold_all:
        rests, other_rests = [kernel_block([side_rows], picked)], [kernel_block([other_rows], picked)]
        parts = [residual_side] + [flip(residual_side, "batch", k) for k in range(1, batch_size)]
        rests, other_rests, parts = lax.optimization_barrier((rests, other_rests, parts))
        residual_side = jnp.concatenate(parts, axis=1)
    residual_other = flip(residual_side, "centre", 1)

    step = 8.0 / math.sqrt(batch_total)
    start = base if hold_all else jnp.zeros_like(base)
    updated, residual = descend(
        place, total, own_count, residual_side, start, kernels, rests, step
    )
    updated = finish(residual_other, updated, kernels, other_rests, rows, step)
    if not hold_all:
        updated = base + lax.psum(updated, "batch")
    return (updated.T, residual)


def solution(mesh):
    return jax.shard_map(
        on_device,
        mesh=mesh,
        in_specs=(
            P(("batch", "centre"), None),
            P(("batch", "centre")),
            P("centre", None),
            P("centre"),
            P(("batch", "centre"), None),
            P("centre", None),
        ),
        out_specs=(P("centre", None), P(("batch", "centre"), None)),
        check_vma=False,
    )
```

```python
import functools
import math

import jax
import jax.numpy as jnp
from jax import lax
from jax.experimental import pallas as pl
from jax.experimental.pallas import tpu as pltpu
from jax.sharding import PartitionSpec as P

LANES = 128


def flip(value, axis, distance):
    count = lax.axis_size(axis)
    return lax.ppermute(value, axis, [(i, i ^ distance) for i in range(count)])


def after(value, *others):
    return lax.optimization_barrier((value,) + others)[0]


def contract_last(left, right):
    return lax.dot_general(
        left, right, (((1,), (1,)), ((), ())), preferred_element_type=jnp.float32
    )


def spans(total, most):
    return [(at, min(most, total - at)) for at in range(0, total, most)]


def tiles(count):
    return -(-count // LANES) * LANES


WHOLE = pl.BlockSpec(memory_space=pltpu.VMEM)
SCALARS = pl.BlockSpec(memory_space=pltpu.SMEM)
FAR = pl.BlockSpec(memory_space=pltpu.HBM)


def call(body, operands, outputs, scratch=(), limit=28):
    arrays = [array for array, _ in operands]
    shapes = [jax.ShapeDtypeStruct(shape, dtype) for shape, dtype, _ in outputs]
    return pl.pallas_call(
        body,
        in_specs=[place for _, place in operands],
        out_specs=[place for _, _, place in outputs],
        out_shape=shapes,
        scratch_shapes=list(scratch),
        cost_estimate=pl.CostEstimate(flops=1024, bytes_accessed=1024, transcendentals=0),
        compiler_params=pltpu.CompilerParams(vmem_limit_bytes=limit << 20),
    )(*arrays)


def staggered(steps):
    held = None
    for first, then in steps:
        result = first()
        if held is not None:
            held()
        held = functools.partial(then, result)
    held()


def one_hot(hit):
    return jnp.where(hit, jnp.bfloat16(1.0), jnp.bfloat16(0.0))


def turned(column):
    return jnp.concatenate(
        [
            jnp.broadcast_to(column[at : at + LANES], (LANES, 8)).T[:1]
            for at in range(0, column.shape[0], LANES)
        ],
        axis=1,
    )


def column_of(row):
    return jnp.concatenate(
        [
            jnp.broadcast_to(row[:, at : at + LANES], (LANES, LANES)).T
            for at in range(0, row.shape[1], LANES)
        ],
        axis=0,
    )


def pool_rows(pool_ref, at, size):
    if at + size <= pool_ref.shape[0]:
        return pool_ref[at : at + size, :]
    whole = (pool_ref.shape[0] - at) // LANES * LANES
    place = lax.broadcasted_iota(jnp.int32, (size - whole, pool_ref.shape[1]), 0)
    rows = jnp.zeros(place.shape, jnp.float32)
    for row in range(at + whole, pool_ref.shape[0]):
        wide = pool_ref[row : row + 1, :].astype(jnp.float32)
        rows = jnp.where(place == row - at - whole, wide, rows)
    rows = rows.astype(jnp.bfloat16)
    if whole == 0:
        return rows
    return jnp.concatenate([pool_ref[at : at + whole, :], rows], axis=0)


def place_body(index_ref, base_ref, pool_far, *refs):
    placed_ref, square_ref, column_ref, kept_ref, pool_ref, done_ref = refs
    fetch = pltpu.make_async_copy(pool_far, pool_ref, done_ref)
    fetch.start()
    index = column_of(index_ref[...]).astype(column_ref.dtype)
    column_ref[...] = index
    base = base_ref[...]
    kept_ref[...] = base
    half = base.astype(jnp.bfloat16)
    lane = lax.broadcasted_iota(index.dtype, index.shape, 1)
    cuts = spans(placed_ref.shape[1], 2 * LANES)
    left, arrival = list(cuts), min(3, len(cuts) - 1)
    for turn, (at, size) in enumerate(cuts):
        chosen = [
            one_hot(index - jnp.asarray(part, index.dtype) == lane)
            for part in range(at, at + size, LANES)
        ]
        placed_ref[:, at : at + size] = jnp.dot(
            half, jnp.concatenate(chosen, axis=1), preferred_element_type=jnp.float32
        ).astype(jnp.bfloat16)
        if turn == arrival:
            fetch.wait()
        share = -(-len(left) // (len(cuts) - turn)) if turn >= arrival else 0
        for from_row, count in left[:share]:
            rows = pool_rows(pool_ref, from_row, count).astype(jnp.float32)
            square_ref[from_row : from_row + count, :] = jnp.broadcast_to(
                jnp.sum(rows * rows, axis=1, keepdims=True), (count, LANES)
            )
        left = left[share:]


def place_coefficients(index, base, pool):
    width = tiles(pool.shape[0])
    narrow = jnp.int16 if pool.shape[0] < 1 << 15 else jnp.int32
    return call(
        place_body,
        [(index, WHOLE), (base, WHOLE), (pool, FAR)],
        [
            ((base.shape[0], width), jnp.bfloat16, WHOLE),
            ((width, LANES), jnp.float32, WHOLE),
            ((index.shape[1], LANES), narrow, WHOLE),
            (base.shape, jnp.float32, WHOLE),
            (pool.shape, jnp.bfloat16, WHOLE),
        ],
        [pltpu.SemaphoreType.DMA(())],
        limit=39,
    )


def turn_over(source_ref, target_ref):
    for row in range(0, source_ref.shape[0], LANES):
        for column in range(0, source_ref.shape[1], LANES):
            target_ref[column : column + LANES, row : row + LANES] = source_ref[
                row : row + LANES, column : column + LANES
            ].T


def arrange_body(place_ref, targets_ref, *refs):
    pieces, (side_ref, placed_ref, wide_ref, tall_ref) = refs[:-4], refs[-4:]
    count = targets_ref.shape[0]
    for k, piece_ref in enumerate(pieces):
        at = pl.multiple_of((place_ref[0] ^ k) * count, count)
        side_ref[pl.ds(at, count), :] = piece_ref[...]
    wide_ref[...] = jnp.zeros_like(wide_ref)
    at = pl.multiple_of(place_ref[0] * count, count)
    wide_ref[pl.ds(at, count), : targets_ref.shape[1]] = targets_ref[...]
    turn_over(wide_ref, tall_ref)
    placed_ref[...] = tall_ref[: placed_ref.shape[0], : placed_ref.shape[1]]


def arrange(place, targets, pieces):
    count, outs = targets.shape
    rows = count * len(pieces)
    high, wide = tiles(rows), tiles(outs)
    return call(
        arrange_body,
        [(place, SCALARS), (targets, WHOLE)] + [(piece, WHOLE) for piece in pieces],
        [
            ((rows, pieces[0].shape[1]), jnp.bfloat16, WHOLE),
            ((outs, rows), jnp.float32, WHOLE),
        ],
        [pltpu.VMEM((high, wide), jnp.float32), pltpu.VMEM((wide, high), jnp.float32)],
    )


def kernel_of(squared):
    least = jnp.maximum(squared, 1e-30)
    return jnp.exp2(least * -math.log2(math.e) * lax.rsqrt(least)).astype(jnp.bfloat16)


def halves_and_squares(samples):
    wide = samples.astype(jnp.float32)
    return (wide * -2.0).astype(jnp.bfloat16), jnp.sum(wide * wide, axis=1, keepdims=True)


def terms_body(side_ref, other_ref, pool_ref, square_ref, placed_ref, *refs):
    terms_ref, other_terms_ref, kernel_ref = refs
    samples = jnp.concatenate([side_ref[...], other_ref[...]], axis=0)
    samples, own_square = halves_and_squares(samples)
    own_square = turned(own_square)

    def product(at, size):
        return contract_last(pool_rows(pool_ref, at, size), samples)

    def values(at, size, cross):
        for lane in range(0, samples.shape[0], LANES):
            lanes = slice(lane, lane + LANES)
            squared = square_ref[at : at + size, :] + own_square[:, lanes] + cross[:, lanes]
            kernel_ref[at : at + size, lanes] = kernel_of(squared)

    staggered(
        (functools.partial(product, at, size), functools.partial(values, at, size))
        for at, size in spans(placed_ref.shape[1], 4 * LANES)
    )
    terms = jnp.dot(placed_ref[...], kernel_ref[...], preferred_element_type=jnp.float32)
    rows = side_ref.shape[0]
    terms_ref[...] = terms[:, :rows]
    other_terms_ref[...] = terms[:, rows:]


def pool_terms(side, other, pool, square, placed):
    outs, rows = placed.shape[0], side.shape[0]
    return call(
        terms_body,
        [(array, WHOLE) for array in (side, other, pool, square, placed)],
        [((outs, rows), jnp.float32, WHOLE)] * 2,
        [pltpu.VMEM((placed.shape[1], 2 * rows), jnp.bfloat16)],
    )


def pick_steps(index_ref, pool_ref, rows_ref, square_ref, first, then=None):
    whole = pool_ref.shape[0] // LANES * LANES

    def product(at, size):
        place = index_ref[first + at : first + at + size, :]
        lane = lax.broadcasted_iota(place.dtype, (size, LANES), 1)
        chosen = jnp.concatenate(
            [
                one_hot(place - jnp.asarray(part, place.dtype) == lane)
                for part in range(0, whole, LANES)
            ],
            axis=1,
        )
        rows = jnp.dot(chosen, pool_ref[:whole, :], preferred_element_type=jnp.float32)
        return place.astype(jnp.int32), rows

    def values(at, size, result):
        wanted, rows = result
        for row in range(whole, pool_ref.shape[0]):
            rows = rows + jnp.where(
                wanted[:, :1] == row, pool_ref[row : row + 1, :].astype(jnp.float32), 0.0
            )
        rows_ref[at : at + size, :] = rows.astype(jnp.bfloat16)
        square_ref[:, at : at + size] = turned(jnp.sum(rows * rows, axis=1, keepdims=True))
        if then is not None:
            then(at, size)

    return [
        (functools.partial(product, at, size), functools.partial(values, at, size))
        for at, size in spans(rows_ref.shape[0], 4 * LANES)
    ]


def pick_body(first, index_ref, pool_ref, rows_ref, square_ref):
    staggered(pick_steps(index_ref, pool_ref, rows_ref, square_ref, first))


def pick_rows(index, pool, first, count):
    return call(
        functools.partial(pick_body, first),
        [(index, WHOLE), (pool, WHOLE)],
        [((count, pool.shape[1]), jnp.bfloat16, WHOLE), ((1, count), jnp.float32, WHOLE)],
    )


def pick_own_body(first, index_ref, pool_ref, side_ref, other_ref, *refs):
    *before, rows_ref, square_ref, kernel_ref = refs
    samples = jnp.concatenate([side_ref[...], other_ref[...]], axis=0)
    samples, own_square = halves_and_squares(samples)

    def early_product(early_ref, early_square_ref, start):
        return contract_last(samples, early_ref[...])

    def early_values(early_ref, early_square_ref, start, cross):
        kernel = kernel_of(own_square + early_square_ref[...] + cross)
        kernel_ref[:, start : start + early_ref.shape[0]] = kernel

    def own_values(at, size):
        cross = contract_last(samples, rows_ref[at : at + size, :])
        kernel = kernel_of(own_square + square_ref[:, at : at + size] + cross)
        kernel_ref[:, start + at : start + at + size] = kernel

    steps, start = [], 0
    for early_ref, early_square_ref in zip(before[::2], before[1::2]):
        place = (early_ref, early_square_ref, start)
        steps.append(
            (functools.partial(early_product, *place), functools.partial(early_values, *place))
        )
        start += early_ref.shape[0]
    staggered(steps + pick_steps(index_ref, pool_ref, rows_ref, square_ref, first, own_values))


def pick_rows_and_own(index, pool, side, other, before, first, count):
    rows = side.shape[0] + other.shape[0]
    early = sum(square.shape[1] for _, square in before)
    return call(
        functools.partial(pick_own_body, first),
        [(array, WHOLE) for array in (index, pool, side, other)]
        + [(array, WHOLE) for pair in before for array in pair],
        [
            ((count, pool.shape[1]), jnp.bfloat16, WHOLE),
            ((1, count), jnp.float32, WHOLE),
            ((rows, early + count), jnp.bfloat16, WHOLE),
        ],
    )


def block_body(parts, *refs):
    samples = jnp.concatenate([ref[...] for ref in refs[:parts]], axis=0)
    kernel_ref = refs[-1]
    samples, own_square = halves_and_squares(samples)

    def product(rows_ref, square_ref, start, at, size):
        return contract_last(samples, rows_ref[at : at + size, :])

    def values(rows_ref, square_ref, start, at, size, cross):
        kernel = kernel_of(own_square + square_ref[:, at : at + size] + cross)
        kernel_ref[:, start + at : start + at + size] = kernel

    steps, start = [], 0
    for rows_ref, square_ref in zip(refs[parts:-1:2], refs[parts + 1 : -1 : 2]):
        for at, size in spans(rows_ref.shape[0], 2 * LANES):
            place = (rows_ref, square_ref, start, at, size)
            steps.append((functools.partial(product, *place), functools.partial(values, *place)))
        start += rows_ref.shape[0]
    staggered(steps)


def kernel_block(samples, picked):
    rows = sum(part.shape[0] for part in samples)
    count = sum(square.shape[1] for _, square in picked)
    return call(
        functools.partial(block_body, len(samples)),
        [(part, WHOLE) for part in samples]
        + [(array, WHOLE) for pair in picked for array in pair],
        [((rows, count), jnp.bfloat16, WHOLE)],
    )[0]


def gradient_span(residual_ref, kernel_refs, owns, first, at, size):
    own_refs, rest_refs = kernel_refs[:owns], kernel_refs[owns:]
    span = own_refs[0].shape[1]
    own_ref, own_at = own_refs[at // span], at % span
    rows = residual_ref.shape[1] - sum(rest_ref.shape[0] for rest_ref in rest_refs)
    gradient = jnp.dot(
        residual_ref[:, :rows],
        own_ref[first : first + rows, own_at : own_at + size],
        preferred_element_type=jnp.float32,
    )
    for rest_ref in rest_refs:
        gradient = gradient + jnp.dot(
            residual_ref[:, rows:], rest_ref[:, at : at + size], preferred_element_type=jnp.float32
        )
    return gradient


def descend_body(step, owns, kernels, place_ref, total_ref, residual_ref, base_ref, *refs):
    kernel_refs, refs = refs[:kernels], refs[kernels:]
    out_ref, own_far, tall_ref, wide_ref, own_ref, done_ref = refs
    outs, rows = total_ref.shape
    count = own_ref.shape[0]
    tall_ref[...] = jnp.zeros_like(tall_ref)
    tall_ref[:outs, :rows] = total_ref[...]
    turn_over(tall_ref, wide_ref)
    at = pl.multiple_of(place_ref[0] * count, count)
    own_ref[...] = wide_ref[pl.ds(at, count), :outs]
    store = pltpu.make_async_copy(own_ref, own_far, done_ref)
    store.start()
    for at, size in spans(base_ref.shape[1], 4 * LANES):
        gradient = gradient_span(residual_ref, kernel_refs, owns, 0, at, size)
        out_ref[:, at : at + size] = base_ref[:, at : at + size] - step * gradient
    store.wait()


def descend(place, total, count, residual, base, owns, rests, step):
    outs, rows = total.shape
    high, wide = tiles(rows), tiles(outs)
    kernels = [*owns, *rests]
    return call(
        functools.partial(descend_body, step, len(owns), len(kernels)),
        [(place, SCALARS)] + [(array, WHOLE) for array in (total, residual, base, *kernels)],
        [(base.shape, jnp.float32, WHOLE), ((count, outs), jnp.float32, FAR)],
        [
            pltpu.VMEM((wide, high), jnp.float32),
            pltpu.VMEM((high, wide), jnp.float32),
            pltpu.VMEM((count, outs), jnp.float32),
            pltpu.SemaphoreType.DMA(()),
        ],
    )


def finish_body(step, owns, kernels, first, residual_ref, base_ref, *refs):
    kernel_refs, (out_far, held_ref, done_ref) = refs[:kernels], refs[kernels:]
    stores = []
    for turn, (at, size) in enumerate(spans(base_ref.shape[1], 4 * LANES)):
        gradient = gradient_span(residual_ref, kernel_refs, owns, first, at, size)
        held_ref[:, at : at + size] = base_ref[:, at : at + size] - step * gradient
        span = pl.ds(at, size)
        stores.append(
            pltpu.make_async_copy(held_ref.at[:, span], out_far.at[:, span], done_ref.at[turn])
        )
        stores[-1].start()
    for store in stores:
        store.wait()


def finish(residual, base, owns, rests, first, step):
    turns = len(spans(base.shape[1], 4 * LANES))
    kernels = [*owns, *rests]
    return call(
        functools.partial(finish_body, step, len(owns), len(kernels), first),
        [(array, WHOLE) for array in (residual, base, *kernels)],
        [(base.shape, jnp.float32, FAR)],
        [pltpu.VMEM(base.shape, jnp.float32), pltpu.SemaphoreType.DMA((turns,))],
    )[0]


def on_device(batch_pool, batch_index, centre_pool, centre_index, targets, coefficients):
    own_count = batch_index.shape[0]
    batch_size, centre_size = lax.axis_size("batch"), lax.axis_size("centre")
    batch_place, centre_place = lax.axis_index("batch"), lax.axis_index("centre")
    device_place = batch_place * centre_size + centre_place
    batch_total = own_count * batch_size * centre_size
    far_size, far_place = centre_size // 2, lax.shift_right_logical(centre_place, 1)
    rows = far_size * own_count
    hold_all = batch_total * (centre_index.shape[0] + batch_pool.shape[1]) * 2 <= 1 << 24

    count = centre_index.shape[0]
    indices = lax.optimization_barrier(
        jnp.concatenate(
            [
                centre_index - centre_place * centre_pool.shape[0],
                batch_index - device_place * batch_pool.shape[0],
            ]
        )
    )
    chosen = indices[count:, None] == jnp.arange(batch_pool.shape[0])
    local_rows = jnp.dot(
        chosen.astype(jnp.bfloat16), batch_pool, preferred_element_type=jnp.float32
    ).astype(jnp.bfloat16)
    pieces = [local_rows] + [flip(local_rows, "centre", 2 * k) for k in range(1, far_size)]

    place = jnp.reshape(far_place, (1,)).astype(jnp.int32)
    index, place = lax.optimization_barrier((indices[:count].reshape(1, -1), place))
    placed, pool_square, index, base, pool = place_coefficients(
        index, coefficients.T, centre_pool
    )
    placed, *pieces = lax.optimization_barrier((placed, *pieces))
    side, placed_targets = arrange(place, targets, pieces)
    other = flip(side, "centre", 1)
    steps = far_size.bit_length() - 1
    span = count // (2 * steps) if steps and count % (2 * steps * LANES) == 0 else count
    early = span // 2 if span < count and span % (2 * LANES) == 0 else 0
    picked = []
    if early:
        picked.append(pick_rows(after(index, side), pool, 0, early))
        other = after(other, *picked[-1])
    terms, other_terms = pool_terms(side, other, pool, pool_square, placed)
    foreign = [flip(side, "batch", k) for k in range(1, batch_size)] if hold_all else []

    flipped = flip(other_terms, "centre", 1)
    if early:
        picked.append(pick_rows(after(index, other_terms), pool, early, early))
        flipped = after(flipped, *picked[-1])
    total = terms - placed_targets + flipped
    kernels, at = [], 2 * early
    distance = 2
    while distance < centre_size:
        if at < count:
            size = span if not kernels else 2 * span
            size = min(size, count - at)
            before = [] if kernels else picked
            *pair, kernel = pick_rows_and_own(
                after(index, total), pool, side, other, before, at, size
            )
            picked, kernels, at = [*picked, pair], [*kernels, kernel], at + size
        total = after(total + flip(total, "centre", distance), *picked[-1])
        distance *= 2
    if hold_all:
        foreign = lax.optimization_barrier((total, *foreign))[1:]
        side_rows = jnp.concatenate(foreign, axis=0)
        other_rows = flip(side_rows, "centre", 1)
    residual_side = total.astype(jnp.bfloat16)
    rests, other_rests = [], []
    if hold_all:
        rests, other_rests = [kernel_block([side_rows], picked)], [kernel_block([other_rows], picked)]
        parts = [residual_side] + [flip(residual_side, "batch", k) for k in range(1, batch_size)]
        rests, other_rests, parts = lax.optimization_barrier((rests, other_rests, parts))
        residual_side = jnp.concatenate(parts, axis=1)
    residual_other = flip(residual_side, "centre", 1)

    step = 8.0 / math.sqrt(batch_total)
    start = base if hold_all else jnp.zeros_like(base)
    updated, residual = descend(
        place, total, own_count, residual_side, start, kernels, rests, step
    )
    updated = finish(residual_other, updated, kernels, other_rests, rows, step)
    if not hold_all:
        updated = base + lax.psum(updated, "batch")
    return (updated.T, residual)


def solution(mesh):
    return jax.shard_map(
        on_device,
        mesh=mesh,
        in_specs=(
            P(("batch", "centre"), None),
            P(("batch", "centre")),
            P("centre", None),
            P("centre"),
            P(("batch", "centre"), None),
            P("centre", None),
        ),
        out_specs=(P("centre", None), P(("batch", "centre"), None)),
        check_vma=False,
    )
```

```python
import functools
import math

import jax
import jax.numpy as jnp
from jax import lax
from jax.experimental import pallas as pl
from jax.experimental.pallas import tpu as pltpu
from jax.sharding import PartitionSpec as P

LANES = 128


def flip(value, axis, distance):
    count = lax.axis_size(axis)
    return lax.ppermute(value, axis, [(i, i ^ distance) for i in range(count)])


def after(value, *others):
    return lax.optimization_barrier((value,) + others)[0]


def contract_last(left, right):
    return lax.dot_general(
        left, right, (((1,), (1,)), ((), ())), preferred_element_type=jnp.float32
    )


def spans(total, most):
    return [(at, min(most, total - at)) for at in range(0, total, most)]


def tiles(count):
    return -(-count // LANES) * LANES


WHOLE = pl.BlockSpec(memory_space=pltpu.VMEM)
SCALARS = pl.BlockSpec(memory_space=pltpu.SMEM)
FAR = pl.BlockSpec(memory_space=pltpu.HBM)


def call(body, operands, outputs, scratch=(), limit=28):
    arrays = [array for array, _ in operands]
    shapes = [jax.ShapeDtypeStruct(shape, dtype) for shape, dtype, _ in outputs]
    return pl.pallas_call(
        body,
        in_specs=[place for _, place in operands],
        out_specs=[place for _, _, place in outputs],
        out_shape=shapes,
        scratch_shapes=list(scratch),
        cost_estimate=pl.CostEstimate(flops=1024, bytes_accessed=1024, transcendentals=0),
        compiler_params=pltpu.CompilerParams(vmem_limit_bytes=limit << 20),
    )(*arrays)


def staggered(steps):
    held = None
    for first, then in steps:
        result = first()
        if held is not None:
            held()
        held = functools.partial(then, result)
    held()


def one_hot(hit):
    return jnp.where(hit, jnp.bfloat16(1.0), jnp.bfloat16(0.0))


def turned(column):
    return jnp.concatenate(
        [
            jnp.broadcast_to(column[at : at + LANES], (LANES, 8)).T[:1]
            for at in range(0, column.shape[0], LANES)
        ],
        axis=1,
    )


def column_of(row):
    return jnp.concatenate(
        [
            jnp.broadcast_to(row[:, at : at + LANES], (LANES, LANES)).T
            for at in range(0, row.shape[1], LANES)
        ],
        axis=0,
    )


def pool_rows(pool_ref, at, size):
    if at + size <= pool_ref.shape[0]:
        return pool_ref[at : at + size, :]
    whole = (pool_ref.shape[0] - at) // LANES * LANES
    place = lax.broadcasted_iota(jnp.int32, (size - whole, pool_ref.shape[1]), 0)
    rows = jnp.zeros(place.shape, jnp.float32)
    for row in range(at + whole, pool_ref.shape[0]):
        wide = pool_ref[row : row + 1, :].astype(jnp.float32)
        rows = jnp.where(place == row - at - whole, wide, rows)
    rows = rows.astype(jnp.bfloat16)
    if whole == 0:
        return rows
    return jnp.concatenate([pool_ref[at : at + whole, :], rows], axis=0)


def place_body(index_ref, base_ref, pool_far, *refs):
    placed_ref, square_ref, column_ref, kept_ref, pool_ref, done_ref = refs
    fetch = pltpu.make_async_copy(pool_far, pool_ref, done_ref)
    fetch.start()
    index = column_of(index_ref[...]).astype(column_ref.dtype)
    column_ref[...] = index
    base = base_ref[...]
    kept_ref[...] = base
    half = base.astype(jnp.bfloat16)
    lane = lax.broadcasted_iota(index.dtype, index.shape, 1)
    cuts = spans(placed_ref.shape[1], 2 * LANES)
    left, arrival = list(cuts), min(3, len(cuts) - 1)
    for turn, (at, size) in enumerate(cuts):
        chosen = [
            one_hot(index - jnp.asarray(part, index.dtype) == lane)
            for part in range(at, at + size, LANES)
        ]
        placed_ref[:, at : at + size] = jnp.dot(
            half, jnp.concatenate(chosen, axis=1), preferred_element_type=jnp.float32
        ).astype(jnp.bfloat16)
        if turn == arrival:
            fetch.wait()
        share = -(-len(left) // (len(cuts) - turn)) if turn >= arrival else 0
        for from_row, count in left[:share]:
            rows = pool_rows(pool_ref, from_row, count).astype(jnp.float32)
            square_ref[from_row : from_row + count, :] = jnp.broadcast_to(
                jnp.sum(rows * rows, axis=1, keepdims=True), (count, LANES)
            )
        left = left[share:]


def place_coefficients(index, base, pool):
    width = tiles(pool.shape[0])
    narrow = jnp.int16 if pool.shape[0] < 1 << 15 else jnp.int32
    return call(
        place_body,
        [(index, WHOLE), (base, WHOLE), (pool, FAR)],
        [
            ((base.shape[0], width), jnp.bfloat16, WHOLE),
            ((width, LANES), jnp.float32, WHOLE),
            ((index.shape[1], LANES), narrow, WHOLE),
            (base.shape, jnp.float32, WHOLE),
            (pool.shape, jnp.bfloat16, WHOLE),
        ],
        [pltpu.SemaphoreType.DMA(())],
        limit=39,
    )


def turn_over(source_ref, target_ref):
    for row in range(0, source_ref.shape[0], LANES):
        for column in range(0, source_ref.shape[1], LANES):
            target_ref[column : column + LANES, row : row + LANES] = source_ref[
                row : row + LANES, column : column + LANES
            ].T


def arrange_body(place_ref, targets_ref, *refs):
    pieces, (side_ref, placed_ref, wide_ref, tall_ref) = refs[:-4], refs[-4:]
    count = targets_ref.shape[0]
    for k, piece_ref in enumerate(pieces):
        at = pl.multiple_of((place_ref[0] ^ k) * count, count)
        side_ref[pl.ds(at, count), :] = piece_ref[...]
    wide_ref[...] = jnp.zeros_like(wide_ref)
    at = pl.multiple_of(place_ref[0] * count, count)
    wide_ref[pl.ds(at, count), : targets_ref.shape[1]] = targets_ref[...]
    turn_over(wide_ref, tall_ref)
    placed_ref[...] = tall_ref[: placed_ref.shape[0], : placed_ref.shape[1]]


def arrange(place, targets, pieces):
    count, outs = targets.shape
    rows = count * len(pieces)
    high, wide = tiles(rows), tiles(outs)
    return call(
        arrange_body,
        [(place, SCALARS), (targets, WHOLE)] + [(piece, WHOLE) for piece in pieces],
        [
            ((rows, pieces[0].shape[1]), jnp.bfloat16, WHOLE),
            ((outs, rows), jnp.float32, WHOLE),
        ],
        [pltpu.VMEM((high, wide), jnp.float32), pltpu.VMEM((wide, high), jnp.float32)],
    )


def kernel_of(squared):
    least = jnp.maximum(squared, 1e-30)
    return jnp.exp2(least * -math.log2(math.e) * lax.rsqrt(least)).astype(jnp.bfloat16)


def halves_and_squares(samples):
    wide = samples.astype(jnp.float32)
    return (wide * -2.0).astype(jnp.bfloat16), jnp.sum(wide * wide, axis=1, keepdims=True)


def terms_body(side_ref, other_ref, pool_ref, square_ref, placed_ref, *refs):
    terms_ref, other_terms_ref, kernel_ref = refs
    samples = jnp.concatenate([side_ref[...], other_ref[...]], axis=0)
    samples, own_square = halves_and_squares(samples)
    own_square = turned(own_square)

    def product(at, size):
        return contract_last(pool_rows(pool_ref, at, size), samples)

    def values(at, size, cross):
        for lane in range(0, samples.shape[0], LANES):
            lanes = slice(lane, lane + LANES)
            squared = square_ref[at : at + size, :] + own_square[:, lanes] + cross[:, lanes]
            kernel_ref[at : at + size, lanes] = kernel_of(squared)

    staggered(
        (functools.partial(product, at, size), functools.partial(values, at, size))
        for at, size in spans(placed_ref.shape[1], 4 * LANES)
    )
    terms = jnp.dot(placed_ref[...], kernel_ref[...], preferred_element_type=jnp.float32)
    rows = side_ref.shape[0]
    terms_ref[...] = terms[:, :rows]
    other_terms_ref[...] = terms[:, rows:]


def pool_terms(side, other, pool, square, placed):
    outs, rows = placed.shape[0], side.shape[0]
    return call(
        terms_body,
        [(array, WHOLE) for array in (side, other, pool, square, placed)],
        [((outs, rows), jnp.float32, WHOLE)] * 2,
        [pltpu.VMEM((placed.shape[1], 2 * rows), jnp.bfloat16)],
    )


def pick_steps(index_ref, pool_ref, rows_ref, square_ref, first, then=None):
    whole = pool_ref.shape[0] // LANES * LANES

    def product(at, size):
        place = index_ref[first + at : first + at + size, :]
        lane = lax.broadcasted_iota(place.dtype, (size, LANES), 1)
        chosen = jnp.concatenate(
            [
                one_hot(place - jnp.asarray(part, place.dtype) == lane)
                for part in range(0, whole, LANES)
            ],
            axis=1,
        )
        rows = jnp.dot(chosen, pool_ref[:whole, :], preferred_element_type=jnp.float32)
        return place.astype(jnp.int32), rows

    def values(at, size, result):
        wanted, rows = result
        for row in range(whole, pool_ref.shape[0]):
            rows = rows + jnp.where(
                wanted[:, :1] == row, pool_ref[row : row + 1, :].astype(jnp.float32), 0.0
            )
        rows_ref[at : at + size, :] = rows.astype(jnp.bfloat16)
        square_ref[:, at : at + size] = turned(jnp.sum(rows * rows, axis=1, keepdims=True))
        if then is not None:
            then(at, size)

    return [
        (functools.partial(product, at, size), functools.partial(values, at, size))
        for at, size in spans(rows_ref.shape[0], 4 * LANES)
    ]


def pick_body(first, index_ref, pool_ref, rows_ref, square_ref):
    staggered(pick_steps(index_ref, pool_ref, rows_ref, square_ref, first))


def pick_rows(index, pool, first, count):
    return call(
        functools.partial(pick_body, first),
        [(index, WHOLE), (pool, WHOLE)],
        [((count, pool.shape[1]), jnp.bfloat16, WHOLE), ((1, count), jnp.float32, WHOLE)],
    )


def pick_own_body(first, index_ref, pool_ref, side_ref, other_ref, *refs):
    *before, rows_ref, square_ref, kernel_ref = refs
    samples = jnp.concatenate([side_ref[...], other_ref[...]], axis=0)
    samples, own_square = halves_and_squares(samples)

    def early_product(early_ref, early_square_ref, start):
        return contract_last(samples, early_ref[...])

    def early_values(early_ref, early_square_ref, start, cross):
        kernel = kernel_of(own_square + early_square_ref[...] + cross)
        kernel_ref[:, start : start + early_ref.shape[0]] = kernel

    def own_values(at, size):
        cross = contract_last(samples, rows_ref[at : at + size, :])
        kernel = kernel_of(own_square + square_ref[:, at : at + size] + cross)
        kernel_ref[:, start + at : start + at + size] = kernel

    steps, start = [], 0
    for early_ref, early_square_ref in zip(before[::2], before[1::2]):
        place = (early_ref, early_square_ref, start)
        steps.append(
            (functools.partial(early_product, *place), functools.partial(early_values, *place))
        )
        start += early_ref.shape[0]
    staggered(steps + pick_steps(index_ref, pool_ref, rows_ref, square_ref, first, own_values))


def pick_rows_and_own(index, pool, side, other, before, first, count):
    rows = side.shape[0] + other.shape[0]
    early = sum(square.shape[1] for _, square in before)
    return call(
        functools.partial(pick_own_body, first),
        [(array, WHOLE) for array in (index, pool, side, other)]
        + [(array, WHOLE) for pair in before for array in pair],
        [
            ((count, pool.shape[1]), jnp.bfloat16, WHOLE),
            ((1, count), jnp.float32, WHOLE),
            ((rows, early + count), jnp.bfloat16, WHOLE),
        ],
    )


def block_body(parts, *refs):
    samples = jnp.concatenate([ref[...] for ref in refs[:parts]], axis=0)
    kernel_ref = refs[-1]
    samples, own_square = halves_and_squares(samples)

    def product(rows_ref, square_ref, start, at, size):
        return contract_last(samples, rows_ref[at : at + size, :])

    def values(rows_ref, square_ref, start, at, size, cross):
        kernel = kernel_of(own_square + square_ref[:, at : at + size] + cross)
        kernel_ref[:, start + at : start + at + size] = kernel

    steps, start = [], 0
    for rows_ref, square_ref in zip(refs[parts:-1:2], refs[parts + 1 : -1 : 2]):
        for at, size in spans(rows_ref.shape[0], 2 * LANES):
            place = (rows_ref, square_ref, start, at, size)
            steps.append((functools.partial(product, *place), functools.partial(values, *place)))
        start += rows_ref.shape[0]
    staggered(steps)


def kernel_block(samples, picked):
    rows = sum(part.shape[0] for part in samples)
    count = sum(square.shape[1] for _, square in picked)
    return call(
        functools.partial(block_body, len(samples)),
        [(part, WHOLE) for part in samples]
        + [(array, WHOLE) for pair in picked for array in pair],
        [((rows, count), jnp.bfloat16, WHOLE)],
    )[0]


def gradient_span(residual_ref, kernel_refs, owns, first, at, size):
    own_refs, rest_refs = kernel_refs[:owns], kernel_refs[owns:]
    span = own_refs[0].shape[1]
    own_ref, own_at = own_refs[at // span], at % span
    rows = residual_ref.shape[1] - sum(rest_ref.shape[0] for rest_ref in rest_refs)
    gradient = jnp.dot(
        residual_ref[:, :rows],
        own_ref[first : first + rows, own_at : own_at + size],
        preferred_element_type=jnp.float32,
    )
    for rest_ref in rest_refs:
        gradient = gradient + jnp.dot(
            residual_ref[:, rows:], rest_ref[:, at : at + size], preferred_element_type=jnp.float32
        )
    return gradient


def descend_body(step, owns, kernels, place_ref, total_ref, residual_ref, base_ref, *refs):
    kernel_refs, refs = refs[:kernels], refs[kernels:]
    out_ref, own_far, tall_ref, wide_ref, own_ref, done_ref = refs
    outs, rows = total_ref.shape
    count = own_ref.shape[0]
    tall_ref[...] = jnp.zeros_like(tall_ref)
    tall_ref[:outs, :rows] = total_ref[...]
    turn_over(tall_ref, wide_ref)
    at = pl.multiple_of(place_ref[0] * count, count)
    own_ref[...] = wide_ref[pl.ds(at, count), :outs]
    store = pltpu.make_async_copy(own_ref, own_far, done_ref)
    store.start()
    for at, size in spans(base_ref.shape[1], 4 * LANES):
        gradient = gradient_span(residual_ref, kernel_refs, owns, 0, at, size)
        out_ref[:, at : at + size] = base_ref[:, at : at + size] - step * gradient
    store.wait()


def descend(place, total, count, residual, base, owns, rests, step):
    outs, rows = total.shape
    high, wide = tiles(rows), tiles(outs)
    kernels = [*owns, *rests]
    return call(
        functools.partial(descend_body, step, len(owns), len(kernels)),
        [(place, SCALARS)] + [(array, WHOLE) for array in (total, residual, base, *kernels)],
        [(base.shape, jnp.float32, WHOLE), ((count, outs), jnp.float32, FAR)],
        [
            pltpu.VMEM((wide, high), jnp.float32),
            pltpu.VMEM((high, wide), jnp.float32),
            pltpu.VMEM((count, outs), jnp.float32),
            pltpu.SemaphoreType.DMA(()),
        ],
    )


def finish_body(step, owns, kernels, first, residual_ref, base_ref, *refs):
    kernel_refs, (out_far, held_ref, done_ref) = refs[:kernels], refs[kernels:]
    stores = []
    for turn, (at, size) in enumerate(spans(base_ref.shape[1], 4 * LANES)):
        gradient = gradient_span(residual_ref, kernel_refs, owns, first, at, size)
        held_ref[:, at : at + size] = base_ref[:, at : at + size] - step * gradient
        span = pl.ds(at, size)
        stores.append(
            pltpu.make_async_copy(held_ref.at[:, span], out_far.at[:, span], done_ref.at[turn])
        )
        stores[-1].start()
    for store in stores:
        store.wait()


def finish(residual, base, owns, rests, first, step):
    turns = len(spans(base.shape[1], 4 * LANES))
    kernels = [*owns, *rests]
    return call(
        functools.partial(finish_body, step, len(owns), len(kernels), first),
        [(array, WHOLE) for array in (residual, base, *kernels)],
        [(base.shape, jnp.float32, FAR)],
        [pltpu.VMEM(base.shape, jnp.float32), pltpu.SemaphoreType.DMA((turns,))],
    )[0]


def on_device(batch_pool, batch_index, centre_pool, centre_index, targets, coefficients):
    own_count = batch_index.shape[0]
    batch_size, centre_size = lax.axis_size("batch"), lax.axis_size("centre")
    batch_place, centre_place = lax.axis_index("batch"), lax.axis_index("centre")
    device_place = batch_place * centre_size + centre_place
    batch_total = own_count * batch_size * centre_size
    far_size, far_place = centre_size // 2, lax.shift_right_logical(centre_place, 1)
    rows = far_size * own_count
    hold_all = batch_total * (centre_index.shape[0] + batch_pool.shape[1]) * 2 <= 1 << 24

    count = centre_index.shape[0]
    both = jnp.concatenate([centre_index, batch_index])
    starts = jnp.where(
        jnp.arange(both.shape[0]) < count,
        centre_place * centre_pool.shape[0],
        device_place * batch_pool.shape[0],
    )
    indices = lax.optimization_barrier(both - starts)
    chosen = indices[count:, None] == jnp.arange(batch_pool.shape[0])
    local_rows = jnp.dot(
        chosen.astype(jnp.bfloat16), batch_pool, preferred_element_type=jnp.float32
    ).astype(jnp.bfloat16)
    pieces = [local_rows] + [flip(local_rows, "centre", 2 * k) for k in range(1, far_size)]

    place = jnp.reshape(far_place, (1,)).astype(jnp.int32)
    index, place = lax.optimization_barrier((indices[:count].reshape(1, -1), place))
    placed, pool_square, index, base, pool = place_coefficients(
        index, coefficients.T, centre_pool
    )
    placed, *pieces = lax.optimization_barrier((placed, *pieces))
    side, placed_targets = arrange(place, targets, pieces)
    other = flip(side, "centre", 1)
    steps = far_size.bit_length() - 1
    span = count // (2 * steps) if steps and count % (2 * steps * LANES) == 0 else count
    early = span // 2 if span < count and span % (2 * LANES) == 0 else 0
    picked = []
    if early:
        picked.append(pick_rows(after(index, side), pool, 0, early))
        other = after(other, *picked[-1])
    terms, other_terms = pool_terms(side, other, pool, pool_square, placed)
    foreign = [flip(side, "batch", k) for k in range(1, batch_size)] if hold_all else []

    flipped = flip(other_terms, "centre", 1)
    if early:
        picked.append(pick_rows(after(index, other_terms), pool, early, early))
        flipped = after(flipped, *picked[-1])
    total = terms - placed_targets + flipped
    kernels, at = [], 2 * early
    distance = 2
    while distance < centre_size:
        if at < count:
            size = span if not kernels else 2 * span
            size = min(size, count - at)
            before = [] if kernels else picked
            *pair, kernel = pick_rows_and_own(
                after(index, total), pool, side, other, before, at, size
            )
            picked, kernels, at = [*picked, pair], [*kernels, kernel], at + size
        total = after(total + flip(total, "centre", distance), *picked[-1])
        distance *= 2
    if hold_all:
        foreign = lax.optimization_barrier((total, *foreign))[1:]
        side_rows = jnp.concatenate(foreign, axis=0)
        other_rows = flip(side_rows, "centre", 1)
    residual_side = total.astype(jnp.bfloat16)
    rests, other_rests = [], []
    if hold_all:
        rests, other_rests = [kernel_block([side_rows], picked)], [kernel_block([other_rows], picked)]
        parts = [residual_side] + [flip(residual_side, "batch", k) for k in range(1, batch_size)]
        rests, other_rests, parts = lax.optimization_barrier((rests, other_rests, parts))
        residual_side = jnp.concatenate(parts, axis=1)
    residual_other = flip(residual_side, "centre", 1)

    step = 8.0 / math.sqrt(batch_total)
    start = base if hold_all else jnp.zeros_like(base)
    updated, residual = descend(
        place, total, own_count, residual_side, start, kernels, rests, step
    )
    updated = finish(residual_other, updated, kernels, other_rests, rows, step)
    if not hold_all:
        updated = base + lax.psum(updated, "batch")
    return (updated.T, residual)


def solution(mesh):
    return jax.shard_map(
        on_device,
        mesh=mesh,
        in_specs=(
            P(("batch", "centre"), None),
            P(("batch", "centre")),
            P("centre", None),
            P("centre"),
            P(("batch", "centre"), None),
            P("centre", None),
        ),
        out_specs=(P("centre", None), P(("batch", "centre"), None)),
        check_vma=False,
    )
```

```python
import functools
import math

import jax
import jax.numpy as jnp
from jax import lax
from jax.experimental import pallas as pl
from jax.experimental.pallas import tpu as pltpu
from jax.sharding import PartitionSpec as P

LANES = 128


def flip(value, axis, distance):
    count = lax.axis_size(axis)
    return lax.ppermute(value, axis, [(i, i ^ distance) for i in range(count)])


def after(value, *others):
    return lax.optimization_barrier((value,) + others)[0]


def contract_last(left, right):
    return lax.dot_general(
        left, right, (((1,), (1,)), ((), ())), preferred_element_type=jnp.float32
    )


def spans(total, most):
    return [(at, min(most, total - at)) for at in range(0, total, most)]


def tiles(count):
    return -(-count // LANES) * LANES


WHOLE = pl.BlockSpec(memory_space=pltpu.VMEM)
SCALARS = pl.BlockSpec(memory_space=pltpu.SMEM)
FAR = pl.BlockSpec(memory_space=pltpu.HBM)


def call(body, operands, outputs, scratch=(), limit=28):
    arrays = [array for array, _ in operands]
    shapes = [jax.ShapeDtypeStruct(shape, dtype) for shape, dtype, _ in outputs]
    return pl.pallas_call(
        body,
        in_specs=[place for _, place in operands],
        out_specs=[place for _, _, place in outputs],
        out_shape=shapes,
        scratch_shapes=list(scratch),
        cost_estimate=pl.CostEstimate(flops=1024, bytes_accessed=1024, transcendentals=0),
        compiler_params=pltpu.CompilerParams(vmem_limit_bytes=limit << 20),
    )(*arrays)


def staggered(steps):
    held = None
    for first, then in steps:
        result = first()
        if held is not None:
            held()
        held = functools.partial(then, result)
    held()


def one_hot(hit):
    return jnp.where(hit, jnp.bfloat16(1.0), jnp.bfloat16(0.0))


def turned(column):
    return jnp.concatenate(
        [
            jnp.broadcast_to(column[at : at + LANES], (LANES, 8)).T[:1]
            for at in range(0, column.shape[0], LANES)
        ],
        axis=1,
    )


def column_of(row):
    return jnp.concatenate(
        [
            jnp.broadcast_to(row[:, at : at + LANES], (LANES, LANES)).T
            for at in range(0, row.shape[1], LANES)
        ],
        axis=0,
    )


def pool_rows(pool_ref, at, size):
    if at + size <= pool_ref.shape[0]:
        return pool_ref[at : at + size, :]
    whole = (pool_ref.shape[0] - at) // LANES * LANES
    place = lax.broadcasted_iota(jnp.int32, (size - whole, pool_ref.shape[1]), 0)
    rows = jnp.zeros(place.shape, jnp.float32)
    for row in range(at + whole, pool_ref.shape[0]):
        wide = pool_ref[row : row + 1, :].astype(jnp.float32)
        rows = jnp.where(place == row - at - whole, wide, rows)
    rows = rows.astype(jnp.bfloat16)
    if whole == 0:
        return rows
    return jnp.concatenate([pool_ref[at : at + whole, :], rows], axis=0)


def place_body(index_ref, base_ref, pool_far, *refs):
    placed_ref, square_ref, column_ref, kept_ref, pool_ref, done_ref = refs
    fetch = pltpu.make_async_copy(pool_far, pool_ref, done_ref)
    fetch.start()
    index = column_of(index_ref[...]).astype(column_ref.dtype)
    column_ref[...] = index
    base = base_ref[...]
    kept_ref[...] = base
    half = base.astype(jnp.bfloat16)
    lane = lax.broadcasted_iota(index.dtype, index.shape, 1)
    cuts = spans(placed_ref.shape[1], 2 * LANES)
    left, arrival = list(cuts), min(3, len(cuts) - 1)
    for turn, (at, size) in enumerate(cuts):
        chosen = [
            one_hot(index - jnp.asarray(part, index.dtype) == lane)
            for part in range(at, at + size, LANES)
        ]
        placed_ref[:, at : at + size] = jnp.dot(
            half, jnp.concatenate(chosen, axis=1), preferred_element_type=jnp.float32
        ).astype(jnp.bfloat16)
        if turn == arrival:
            fetch.wait()
        share = -(-len(left) // (len(cuts) - turn)) if turn >= arrival else 0
        for from_row, count in left[:share]:
            rows = pool_rows(pool_ref, from_row, count).astype(jnp.float32)
            square_ref[from_row : from_row + count, :] = jnp.broadcast_to(
                jnp.sum(rows * rows, axis=1, keepdims=True), (count, LANES)
            )
        left = left[share:]


def place_coefficients(index, base, pool):
    width = tiles(pool.shape[0])
    narrow = jnp.int16 if pool.shape[0] < 1 << 15 else jnp.int32
    return call(
        place_body,
        [(index, WHOLE), (base, WHOLE), (pool, FAR)],
        [
            ((base.shape[0], width), jnp.bfloat16, WHOLE),
            ((width, LANES), jnp.float32, WHOLE),
            ((index.shape[1], LANES), narrow, WHOLE),
            (base.shape, jnp.float32, WHOLE),
            (pool.shape, jnp.bfloat16, WHOLE),
        ],
        [pltpu.SemaphoreType.DMA(())],
        limit=39,
    )


def turn_over(source_ref, target_ref):
    for row in range(0, source_ref.shape[0], LANES):
        for column in range(0, source_ref.shape[1], LANES):
            target_ref[column : column + LANES, row : row + LANES] = source_ref[
                row : row + LANES, column : column + LANES
            ].T


def arrange_body(place_ref, targets_ref, *refs):
    pieces, (side_ref, placed_ref, wide_ref, tall_ref) = refs[:-4], refs[-4:]
    count = targets_ref.shape[0]
    for k, piece_ref in enumerate(pieces):
        at = pl.multiple_of((place_ref[0] ^ k) * count, count)
        side_ref[pl.ds(at, count), :] = piece_ref[...]
    wide_ref[...] = jnp.zeros_like(wide_ref)
    at = pl.multiple_of(place_ref[0] * count, count)
    wide_ref[pl.ds(at, count), : targets_ref.shape[1]] = targets_ref[...]
    turn_over(wide_ref, tall_ref)
    placed_ref[...] = tall_ref[: placed_ref.shape[0], : placed_ref.shape[1]]


def arrange(place, targets, pieces):
    count, outs = targets.shape
    rows = count * len(pieces)
    high, wide = tiles(rows), tiles(outs)
    return call(
        arrange_body,
        [(place, SCALARS), (targets, WHOLE)] + [(piece, WHOLE) for piece in pieces],
        [
            ((rows, pieces[0].shape[1]), jnp.bfloat16, WHOLE),
            ((outs, rows), jnp.float32, WHOLE),
        ],
        [pltpu.VMEM((high, wide), jnp.float32), pltpu.VMEM((wide, high), jnp.float32)],
    )


def kernel_of(squared):
    least = jnp.maximum(squared, 1e-30)
    return jnp.exp2(least * -math.log2(math.e) * lax.rsqrt(least)).astype(jnp.bfloat16)


def halves_and_squares(samples):
    wide = samples.astype(jnp.float32)
    return (wide * -2.0).astype(jnp.bfloat16), jnp.sum(wide * wide, axis=1, keepdims=True)


def terms_body(side_ref, other_ref, pool_ref, square_ref, placed_ref, *refs):
    terms_ref, other_terms_ref, kernel_ref = refs
    samples = jnp.concatenate([side_ref[...], other_ref[...]], axis=0)
    samples, own_square = halves_and_squares(samples)
    own_square = turned(own_square)

    def product(at, size):
        return contract_last(pool_rows(pool_ref, at, size), samples)

    def values(at, size, cross):
        for lane in range(0, samples.shape[0], LANES):
            lanes = slice(lane, lane + LANES)
            squared = square_ref[at : at + size, :] + own_square[:, lanes] + cross[:, lanes]
            kernel_ref[at : at + size, lanes] = kernel_of(squared)

    staggered(
        (functools.partial(product, at, size), functools.partial(values, at, size))
        for at, size in spans(placed_ref.shape[1], 4 * LANES)
    )
    terms = jnp.dot(placed_ref[...], kernel_ref[...], preferred_element_type=jnp.float32)
    rows = side_ref.shape[0]
    terms_ref[...] = terms[:, :rows]
    other_terms_ref[...] = terms[:, rows:]


def pool_terms(side, other, pool, square, placed):
    outs, rows = placed.shape[0], side.shape[0]
    return call(
        terms_body,
        [(array, WHOLE) for array in (side, other, pool, square, placed)],
        [((outs, rows), jnp.float32, WHOLE)] * 2,
        [pltpu.VMEM((placed.shape[1], 2 * rows), jnp.bfloat16)],
    )


def pick_steps(index_ref, pool_ref, rows_ref, square_ref, first, then=None):
    whole = pool_ref.shape[0] // LANES * LANES

    def product(at, size):
        place = index_ref[first + at : first + at + size, :]
        lane = lax.broadcasted_iota(place.dtype, (size, LANES), 1)
        chosen = jnp.concatenate(
            [
                one_hot(place - jnp.asarray(part, place.dtype) == lane)
                for part in range(0, whole, LANES)
            ],
            axis=1,
        )
        rows = jnp.dot(chosen, pool_ref[:whole, :], preferred_element_type=jnp.float32)
        return place.astype(jnp.int32), rows

    def values(at, size, result):
        wanted, rows = result
        for row in range(whole, pool_ref.shape[0]):
            rows = rows + jnp.where(
                wanted[:, :1] == row, pool_ref[row : row + 1, :].astype(jnp.float32), 0.0
            )
        rows_ref[at : at + size, :] = rows.astype(jnp.bfloat16)
        square_ref[:, at : at + size] = turned(jnp.sum(rows * rows, axis=1, keepdims=True))
        if then is not None:
            then(at, size)

    return [
        (functools.partial(product, at, size), functools.partial(values, at, size))
        for at, size in spans(rows_ref.shape[0], 4 * LANES)
    ]


def pick_body(first, index_ref, pool_ref, rows_ref, square_ref):
    staggered(pick_steps(index_ref, pool_ref, rows_ref, square_ref, first))


def pick_rows(index, pool, first, count):
    return call(
        functools.partial(pick_body, first),
        [(index, WHOLE), (pool, WHOLE)],
        [((count, pool.shape[1]), jnp.bfloat16, WHOLE), ((1, count), jnp.float32, WHOLE)],
    )


def pick_own_body(first, index_ref, pool_ref, side_ref, other_ref, *refs):
    *before, rows_ref, square_ref, kernel_ref = refs
    samples = jnp.concatenate([side_ref[...], other_ref[...]], axis=0)
    samples, own_square = halves_and_squares(samples)

    def early_product(early_ref, early_square_ref, start):
        return contract_last(samples, early_ref[...])

    def early_values(early_ref, early_square_ref, start, cross):
        kernel = kernel_of(own_square + early_square_ref[...] + cross)
        kernel_ref[:, start : start + early_ref.shape[0]] = kernel

    def own_values(at, size):
        cross = contract_last(samples, rows_ref[at : at + size, :])
        kernel = kernel_of(own_square + square_ref[:, at : at + size] + cross)
        kernel_ref[:, start + at : start + at + size] = kernel

    steps, start = [], 0
    for early_ref, early_square_ref in zip(before[::2], before[1::2]):
        place = (early_ref, early_square_ref, start)
        steps.append(
            (functools.partial(early_product, *place), functools.partial(early_values, *place))
        )
        start += early_ref.shape[0]
    staggered(steps + pick_steps(index_ref, pool_ref, rows_ref, square_ref, first, own_values))


def pick_rows_and_own(index, pool, side, other, before, first, count):
    rows = side.shape[0] + other.shape[0]
    early = sum(square.shape[1] for _, square in before)
    return call(
        functools.partial(pick_own_body, first),
        [(array, WHOLE) for array in (index, pool, side, other)]
        + [(array, WHOLE) for pair in before for array in pair],
        [
            ((count, pool.shape[1]), jnp.bfloat16, WHOLE),
            ((1, count), jnp.float32, WHOLE),
            ((rows, early + count), jnp.bfloat16, WHOLE),
        ],
    )


def block_body(parts, *refs):
    samples = jnp.concatenate([ref[...] for ref in refs[:parts]], axis=0)
    kernel_ref = refs[-1]
    samples, own_square = halves_and_squares(samples)

    def product(rows_ref, square_ref, start, at, size):
        return contract_last(samples, rows_ref[at : at + size, :])

    def values(rows_ref, square_ref, start, at, size, cross):
        kernel = kernel_of(own_square + square_ref[:, at : at + size] + cross)
        kernel_ref[:, start + at : start + at + size] = kernel

    steps, start = [], 0
    for rows_ref, square_ref in zip(refs[parts:-1:2], refs[parts + 1 : -1 : 2]):
        for at, size in spans(rows_ref.shape[0], 2 * LANES):
            place = (rows_ref, square_ref, start, at, size)
            steps.append((functools.partial(product, *place), functools.partial(values, *place)))
        start += rows_ref.shape[0]
    staggered(steps)


def kernel_block(samples, picked):
    rows = sum(part.shape[0] for part in samples)
    count = sum(square.shape[1] for _, square in picked)
    return call(
        functools.partial(block_body, len(samples)),
        [(part, WHOLE) for part in samples]
        + [(array, WHOLE) for pair in picked for array in pair],
        [((rows, count), jnp.bfloat16, WHOLE)],
    )[0]


def gradient_span(residual_ref, kernel_refs, owns, first, at, size):
    own_refs, rest_refs = kernel_refs[:owns], kernel_refs[owns:]
    span = own_refs[0].shape[1]
    own_ref, own_at = own_refs[at // span], at % span
    rows = own_ref.shape[0] // 2
    rest_rows = residual_ref.shape[1] - rows
    rest_at = rest_rows if first else 0
    gradient = jnp.dot(
        residual_ref[:, :rows],
        own_ref[first : first + rows, own_at : own_at + size],
        preferred_element_type=jnp.float32,
    )
    for rest_ref in rest_refs:
        gradient = gradient + jnp.dot(
            residual_ref[:, rows:],
            rest_ref[rest_at : rest_at + rest_rows, at : at + size],
            preferred_element_type=jnp.float32,
        )
    return gradient


def descend_body(step, owns, kernels, place_ref, total_ref, residual_ref, base_ref, *refs):
    kernel_refs, refs = refs[:kernels], refs[kernels:]
    out_ref, own_far, tall_ref, wide_ref, own_ref, done_ref = refs
    outs, rows = total_ref.shape
    count = own_ref.shape[0]
    tall_ref[...] = jnp.zeros_like(tall_ref)
    tall_ref[:outs, :rows] = total_ref[...]
    turn_over(tall_ref, wide_ref)
    at = pl.multiple_of(place_ref[0] * count, count)
    own_ref[...] = wide_ref[pl.ds(at, count), :outs]
    store = pltpu.make_async_copy(own_ref, own_far, done_ref)
    store.start()
    for at, size in spans(base_ref.shape[1], 4 * LANES):
        gradient = gradient_span(residual_ref, kernel_refs, owns, 0, at, size)
        out_ref[:, at : at + size] = base_ref[:, at : at + size] - step * gradient
    store.wait()


def descend(place, total, count, residual, base, owns, rests, step):
    outs, rows = total.shape
    high, wide = tiles(rows), tiles(outs)
    kernels = [*owns, *rests]
    return call(
        functools.partial(descend_body, step, len(owns), len(kernels)),
        [(place, SCALARS)] + [(array, WHOLE) for array in (total, residual, base, *kernels)],
        [(base.shape, jnp.float32, WHOLE), ((count, outs), jnp.float32, FAR)],
        [
            pltpu.VMEM((wide, high), jnp.float32),
            pltpu.VMEM((high, wide), jnp.float32),
            pltpu.VMEM((count, outs), jnp.float32),
            pltpu.SemaphoreType.DMA(()),
        ],
    )


def finish_body(step, owns, kernels, first, residual_ref, base_ref, *refs):
    kernel_refs, (out_far, held_ref, done_ref) = refs[:kernels], refs[kernels:]
    stores = []
    for turn, (at, size) in enumerate(spans(base_ref.shape[1], 4 * LANES)):
        gradient = gradient_span(residual_ref, kernel_refs, owns, first, at, size)
        held_ref[:, at : at + size] = base_ref[:, at : at + size] - step * gradient
        span = pl.ds(at, size)
        stores.append(
            pltpu.make_async_copy(held_ref.at[:, span], out_far.at[:, span], done_ref.at[turn])
        )
        stores[-1].start()
    for store in stores:
        store.wait()


def finish(residual, base, owns, rests, first, step):
    turns = len(spans(base.shape[1], 4 * LANES))
    kernels = [*owns, *rests]
    return call(
        functools.partial(finish_body, step, len(owns), len(kernels), first),
        [(array, WHOLE) for array in (residual, base, *kernels)],
        [(base.shape, jnp.float32, FAR)],
        [pltpu.VMEM(base.shape, jnp.float32), pltpu.SemaphoreType.DMA((turns,))],
    )[0]


def on_device(batch_pool, batch_index, centre_pool, centre_index, targets, coefficients):
    own_count = batch_index.shape[0]
    batch_size, centre_size = lax.axis_size("batch"), lax.axis_size("centre")
    batch_place, centre_place = lax.axis_index("batch"), lax.axis_index("centre")
    device_place = batch_place * centre_size + centre_place
    batch_total = own_count * batch_size * centre_size
    far_size, far_place = centre_size // 2, lax.shift_right_logical(centre_place, 1)
    rows = far_size * own_count
    hold_all = batch_total * (centre_index.shape[0] + batch_pool.shape[1]) * 2 <= 1 << 24

    count = centre_index.shape[0]
    both = jnp.concatenate([centre_index, batch_index])
    starts = jnp.where(
        jnp.arange(both.shape[0]) < count,
        centre_place * centre_pool.shape[0],
        device_place * batch_pool.shape[0],
    )
    indices = lax.optimization_barrier(both - starts)
    chosen = indices[count:, None] == jnp.arange(batch_pool.shape[0])
    local_rows = jnp.dot(
        chosen.astype(jnp.bfloat16), batch_pool, preferred_element_type=jnp.float32
    ).astype(jnp.bfloat16)
    pieces = [local_rows] + [flip(local_rows, "centre", 2 * k) for k in range(1, far_size)]

    place = jnp.reshape(far_place, (1,)).astype(jnp.int32)
    index, place = lax.optimization_barrier((indices[:count].reshape(1, -1), place))
    placed, pool_square, index, base, pool = place_coefficients(
        index, coefficients.T, centre_pool
    )
    placed, *pieces = lax.optimization_barrier((placed, *pieces))
    side, placed_targets = arrange(place, targets, pieces)
    other = flip(side, "centre", 1)
    steps = far_size.bit_length() - 1
    span = count // (2 * steps) if steps and count % (2 * steps * LANES) == 0 else count
    early = span // 2 if span < count and span % (2 * LANES) == 0 else 0
    picked = []
    if early:
        picked.append(pick_rows(after(index, side), pool, 0, early))
        other = after(other, *picked[-1])
    terms, other_terms = pool_terms(side, other, pool, pool_square, placed)
    foreign = [flip(side, "batch", k) for k in range(1, batch_size)] if hold_all else []

    flipped = flip(other_terms, "centre", 1)
    if early:
        picked.append(pick_rows(after(index, other_terms), pool, early, early))
        flipped = after(flipped, *picked[-1])
    total = terms - placed_targets + flipped
    kernels, at = [], 2 * early
    distance = 2
    while distance < centre_size:
        if at < count:
            size = span if not kernels else 2 * span
            size = min(size, count - at)
            before = [] if kernels else picked
            *pair, kernel = pick_rows_and_own(
                after(index, total), pool, side, other, before, at, size
            )
            picked, kernels, at = [*picked, pair], [*kernels, kernel], at + size
        total = after(total + flip(total, "centre", distance), *picked[-1])
        distance *= 2
    if hold_all:
        foreign = lax.optimization_barrier((total, *foreign))[1:]
        side_rows = jnp.concatenate(foreign, axis=0)
        other_rows = flip(side_rows, "centre", 1)
    residual_side = total.astype(jnp.bfloat16)
    rests = []
    if hold_all:
        rests = [kernel_block([side_rows, other_rows], picked)]
        parts = [residual_side] + [flip(residual_side, "batch", k) for k in range(1, batch_size)]
        rests, parts = lax.optimization_barrier((rests, parts))
        residual_side = jnp.concatenate(parts, axis=1)
    residual_other = flip(residual_side, "centre", 1)

    step = 8.0 / math.sqrt(batch_total)
    start = base if hold_all else jnp.zeros_like(base)
    updated, residual = descend(
        place, total, own_count, residual_side, start, kernels, rests, step
    )
    updated = finish(residual_other, updated, kernels, rests, rows, step)
    if not hold_all:
        updated = base + lax.psum(updated, "batch")
    return (updated.T, residual)


def solution(mesh):
    return jax.shard_map(
        on_device,
        mesh=mesh,
        in_specs=(
            P(("batch", "centre"), None),
            P(("batch", "centre")),
            P("centre", None),
            P("centre"),
            P(("batch", "centre"), None),
            P("centre", None),
        ),
        out_specs=(P("centre", None), P(("batch", "centre"), None)),
        check_vma=False,
    )
```

```python
import functools
import math

import jax
import jax.numpy as jnp
from jax import lax
from jax.experimental import pallas as pl
from jax.experimental.pallas import tpu as pltpu
from jax.sharding import PartitionSpec as P

LANES = 128


def flip(value, axis, distance):
    count = lax.axis_size(axis)
    return lax.ppermute(value, axis, [(i, i ^ distance) for i in range(count)])


def after(value, *others):
    return lax.optimization_barrier((value,) + others)[0]


def contract_last(left, right):
    return lax.dot_general(
        left, right, (((1,), (1,)), ((), ())), preferred_element_type=jnp.float32
    )


def spans(total, most):
    return [(at, min(most, total - at)) for at in range(0, total, most)]


def tiles(count):
    return -(-count // LANES) * LANES


WHOLE = pl.BlockSpec(memory_space=pltpu.VMEM)
SCALARS = pl.BlockSpec(memory_space=pltpu.SMEM)
FAR = pl.BlockSpec(memory_space=pltpu.HBM)


def call(body, operands, outputs, scratch=(), limit=28):
    arrays = [array for array, _ in operands]
    shapes = [jax.ShapeDtypeStruct(shape, dtype) for shape, dtype, _ in outputs]
    return pl.pallas_call(
        body,
        in_specs=[place for _, place in operands],
        out_specs=[place for _, _, place in outputs],
        out_shape=shapes,
        scratch_shapes=list(scratch),
        cost_estimate=pl.CostEstimate(flops=1024, bytes_accessed=1024, transcendentals=0),
        compiler_params=pltpu.CompilerParams(vmem_limit_bytes=limit << 20),
    )(*arrays)


def staggered(steps):
    held = None
    for first, then in steps:
        result = first()
        if held is not None:
            held()
        held = functools.partial(then, result)
    held()


def one_hot(hit):
    return jnp.where(hit, jnp.bfloat16(1.0), jnp.bfloat16(0.0))


def turned(column):
    return jnp.concatenate(
        [
            jnp.broadcast_to(column[at : at + LANES], (LANES, 8)).T[:1]
            for at in range(0, column.shape[0], LANES)
        ],
        axis=1,
    )


def column_of(row):
    return jnp.concatenate(
        [
            jnp.broadcast_to(row[:, at : at + LANES], (LANES, LANES)).T
            for at in range(0, row.shape[1], LANES)
        ],
        axis=0,
    )


def pool_rows(pool_ref, at, size):
    if at + size <= pool_ref.shape[0]:
        return pool_ref[at : at + size, :]
    whole = (pool_ref.shape[0] - at) // LANES * LANES
    place = lax.broadcasted_iota(jnp.int32, (size - whole, pool_ref.shape[1]), 0)
    rows = jnp.zeros(place.shape, jnp.float32)
    for row in range(at + whole, pool_ref.shape[0]):
        wide = pool_ref[row : row + 1, :].astype(jnp.float32)
        rows = jnp.where(place == row - at - whole, wide, rows)
    rows = rows.astype(jnp.bfloat16)
    if whole == 0:
        return rows
    return jnp.concatenate([pool_ref[at : at + whole, :], rows], axis=0)


def place_body(index_ref, base_ref, pool_far, *refs):
    placed_ref, square_ref, column_ref, kept_ref, pool_ref, done_ref = refs
    fetch = pltpu.make_async_copy(pool_far, pool_ref, done_ref)
    fetch.start()
    index = column_of(index_ref[...]).astype(column_ref.dtype)
    column_ref[...] = index
    base = base_ref[...]
    kept_ref[...] = base
    half = base.astype(jnp.bfloat16)
    lane = lax.broadcasted_iota(index.dtype, index.shape, 1)
    cuts = spans(placed_ref.shape[1], 2 * LANES)
    left, arrival = list(cuts), min(3, len(cuts) - 1)
    for turn, (at, size) in enumerate(cuts):
        chosen = [
            one_hot(index - jnp.asarray(part, index.dtype) == lane)
            for part in range(at, at + size, LANES)
        ]
        placed_ref[:, at : at + size] = jnp.dot(
            half, jnp.concatenate(chosen, axis=1), preferred_element_type=jnp.float32
        ).astype(jnp.bfloat16)
        if turn == arrival:
            fetch.wait()
        share = -(-len(left) // (len(cuts) - turn)) if turn >= arrival else 0
        for from_row, count in left[:share]:
            rows = pool_rows(pool_ref, from_row, count).astype(jnp.float32)
            square_ref[from_row : from_row + count, :] = jnp.broadcast_to(
                jnp.sum(rows * rows, axis=1, keepdims=True), (count, LANES)
            )
        left = left[share:]


def place_coefficients(index, base, pool):
    width = tiles(pool.shape[0])
    narrow = jnp.int16 if pool.shape[0] < 1 << 15 else jnp.int32
    return call(
        place_body,
        [(index, WHOLE), (base, WHOLE), (pool, FAR)],
        [
            ((base.shape[0], width), jnp.bfloat16, WHOLE),
            ((width, LANES), jnp.float32, WHOLE),
            ((index.shape[1], LANES), narrow, WHOLE),
            (base.shape, jnp.float32, WHOLE),
            (pool.shape, jnp.bfloat16, WHOLE),
        ],
        [pltpu.SemaphoreType.DMA(())],
        limit=39,
    )


def turn_over(source_ref, target_ref):
    for row in range(0, source_ref.shape[0], LANES):
        for column in range(0, source_ref.shape[1], LANES):
            target_ref[column : column + LANES, row : row + LANES] = source_ref[
                row : row + LANES, column : column + LANES
            ].T


def arrange_body(place_ref, targets_ref, *refs):
    pieces, (side_ref, placed_ref, wide_ref, tall_ref) = refs[:-4], refs[-4:]
    count = targets_ref.shape[0]
    for k, piece_ref in enumerate(pieces):
        at = pl.multiple_of((place_ref[0] ^ k) * count, count)
        side_ref[pl.ds(at, count), :] = piece_ref[...]
    wide_ref[...] = jnp.zeros_like(wide_ref)
    at = pl.multiple_of(place_ref[0] * count, count)
    wide_ref[pl.ds(at, count), : targets_ref.shape[1]] = targets_ref[...]
    turn_over(wide_ref, tall_ref)
    placed_ref[...] = tall_ref[: placed_ref.shape[0], : placed_ref.shape[1]]


def arrange(place, targets, pieces):
    count, outs = targets.shape
    rows = count * len(pieces)
    high, wide = tiles(rows), tiles(outs)
    return call(
        arrange_body,
        [(place, SCALARS), (targets, WHOLE)] + [(piece, WHOLE) for piece in pieces],
        [
            ((rows, pieces[0].shape[1]), jnp.bfloat16, WHOLE),
            ((outs, rows), jnp.float32, WHOLE),
        ],
        [pltpu.VMEM((high, wide), jnp.float32), pltpu.VMEM((wide, high), jnp.float32)],
    )


def kernel_of(squared):
    least = jnp.maximum(squared, 1e-30)
    return jnp.exp2(least * -math.log2(math.e) * lax.rsqrt(least)).astype(jnp.bfloat16)


def halves_and_squares(samples):
    wide = samples.astype(jnp.float32)
    return (wide * -2.0).astype(jnp.bfloat16), jnp.sum(wide * wide, axis=1, keepdims=True)


def terms_body(side_ref, other_ref, pool_ref, square_ref, placed_ref, *refs):
    terms_ref, other_terms_ref, kernel_ref = refs
    samples = jnp.concatenate([side_ref[...], other_ref[...]], axis=0)
    samples, own_square = halves_and_squares(samples)
    own_square = turned(own_square)

    def product(at, size):
        return contract_last(pool_rows(pool_ref, at, size), samples)

    def values(at, size, cross):
        for lane in range(0, samples.shape[0], LANES):
            lanes = slice(lane, lane + LANES)
            squared = square_ref[at : at + size, :] + own_square[:, lanes] + cross[:, lanes]
            kernel_ref[at : at + size, lanes] = kernel_of(squared)

    staggered(
        (functools.partial(product, at, size), functools.partial(values, at, size))
        for at, size in spans(placed_ref.shape[1], 4 * LANES)
    )
    terms = jnp.dot(placed_ref[...], kernel_ref[...], preferred_element_type=jnp.float32)
    rows = side_ref.shape[0]
    terms_ref[...] = terms[:, :rows]
    other_terms_ref[...] = terms[:, rows:]


def pool_terms(side, other, pool, square, placed):
    outs, rows = placed.shape[0], side.shape[0]
    return call(
        terms_body,
        [(array, WHOLE) for array in (side, other, pool, square, placed)],
        [((outs, rows), jnp.float32, WHOLE)] * 2,
        [pltpu.VMEM((placed.shape[1], 2 * rows), jnp.bfloat16)],
    )


def pick_steps(index_ref, pool_ref, rows_ref, square_ref, first, then=None):
    whole = pool_ref.shape[0] // LANES * LANES

    def product(at, size):
        place = index_ref[first + at : first + at + size, :]
        lane = lax.broadcasted_iota(place.dtype, (size, LANES), 1)
        chosen = jnp.concatenate(
            [
                one_hot(place - jnp.asarray(part, place.dtype) == lane)
                for part in range(0, whole, LANES)
            ],
            axis=1,
        )
        rows = jnp.dot(chosen, pool_ref[:whole, :], preferred_element_type=jnp.float32)
        return place.astype(jnp.int32), rows

    def values(at, size, result):
        wanted, rows = result
        for row in range(whole, pool_ref.shape[0]):
            rows = rows + jnp.where(
                wanted[:, :1] == row, pool_ref[row : row + 1, :].astype(jnp.float32), 0.0
            )
        rows_ref[at : at + size, :] = rows.astype(jnp.bfloat16)
        square_ref[:, at : at + size] = turned(jnp.sum(rows * rows, axis=1, keepdims=True))
        if then is not None:
            then(at, size)

    return [
        (functools.partial(product, at, size), functools.partial(values, at, size))
        for at, size in spans(rows_ref.shape[0], 4 * LANES)
    ]


def pick_body(first, index_ref, pool_ref, rows_ref, square_ref):
    staggered(pick_steps(index_ref, pool_ref, rows_ref, square_ref, first))


def pick_rows(index, pool, first, count):
    return call(
        functools.partial(pick_body, first),
        [(index, WHOLE), (pool, WHOLE)],
        [((count, pool.shape[1]), jnp.bfloat16, WHOLE), ((1, count), jnp.float32, WHOLE)],
    )


def pick_own_body(first, index_ref, pool_ref, side_ref, other_ref, *refs):
    *before, rows_ref, square_ref, kernel_ref = refs
    samples = jnp.concatenate([side_ref[...], other_ref[...]], axis=0)
    samples, own_square = halves_and_squares(samples)

    def early_product(early_ref, early_square_ref, start):
        return contract_last(samples, early_ref[...])

    def early_values(early_ref, early_square_ref, start, cross):
        kernel = kernel_of(own_square + early_square_ref[...] + cross)
        kernel_ref[:, start : start + early_ref.shape[0]] = kernel

    def own_values(at, size):
        cross = contract_last(samples, rows_ref[at : at + size, :])
        kernel = kernel_of(own_square + square_ref[:, at : at + size] + cross)
        kernel_ref[:, start + at : start + at + size] = kernel

    steps, start = [], 0
    for early_ref, early_square_ref in zip(before[::2], before[1::2]):
        place = (early_ref, early_square_ref, start)
        steps.append(
            (functools.partial(early_product, *place), functools.partial(early_values, *place))
        )
        start += early_ref.shape[0]
    staggered(steps + pick_steps(index_ref, pool_ref, rows_ref, square_ref, first, own_values))


def pick_rows_and_own(index, pool, side, other, before, first, count):
    rows = side.shape[0] + other.shape[0]
    early = sum(square.shape[1] for _, square in before)
    return call(
        functools.partial(pick_own_body, first),
        [(array, WHOLE) for array in (index, pool, side, other)]
        + [(array, WHOLE) for pair in before for array in pair],
        [
            ((count, pool.shape[1]), jnp.bfloat16, WHOLE),
            ((1, count), jnp.float32, WHOLE),
            ((rows, early + count), jnp.bfloat16, WHOLE),
        ],
    )


def block_body(parts, *refs):
    samples = jnp.concatenate([ref[...] for ref in refs[:parts]], axis=0)
    kernel_ref = refs[-1]
    samples, own_square = halves_and_squares(samples)

    def product(rows_ref, square_ref, start, at, size):
        return contract_last(samples, rows_ref[at : at + size, :])

    def values(rows_ref, square_ref, start, at, size, cross):
        kernel = kernel_of(own_square + square_ref[:, at : at + size] + cross)
        kernel_ref[:, start + at : start + at + size] = kernel

    steps, start = [], 0
    for rows_ref, square_ref in zip(refs[parts:-1:2], refs[parts + 1 : -1 : 2]):
        for at, size in spans(rows_ref.shape[0], 2 * LANES):
            place = (rows_ref, square_ref, start, at, size)
            steps.append((functools.partial(product, *place), functools.partial(values, *place)))
        start += rows_ref.shape[0]
    staggered(steps)


def kernel_block(samples, picked):
    rows = sum(part.shape[0] for part in samples)
    count = sum(square.shape[1] for _, square in picked)
    return call(
        functools.partial(block_body, len(samples)),
        [(part, WHOLE) for part in samples]
        + [(array, WHOLE) for pair in picked for array in pair],
        [((rows, count), jnp.bfloat16, WHOLE)],
    )[0]


def gradient_span(residual_ref, kernel_refs, owns, first, at, size):
    own_refs, rest_refs = kernel_refs[:owns], kernel_refs[owns:]
    span = own_refs[0].shape[1]
    own_ref, own_at = own_refs[at // span], at % span
    rows = own_ref.shape[0] // 2
    rest_rows = residual_ref.shape[1] - rows
    rest_at = rest_rows if first else 0
    gradient = jnp.dot(
        residual_ref[:, :rows],
        own_ref[first : first + rows, own_at : own_at + size],
        preferred_element_type=jnp.float32,
    )
    for rest_ref in rest_refs:
        gradient = gradient + jnp.dot(
            residual_ref[:, rows:],
            rest_ref[rest_at : rest_at + rest_rows, at : at + size],
            preferred_element_type=jnp.float32,
        )
    return gradient


def descend_body(step, owns, kernels, place_ref, total_ref, residual_ref, base_ref, *refs):
    kernel_refs, refs = refs[:kernels], refs[kernels:]
    out_ref, own_far, tall_ref, wide_ref, own_ref, done_ref = refs
    outs, rows = total_ref.shape
    count = own_ref.shape[0]
    tall_ref[...] = jnp.zeros_like(tall_ref)
    tall_ref[:outs, :rows] = total_ref[...]
    turn_over(tall_ref, wide_ref)
    at = pl.multiple_of(place_ref[0] * count, count)
    own_ref[...] = wide_ref[pl.ds(at, count), :outs]
    store = pltpu.make_async_copy(own_ref, own_far, done_ref)
    store.start()
    for at, size in spans(base_ref.shape[1], 4 * LANES):
        gradient = gradient_span(residual_ref, kernel_refs, owns, 0, at, size)
        out_ref[:, at : at + size] = base_ref[:, at : at + size] - step * gradient
    store.wait()


def descend(place, total, count, residual, base, owns, rests, step):
    outs, rows = total.shape
    high, wide = tiles(rows), tiles(outs)
    kernels = [*owns, *rests]
    return call(
        functools.partial(descend_body, step, len(owns), len(kernels)),
        [(place, SCALARS)] + [(array, WHOLE) for array in (total, residual, base, *kernels)],
        [(base.shape, jnp.float32, WHOLE), ((count, outs), jnp.float32, FAR)],
        [
            pltpu.VMEM((wide, high), jnp.float32),
            pltpu.VMEM((high, wide), jnp.float32),
            pltpu.VMEM((count, outs), jnp.float32),
            pltpu.SemaphoreType.DMA(()),
        ],
    )


def finish_body(step, owns, kernels, first, residual_ref, base_ref, *refs):
    kernel_refs, (out_far, held_ref, done_ref) = refs[:kernels], refs[kernels:]
    stores = []
    for turn, (at, size) in enumerate(spans(base_ref.shape[1], 4 * LANES)):
        gradient = gradient_span(residual_ref, kernel_refs, owns, first, at, size)
        held_ref[:, at : at + size] = base_ref[:, at : at + size] - step * gradient
        span = pl.ds(at, size)
        stores.append(
            pltpu.make_async_copy(held_ref.at[:, span], out_far.at[:, span], done_ref.at[turn])
        )
        stores[-1].start()
    for store in stores:
        store.wait()


def finish(residual, base, owns, rests, first, step):
    turns = len(spans(base.shape[1], 4 * LANES))
    kernels = [*owns, *rests]
    return call(
        functools.partial(finish_body, step, len(owns), len(kernels), first),
        [(array, WHOLE) for array in (residual, base, *kernels)],
        [(base.shape, jnp.float32, FAR)],
        [pltpu.VMEM(base.shape, jnp.float32), pltpu.SemaphoreType.DMA((turns,))],
    )[0]


def on_device(batch_pool, batch_index, centre_pool, centre_index, targets, coefficients):
    own_count = batch_index.shape[0]
    batch_size, centre_size = lax.axis_size("batch"), lax.axis_size("centre")
    batch_place, centre_place = lax.axis_index("batch"), lax.axis_index("centre")
    device_place = batch_place * centre_size + centre_place
    batch_total = own_count * batch_size * centre_size
    far_size, far_place = centre_size // 2, lax.shift_right_logical(centre_place, 1)
    rows = far_size * own_count
    hold_all = batch_total * (centre_index.shape[0] + batch_pool.shape[1]) * 2 <= 1 << 24

    count = centre_index.shape[0]
    both = jnp.concatenate([centre_index, batch_index])
    starts = jnp.where(
        jnp.arange(both.shape[0]) < count,
        centre_place * centre_pool.shape[0],
        device_place * batch_pool.shape[0],
    )
    indices = lax.optimization_barrier(both - starts)
    chosen = indices[count:, None] == jnp.arange(batch_pool.shape[0])
    local_rows = jnp.dot(
        chosen.astype(jnp.bfloat16), batch_pool, preferred_element_type=jnp.float32
    ).astype(jnp.bfloat16)
    pieces = [local_rows] + [flip(local_rows, "centre", 2 * k) for k in range(1, far_size)]

    place = jnp.reshape(far_place, (1,)).astype(jnp.int32)
    index, place = lax.optimization_barrier((indices[:count].reshape(1, -1), place))
    placed, pool_square, index, base, pool = place_coefficients(
        index, coefficients.T, centre_pool
    )
    placed, *pieces = lax.optimization_barrier((placed, *pieces))
    side, placed_targets = arrange(place, targets, pieces)
    other = flip(side, "centre", 1)
    steps = far_size.bit_length() - 1
    span = count // (2 * steps) if steps and count % (2 * steps * LANES) == 0 else count
    early = span // 2 if span < count and span % (2 * LANES) == 0 else 0
    picked = []
    if early:
        picked.append(pick_rows(after(index, side), pool, 0, early))
        other = after(other, *picked[-1])
    terms, other_terms = pool_terms(side, other, pool, pool_square, placed)
    foreign = [flip(side, "batch", k) for k in range(1, batch_size)] if hold_all else []

    flipped = flip(other_terms, "centre", 1)
    if early:
        picked.append(pick_rows(after(index, other_terms), pool, early, early))
        flipped = after(flipped, *picked[-1])
    total = terms - placed_targets + flipped
    kernels, at = [], 2 * early
    distance = 2
    while distance < centre_size:
        if at < count:
            size = span if not kernels else 2 * span
            size = min(size, count - at)
            before = [] if kernels else picked
            *pair, kernel = pick_rows_and_own(
                after(index, total), pool, side, other, before, at, size
            )
            picked, kernels, at = [*picked, pair], [*kernels, kernel], at + size
        if 2 * distance == centre_size:
            half = total.astype(jnp.bfloat16)
            summed = half.astype(jnp.float32) + flip(half, "centre", distance).astype(jnp.float32)
        else:
            summed = total + flip(total, "centre", distance)
        total = after(summed, *picked[-1])
        distance *= 2
    if hold_all:
        foreign = lax.optimization_barrier((total, *foreign))[1:]
        side_rows = jnp.concatenate(foreign, axis=0)
        other_rows = flip(side_rows, "centre", 1)
    residual_side = total.astype(jnp.bfloat16)
    rests = []
    if hold_all:
        rests = [kernel_block([side_rows, other_rows], picked)]
        parts = [residual_side] + [flip(residual_side, "batch", k) for k in range(1, batch_size)]
        rests, parts = lax.optimization_barrier((rests, parts))
        residual_side = jnp.concatenate(parts, axis=1)
    residual_other = flip(residual_side, "centre", 1)

    step = 8.0 / math.sqrt(batch_total)
    start = base if hold_all else jnp.zeros_like(base)
    updated, residual = descend(
        place, total, own_count, residual_side, start, kernels, rests, step
    )
    updated = finish(residual_other, updated, kernels, rests, rows, step)
    if not hold_all:
        updated = base + lax.psum(updated, "batch")
    return (updated.T, residual)


def solution(mesh):
    return jax.shard_map(
        on_device,
        mesh=mesh,
        in_specs=(
            P(("batch", "centre"), None),
            P(("batch", "centre")),
            P("centre", None),
            P("centre"),
            P(("batch", "centre"), None),
            P("centre", None),
        ),
        out_specs=(P("centre", None), P(("batch", "centre"), None)),
        check_vma=False,
    )
```
